32 devices in a mesh: seq: 8 (over y, x, core), vocab: 4 (over z).
Axes of the slice: x: 2, y: 2, z: 4, core: 2. Of those that a mesh axis runs over, the one named last changes fastest.
Arguments:
- hidden: bfloat16 [1024, 8192], P('seq'), may hold values from -120 to 120
- head: bfloat16 [8192, 8192], P(None, ('seq', 'vocab')), may hold values from -0.5 to 0.5
- mask: int32 [1024], P('seq'), may hold values from 0 to 1, as said below
Outputs:
- positionwise_uncertainty: float32 [1024], P('seq')
- average_uncertainty_reward: float32 [], replicated
- derivative_wrt_latent_vectors: bfloat16 [1024, 8192], P('seq', 'vocab')
The draws below stay inside these ranges and needn't reach their ends.
Inputs may be any that keep to these rules, and one draw needn't show every extreme that they name: Among the 128 tokens of one index of seq at least half of 16 and at most 16 have mask 1, and the last index of seq has exactly 16; later indices have no fewer than earlier ones.
All inputs are finite; a program needn't handle non-finite values.
Results may differ from the reference program's by a relative error of at most 0.019.
Values may be sent and summed in bfloat16 or wider, within the bound.
No kernel may reach another device: no remote copies, remote signals or barrier semaphores. Data moves between devices by JAX's collectives and lax.ppermute only.
A program may use at most 64 MiB of HBM per device.

```python
import jax
import jax.numpy as jnp
from jax import lax

D = 8192
TOK_DEV = 128
ACT_DEV = 16
TOKENS = 1024
VOCAB = 8192


def draw_hidden(key, part):
    first = jax.random.fold_in(key, 0)
    values = jnp.clip(jax.random.normal(first, (TOKENS, D), jnp.float32), -6.0, 6.0)
    return values.astype(jnp.bfloat16)


def draw_mask(key, part):
    block_list = TOKENS // TOK_DEV
    lowest = max(ACT_DEV // 2, 1)
    first, second = jax.random.split(jax.random.fold_in(key, 7))
    token_counts = jnp.sort(jax.random.randint(first, (block_list,), lowest, ACT_DEV + 1))
    token_counts = token_counts.at[block_list - 1].set(ACT_DEV)
    scores = jax.random.randint(second, (block_list, TOK_DEV), 0, 2 ** 20)
    scores = scores * TOK_DEV + jnp.arange(TOK_DEV, dtype=jnp.int32)[None, :]
    ranks = jnp.argsort(jnp.argsort(scores, axis=1), axis=1)
    response_indicator = (ranks < token_counts[:, None]).astype(jnp.int32)
    return response_indicator.reshape(TOKENS)


def shard_levels(own_key, shape, cuts, smallest, largest):
    gain, own = 1.0, jax.random.fold_in(own_key, 6)
    for axis_at, shards_of in cuts:
        draws = jnp.exp(jax.random.uniform(jax.random.fold_in(own, axis_at), (shards_of,), jnp.float32, smallest / len(cuts), largest / len(cuts)))
        gain = gain * jnp.repeat(draws, shape[axis_at] // shards_of).reshape([-1 if axis == axis_at else 1 for axis in range(len(shape))])
    return gain


def scatter_about(own_key, dims, spread, reach, cuts=(), kind=jnp.bfloat16):
    values = jax.random.normal(own_key, dims, jnp.float32) * spread
    if len(cuts) > 0:
        values = shard_levels(own_key, dims, cuts, -0.22, 0.18) * values
    return jnp.clip(values, min=-reach, max=reach).astype(kind)


def setup_inputs(seed: int = 0) -> dict:
    keys = jax.random.split(jax.random.key(seed), 4)
    return {
        "hidden": draw_hidden(jax.random.fold_in(keys[3], 71), 0),
        "head": scatter_about(keys[1], (D, VOCAB), (3.0 / D ** 0.5), 0.5, ((1, 32),)),
        "mask": draw_mask(jax.random.fold_in(keys[3], 71), 0),
    }


def reference(hidden, head, mask):
    logits = jnp.dot(hidden, head, preferred_element_type=jnp.float32)
    top = jnp.max(logits, axis=1)
    ex = jnp.exp(logits - top[:, None])
    total = jnp.sum(ex, axis=1)
    weighted = jnp.sum(ex * logits, axis=1)
    mean_logit = weighted / total
    distribution_uncertainty = top + jnp.log(total) - mean_logit
    inclusion_indicator = mask.astype(jnp.float32)
    positionwise_uncertainty = inclusion_indicator * distribution_uncertainty
    average_uncertainty_reward = jnp.sum(positionwise_uncertainty) / jnp.sum(inclusion_indicator)
    prob = ex / total[:, None]
    score_grad = (inclusion_indicator[:, None] * (-(prob * (logits - mean_logit[:, None])))).astype(jnp.bfloat16)
    derivative_wrt_latent_vectors = lax.dot_general(score_grad, head, (((1,), (1,)), ((), ())), preferred_element_type=jnp.float32)
    return positionwise_uncertainty, average_uncertainty_reward, derivative_wrt_latent_vectors.astype(jnp.bfloat16)
```

```python
import jax
import jax.numpy as jnp
from jax import lax
from jax.sharding import PartitionSpec as P

ACT_DEV = 16


def swap(value, axis, size, mask):
    return lax.ppermute(value, axis, [(i, i ^ mask) for i in range(size)])


def body(n_seq, n_vocab, hidden, head, mask):
    f32, bf16 = jnp.float32, jnp.bfloat16
    n_chip = n_seq // 2
    width = hidden.shape[1]
    me = lax.axis_index("seq")
    column = lax.axis_index("vocab")

    slots = jnp.cumsum(mask) - 1
    picker = (slots[None, :] == jnp.arange(ACT_DEV, dtype=jnp.int32)[:, None]) & (
        mask[None, :] == 1
    )
    count = jnp.sum(mask).astype(f32)
    own = jnp.dot(picker.astype(bf16), hidden, preferred_element_type=f32).astype(bf16)

    near = [own] + [swap(own, "seq", n_seq, g << 1) for g in range(1, n_chip)]
    near = jnp.concatenate(near, axis=0)
    far = swap(near, "seq", n_seq, 1)
    rows = jnp.concatenate([near, far], axis=0)

    logits = jnp.dot(rows, head, preferred_element_type=f32)
    local_top = jnp.max(logits, axis=1)
    local_ex = jnp.exp(logits - local_top[:, None])
    local_total = jnp.sum(local_ex, axis=1)
    local_weighted = jnp.sum(local_ex * (logits - local_top[:, None]), axis=1)

    place = jnp.arange(n_seq, dtype=jnp.int32)
    relative = (place % n_chip) * 2 + place // n_chip
    order = (relative ^ me)[:, None] == place[None, :]

    def to_device_order(value):
        value = value.reshape(n_seq, ACT_DEV)
        return jnp.sum(jnp.where(order[:, :, None], value[:, None, :], 0.0), axis=0).reshape(-1)

    def to_relative_order(value):
        value = value.reshape(n_seq, ACT_DEV)
        return jnp.sum(jnp.where(order[:, :, None], value[None, :, :], 0.0), axis=1).reshape(-1)

    stats = jnp.stack(
        [
            to_device_order(local_top),
            to_device_order(local_total),
            to_device_order(local_weighted),
            jnp.full_like(local_top, count),
        ]
    )
    n_all = n_seq * n_vocab
    stats = jnp.broadcast_to(stats[None], (n_all,) + stats.shape)
    stats = lax.all_to_all(stats, ("seq", "vocab"), 0, 0, tiled=True)
    tops, totals, weights = stats[:, 0], stats[:, 1], stats[:, 2]
    top = jnp.max(tops, axis=0)
    offset = tops - top[None]
    scale = jnp.exp(offset)
    total = jnp.sum(scale * totals, axis=0)
    centred = jnp.sum(scale * (weights + offset * totals), axis=0) / total
    entropy = jnp.log(total) - centred
    counts = stats.reshape(n_seq, n_vocab, 4, -1)[:, 0, 3, :ACT_DEV]
    valid = jnp.arange(ACT_DEV, dtype=jnp.int32).astype(f32)[None, :] < counts
    entropy = entropy.reshape(n_seq, ACT_DEV)
    average = jnp.sum(jnp.where(valid, entropy, 0.0)) / jnp.sum(counts[:, 0])
    mine = jnp.sum(jnp.where((place == me)[:, None], entropy, 0.0), axis=0)
    positionwise = jnp.sum(jnp.where(picker, mine[:, None], 0.0), axis=0)

    row_top = to_relative_order(top)[:, None]
    row_total = to_relative_order(total)[:, None]
    row_mean = row_top + to_relative_order(centred)[:, None]
    prob = jnp.exp(logits - row_top) / row_total
    score = (-(prob * (logits - row_mean))).astype(bf16)

    half = n_chip * ACT_DEV

    def gradient(part):
        return lax.dot_general(part, head, (((1,), (1,)), ((), ())), preferred_element_type=f32)

    away = swap(gradient(score[half:]).astype(bf16), "seq", n_seq, 1)
    here = gradient(score[:half]) + away.astype(f32)
    sums = here[:ACT_DEV]
    for g in range(1, n_chip):
        block = here[g * ACT_DEV : (g + 1) * ACT_DEV].astype(bf16)
        sums = sums + swap(block, "seq", n_seq, g << 1).astype(f32)

    wide = width // n_vocab

    def columns(k):
        return lax.dynamic_slice_in_dim(sums, (column ^ k) * wide, wide, 1)

    result = columns(0)
    for k in range(1, n_vocab):
        result = result + swap(columns(k).astype(bf16), "vocab", n_vocab, k).astype(f32)
    spread = picker.astype(bf16)
    derivative = lax.dot_general(
        spread, result.astype(bf16), (((0,), (0,)), ((), ())), preferred_element_type=f32
    ).astype(bf16)
    return positionwise, average, derivative


def solution(mesh):
    n_seq, n_vocab = mesh.shape["seq"], mesh.shape["vocab"]

    def run(hidden, head, mask):
        return body(n_seq, n_vocab, hidden, head, mask)

    return jax.shard_map(
        run,
        mesh=mesh,
        in_specs=(P("seq", None), P(None, ("seq", "vocab")), P("seq")),
        out_specs=(P("seq"), P(), P("seq", "vocab")),
        check_vma=False,
    )
```

```python
import functools

import jax
import jax.numpy as jnp
from jax import lax
from jax.experimental import pallas as pl
from jax.experimental.pallas import tpu as pltpu
from jax.sharding import PartitionSpec as P

ACT_DEV = 16
VMEM_BYTES = 16 * 2**20
F32, BF16 = jnp.float32, jnp.bfloat16


def params():
    return pltpu.CompilerParams(vmem_limit_bytes=VMEM_BYTES)


def iota(shape, axis):
    return lax.broadcasted_iota(jnp.int32, shape, axis)


def turn(bits, index):
    return sum(((index >> b) & 1) << (bits - 1 - b) for b in range(bits))


def owner_of(n_seq, core, chip):
    me = lax.axis_index("seq")
    bits = (n_seq // 2).bit_length() - 1
    odd = (me & 1) ^ core
    return me ^ (jnp.where(odd == 1, turn(bits, chip), chip) * 2 + core)


def select_kernel(mask_ref, hidden_ref, own_ref, picker_ref):
    tokens = mask_ref.shape[1]
    mask = mask_ref[...]
    upper = (iota((tokens, tokens), 0) <= iota((tokens, tokens), 1)).astype(BF16)
    ones = jnp.broadcast_to(mask.astype(F32).astype(BF16), (ACT_DEV, tokens))
    slots = jnp.dot(ones, upper, preferred_element_type=F32).astype(jnp.int32) - 1
    picker = (slots == iota((ACT_DEV, tokens), 0)) & (mask == 1)
    picker = picker.astype(F32).astype(BF16)
    picker_ref[...] = picker
    own_ref[...] = jnp.dot(picker, hidden_ref[...], preferred_element_type=F32).astype(BF16)


def select(mask, hidden):
    tokens, width = hidden.shape
    step = width // 4
    return pl.pallas_call(
        select_kernel,
        grid=(width // step,),
        in_specs=[
            pl.BlockSpec((1, tokens), lambda i: (0, 0)),
            pl.BlockSpec((tokens, step), lambda i: (0, i)),
        ],
        out_specs=[
            pl.BlockSpec((ACT_DEV, step), lambda i: (0, i)),
            pl.BlockSpec((ACT_DEV, tokens), lambda i: (0, 0)),
        ],
        out_shape=[
            jax.ShapeDtypeStruct((ACT_DEV, width), BF16),
            jax.ShapeDtypeStruct((ACT_DEV, tokens), BF16),
        ],
        compiler_params=params(),
        name="select_rows",
    )(mask.reshape(1, tokens), hidden)


def logits_kernel(
    n_seq, near_ref, far_ref, head_ref, picker_ref, logits_ref, stats_ref, total, packed
):
    step = pl.program_id(0)
    rows = jnp.concatenate([near_ref[...], far_ref[...]], axis=0)
    part = jnp.dot(rows, head_ref[...], preferred_element_type=F32)

    @pl.when(step == 0)
    def _():
        total[...] = part

    @pl.when(step > 0)
    def _():
        total[...] += part

    @pl.when(step == pl.num_programs(0) - 1)
    def _():
        logits = total[...]
        logits_ref[...] = logits
        top = jnp.max(logits, axis=1, keepdims=True)
        away = logits - top
        ex = jnp.exp(away)
        sums = jnp.sum(ex, axis=1, keepdims=True)
        weighted = jnp.sum(ex * away, axis=1, keepdims=True)
        count = jnp.sum(picker_ref[...].astype(F32))
        lane = iota((logits.shape[0], 128), 1)
        pack = jnp.where(lane == 0, top, jnp.where(lane == 1, sums, weighted))
        pack = jnp.where(lane == 3, count, pack)
        n_chip = n_seq // 2
        for q in range(n_seq):
            place = pl.multiple_of(owner_of(n_seq, q // n_chip, q % n_chip) * ACT_DEV, ACT_DEV)
            packed[pl.ds(place, ACT_DEV), :] = pack[q * ACT_DEV : (q + 1) * ACT_DEV]
        rows8 = packed[...].T[:8]
        stats_ref[...] = jnp.broadcast_to(rows8[None], stats_ref.shape)


def local_logits(n_seq, n_vocab, near, far, head, picker):
    half, width = near.shape
    shard = head.shape[1]
    step = width // 8
    rows = 2 * half
    return pl.pallas_call(
        functools.partial(logits_kernel, n_seq),
        grid=(width // step,),
        in_specs=[
            pl.BlockSpec((half, step), lambda i: (0, i)),
            pl.BlockSpec((half, step), lambda i: (0, i)),
            pl.BlockSpec((step, shard), lambda i: (i, 0)),
            pl.BlockSpec(picker.shape, lambda i: (0, 0)),
        ],
        out_specs=[
            pl.BlockSpec((rows, shard), lambda i: (0, 0)),
            pl.BlockSpec((n_vocab, 8, rows), lambda i: (0, 0, 0)),
        ],
        out_shape=[
            jax.ShapeDtypeStruct((rows, shard), F32),
            jax.ShapeDtypeStruct((n_vocab, 8, rows), F32),
        ],
        scratch_shapes=[pltpu.VMEM((rows, shard), F32), pltpu.VMEM((rows, 128), F32)],
        compiler_params=params(),
        name="local_logits",
    )(near, far, head, picker)


def merged(stats):
    tops, sums, weights = stats[:, 0], stats[:, 1], stats[:, 2]
    top = jnp.max(tops, axis=0, keepdims=True)
    offset = tops - top
    scale = jnp.exp(offset)
    total = jnp.sum(scale * sums, axis=0, keepdims=True)
    weighted = jnp.sum(scale * (weights + offset * sums), axis=0, keepdims=True)
    return top, total, weighted


def stack_rows(top, total, weighted, other):
    row = iota((8, top.shape[1]), 0)
    low = jnp.where(row == 0, top, total)
    high = jnp.where(row == 2, weighted, other)
    return jnp.where(row < 2, low, high)


def merge_kernel(stats_ref, out_ref):
    stats = stats_ref[...]
    top, total, weighted = merged(stats)
    out_ref[...] = jnp.broadcast_to(
        stack_rows(top, total, weighted, stats[0, 3:4])[None], out_ref.shape
    )


def merge(stats, copies):
    return pl.pallas_call(
        merge_kernel,
        out_shape=jax.ShapeDtypeStruct((copies,) + stats.shape[1:], F32),
        compiler_params=params(),
        name="merge_stats",
    )(stats)


def entropy_kernel(stats_ref, picker_ref, each_ref, average_ref, column):
    stats = stats_ref[...]
    n_seq, _, rows = stats.shape
    top, total, weighted = merged(stats)
    entropy = jnp.log(total) - weighted / total
    block = iota((n_seq, rows), 1) // ACT_DEV
    counts = jnp.where(block == iota((n_seq, rows), 0), stats[:, 3], 0.0)
    counts = jnp.sum(counts, axis=0, keepdims=True)
    valid = (iota((1, rows), 1) % ACT_DEV).astype(F32) < counts
    sums = jnp.sum(jnp.where(valid, entropy, 0.0), axis=1, keepdims=True)
    average_ref[...] = sums / jnp.sum(valid.astype(F32), axis=1, keepdims=True)
    column[...] = jnp.broadcast_to(entropy, (128, rows)).T
    place = pl.multiple_of(lax.axis_index("seq") * ACT_DEV, ACT_DEV)
    mine = column[pl.ds(place, ACT_DEV), :][:, :1]
    each_ref[...] = jnp.sum(
        jnp.where(picker_ref[...].astype(F32) > 0.5, mine, 0.0), axis=0, keepdims=True
    )


def entropies(stats, picker):
    tokens = picker.shape[1]
    return pl.pallas_call(
        entropy_kernel,
        out_shape=[
            jax.ShapeDtypeStruct((1, tokens), F32),
            jax.ShapeDtypeStruct((1, 1), F32),
        ],
        scratch_shapes=[pltpu.VMEM((stats.shape[2], 128), F32)],
        compiler_params=params(),
        name="entropies",
    )(stats, picker)


def gradient_kernel(n_seq, stats_ref, logits_ref, head_ref, near_ref, far_ref, columns, ordered, score):
    n_chip = n_seq // 2

    @pl.when(pl.program_id(0) == 0)
    def _():
        top, total, weighted = merged(stats_ref[...])
        rows = top.shape[1]
        mean = top + weighted / total
        lines = stack_rows(top, 1.0 / total, mean, mean)
        columns[...] = jnp.concatenate([lines] * 16, axis=0).T
        for q in range(n_seq):
            place = pl.multiple_of(owner_of(n_seq, q // n_chip, q % n_chip) * ACT_DEV, ACT_DEV)
            ordered[q * ACT_DEV : (q + 1) * ACT_DEV] = columns[pl.ds(place, ACT_DEV), :]
        logits = logits_ref[...]
        prob = jnp.exp(logits - ordered[:, 0:1]) * ordered[:, 1:2]
        score[...] = (prob * (ordered[:, 2:3] - logits)).astype(BF16)

    part = lax.dot_general(
        score[...], head_ref[...], (((1,), (1,)), ((), ())), preferred_element_type=F32
    ).astype(BF16)
    shape = near_ref.shape
    half = n_chip * ACT_DEV
    near_ref[...] = part[:half].reshape(shape)
    far_ref[...] = part[half:].reshape(shape)


def gradients(n_seq, n_vocab, stats, logits, head):
    rows, shard = logits.shape
    width = head.shape[0]
    wide = width // n_vocab
    n_chip = n_seq // 2
    out = jax.ShapeDtypeStruct((n_chip, n_vocab, ACT_DEV, wide), BF16)
    out_spec = pl.BlockSpec((n_chip, 1, ACT_DEV, wide), lambda i: (0, i, 0, 0))
    return pl.pallas_call(
        functools.partial(gradient_kernel, n_seq),
        grid=(n_vocab,),
        in_specs=[
            pl.BlockSpec(stats.shape, lambda i: (0, 0, 0)),
            pl.BlockSpec(logits.shape, lambda i: (0, 0)),
            pl.BlockSpec((wide, shard), lambda i: (i, 0)),
        ],
        out_specs=[out_spec, out_spec],
        out_shape=[out, out],
        scratch_shapes=[
            pltpu.VMEM((rows, 128), F32),
            pltpu.VMEM((rows, 128), F32),
            pltpu.VMEM((rows, shard), BF16),
        ],
        compiler_params=params(),
        name="gradients",
    )(stats, logits, head)


def body(n_seq, n_vocab, hidden, head, mask):
    n_chip = n_seq // 2
    bits = n_chip.bit_length() - 1

    def swap_core(value):
        return lax.ppermute(value, "seq", [(i, i ^ 1) for i in range(n_seq)])

    def swap_chip(value, step):
        flips = (2 << step, 2 << (bits - 1 - step))
        return lax.ppermute(value, "seq", [(i, i ^ flips[i & 1]) for i in range(n_seq)])

    own, picker = select(mask, hidden)

    blocks = [own]
    for a in range(1, n_chip):
        step = a.bit_length() - 1
        blocks.append(swap_chip(blocks[a ^ (1 << step)], step))
    near = jnp.concatenate(blocks, axis=0)
    far = swap_core(near)

    logits, stats = local_logits(n_seq, n_vocab, near, far, head, picker)
    stats = lax.all_to_all(stats, "vocab", 0, 0, tiled=True)
    stats = merge(stats, n_seq)
    stats = lax.all_to_all(stats, "seq", 0, 0, tiled=True)

    near, far = gradients(n_seq, n_vocab, stats, logits, head)
    each, average = entropies(stats, picker)

    here = near.astype(F32) + swap_core(far).astype(F32)
    sums = [here[a] for a in range(n_chip)]
    for a in range(n_chip - 1, 0, -1):
        step = a.bit_length() - 1
        moved = swap_chip(sums[a].astype(BF16), step)
        sums[a ^ (1 << step)] += moved.astype(F32)
    parts = lax.all_to_all(sums[0].astype(BF16), "vocab", 0, 0, tiled=True)
    result = jnp.sum(parts.astype(F32), axis=0).astype(BF16)
    derivative = lax.dot_general(
        picker, result, (((0,), (0,)), ((), ())), preferred_element_type=F32
    ).astype(BF16)
    return each.reshape(-1), average.reshape(()), derivative


def solution(mesh):
    n_seq, n_vocab = mesh.shape["seq"], mesh.shape["vocab"]

    def run(hidden, head, mask):
        return body(n_seq, n_vocab, hidden, head, mask)

    return jax.shard_map(
        run,
        mesh=mesh,
        in_specs=(P("seq", None), P(None, ("seq", "vocab")), P("seq")),
        out_specs=(P("seq"), P(), P("seq", "vocab")),
        check_vma=False,
    )
```

```python
import functools

import jax
import jax.numpy as jnp
from jax import lax
from jax.experimental import pallas as pl
from jax.experimental.pallas import tpu as pltpu
from jax.sharding import PartitionSpec as P

ACT_DEV = 16
VMEM_BYTES = 16 * 2**20
F32, BF16 = jnp.float32, jnp.bfloat16


def params():
    return pltpu.CompilerParams(vmem_limit_bytes=VMEM_BYTES)


def iota(shape, axis):
    return lax.broadcasted_iota(jnp.int32, shape, axis)


def turn(bits, index):
    return sum(((index >> b) & 1) << (bits - 1 - b) for b in range(bits))


def owner_of(n_seq, core, chip):
    me = lax.axis_index("seq")
    bits = (n_seq // 2).bit_length() - 1
    odd = (me & 1) ^ core
    return me ^ (jnp.where(odd == 1, turn(bits, chip), chip) * 2 + core)


def select_kernel(mask_ref, hidden_ref, own_ref, picker_ref, mask_here, hidden_here, mask_sem, sems):
    parts, tokens, step = hidden_here.shape
    copies = [
        pltpu.make_async_copy(
            hidden_ref.at[:, pl.ds(i * step, step)], hidden_here.at[i], sems.at[i]
        )
        for i in range(parts)
    ]
    mask_copy = pltpu.make_async_copy(mask_ref, mask_here, mask_sem)
    mask_copy.start()
    for copy in copies:
        copy.start()
    mask_copy.wait()
    mask = mask_here[...]
    upper = (iota((tokens, tokens), 0) <= iota((tokens, tokens), 1)).astype(BF16)
    ones = jnp.broadcast_to(mask.astype(F32).astype(BF16), (ACT_DEV, tokens))
    slots = jnp.dot(ones, upper, preferred_element_type=F32).astype(jnp.int32) - 1
    picker = (slots == iota((ACT_DEV, tokens), 0)) & (mask == 1)
    picker = picker.astype(F32).astype(BF16)
    picker_ref[...] = picker
    for i in range(parts):
        copies[i].wait()
        own = jnp.dot(picker, hidden_here[i], preferred_element_type=F32)
        own_ref[:, i * step : (i + 1) * step] = own.astype(BF16)


def select(mask, hidden):
    tokens, width = hidden.shape
    parts = 4
    return pl.pallas_call(
        select_kernel,
        in_specs=[pl.BlockSpec(memory_space=pltpu.HBM)] * 2,
        out_shape=[
            jax.ShapeDtypeStruct((ACT_DEV, width), BF16),
            jax.ShapeDtypeStruct((ACT_DEV, tokens), BF16),
        ],
        scratch_shapes=[
            pltpu.VMEM((1, tokens), jnp.int32),
            pltpu.VMEM((parts, tokens, width // parts), BF16),
            pltpu.SemaphoreType.DMA,
            pltpu.SemaphoreType.DMA((parts,)),
        ],
        compiler_params=params(),
        name="select_rows",
    )(mask.reshape(1, tokens), hidden)


def row_order(n_seq):
    last = n_seq // 2 - 1
    early = [(core, chip) for core in (0, 1) for chip in range(last)]
    return early + [(0, last), (1, last)]


def product(block_refs, head_ref):
    width = head_ref.shape[0]
    step = width // 8
    total = None
    for i in range(8):
        rows = jnp.concatenate([ref[:, i * step : (i + 1) * step] for ref in block_refs], axis=0)
        part = jnp.dot(rows, head_ref[i * step : (i + 1) * step, :], preferred_element_type=F32)
        total = part if total is None else total + part
    return total


def early_kernel(*refs):
    *blocks, head_ref, out_ref = refs
    out_ref[...] = product(blocks, head_ref)


def early_logits(blocks, head):
    rows = sum(block.shape[0] for block in blocks)
    return pl.pallas_call(
        early_kernel,
        out_shape=jax.ShapeDtypeStruct((rows, head.shape[1]), F32),
        compiler_params=params(),
        name="early_logits",
    )(*blocks, head)


def late_kernel(n_seq, early_ref, near_ref, far_ref, head_ref, picker_ref, logits_ref, stats_ref, packed):
    late = product([near_ref, far_ref], head_ref)
    logits = jnp.concatenate([early_ref[...], late], axis=0)
    logits_ref[...] = logits
    top = jnp.max(logits, axis=1, keepdims=True)
    away = logits - top
    ex = jnp.exp(away)
    sums = jnp.sum(ex, axis=1, keepdims=True)
    weighted = jnp.sum(ex * away, axis=1, keepdims=True)
    lane = iota((logits.shape[0], 128), 1)
    pack = jnp.where(lane == 0, top, jnp.where(lane == 1, sums, weighted))
    for q, (core, chip) in enumerate(row_order(n_seq)):
        place = pl.multiple_of(owner_of(n_seq, core, chip) * ACT_DEV, ACT_DEV)
        packed[pl.ds(place, ACT_DEV), :] = pack[q * ACT_DEV : (q + 1) * ACT_DEV]
    lines = packed[...].T[:8]
    count = jnp.sum(picker_ref[...].astype(F32))
    mine = iota(lines.shape, 1) // ACT_DEV == lax.axis_index("seq")
    counts = jnp.where(mine, count, 0.0)
    stats_ref[...] = jnp.where(iota(lines.shape, 0) == 3, counts, lines)


def late_logits(n_seq, early, near, far, head, picker):
    shard = head.shape[1]
    rows = n_seq * ACT_DEV
    return pl.pallas_call(
        functools.partial(late_kernel, n_seq),
        out_shape=[
            jax.ShapeDtypeStruct((rows, shard), F32),
            jax.ShapeDtypeStruct((8, rows), F32),
        ],
        scratch_shapes=[pltpu.VMEM((rows, 128), F32)],
        compiler_params=params(),
        name="late_logits",
    )(early, near, far, head, picker)


def merged(refs, index):
    stats = [ref[...] for ref in refs]
    for b in range(len(refs).bit_length() - 1):
        here = ((index >> b) & 1) == 1
        stats = [jnp.where(here, stats[k ^ (1 << b)], stats[k]) for k in range(len(refs))]
    top = functools.reduce(jnp.maximum, [s[0:1] for s in stats])
    total = jnp.zeros_like(top)
    weighted = jnp.zeros_like(top)
    counts = jnp.zeros_like(top)
    for s in stats:
        offset = s[0:1] - top
        scale = jnp.exp(offset)
        total += scale * s[1:2]
        weighted += scale * (s[2:3] + offset * s[1:2])
        counts += s[3:4]
    return top, total, weighted, counts


def stack_rows(first, second, third, fourth):
    row = iota((8, first.shape[1]), 0)
    low = jnp.where(row == 0, first, second)
    high = jnp.where(row == 2, third, fourth)
    return jnp.where(row < 2, low, high)


def merge_kernel(position, *refs):
    *stats, out_ref = refs
    out_ref[...] = stack_rows(*merged(stats, position()))


def merge(stats, position):
    return pl.pallas_call(
        functools.partial(merge_kernel, position),
        out_shape=jax.ShapeDtypeStruct(stats[0].shape, F32),
        compiler_params=params(),
        name="merge_stats",
    )(*stats)


def entropy_kernel(*refs):
    *stats, picker_ref, each_ref, average_ref, column = refs
    top, total, weighted, counts = merged(stats, lax.axis_index("vocab"))
    counts = counts * (1.0 / len(stats))
    rows = top.shape[1]
    entropy = jnp.log(total) - weighted / total
    valid = (iota((1, rows), 1) % ACT_DEV).astype(F32) + 0.5 < counts
    sums = jnp.sum(jnp.where(valid, entropy, 0.0), axis=1, keepdims=True)
    average_ref[...] = sums / jnp.sum(valid.astype(F32), axis=1, keepdims=True)
    column[...] = jnp.broadcast_to(entropy, (128, rows)).T
    place = pl.multiple_of(lax.axis_index("seq") * ACT_DEV, ACT_DEV)
    mine = column[pl.ds(place, ACT_DEV), :][:, :1]
    each_ref[...] = jnp.sum(
        jnp.where(picker_ref[...].astype(F32) > 0.5, mine, 0.0), axis=0, keepdims=True
    )


def entropies(stats, picker):
    tokens = picker.shape[1]
    return pl.pallas_call(
        entropy_kernel,
        out_shape=[
            jax.ShapeDtypeStruct((1, tokens), F32),
            jax.ShapeDtypeStruct((1, 1), F32),
        ],
        scratch_shapes=[pltpu.VMEM((stats[0].shape[1], 128), F32)],
        compiler_params=params(),
        name="entropies",
    )(*stats, picker)


def gradient_kernel(n_seq, *refs):
    *stats, logits_ref, head_ref, near_ref, far_ref, last_ref, columns, ordered = refs
    top, total, weighted, _ = merged(stats, lax.axis_index("vocab"))
    mean = top + weighted / total
    lines = stack_rows(top, 1.0 / total, mean, mean)
    columns[...] = jnp.concatenate([lines] * 16, axis=0).T
    for q, (core, chip) in enumerate(row_order(n_seq)):
        place = pl.multiple_of(owner_of(n_seq, core, chip) * ACT_DEV, ACT_DEV)
        ordered[q * ACT_DEV : (q + 1) * ACT_DEV] = columns[pl.ds(place, ACT_DEV), :]
    logits = logits_ref[...]
    prob = jnp.exp(logits - ordered[:, 0:1]) * ordered[:, 1:2]
    score = (prob * (ordered[:, 2:3] - logits)).astype(BF16)
    n_chip, n_vocab, _, wide = near_ref.shape
    most = (n_chip - 1) * ACT_DEV
    for v in range(n_vocab):
        part = lax.dot_general(
            score,
            head_ref[v * wide : (v + 1) * wide, :],
            (((1,), (1,)), ((), ())),
            preferred_element_type=F32,
        ).astype(BF16)
        blocks = part.reshape(2 * n_chip, ACT_DEV, wide)
        near_ref[: n_chip - 1, v] = blocks[: n_chip - 1]
        near_ref[n_chip - 1, v] = blocks[2 * n_chip - 2]
        far_ref[:, v] = blocks[n_chip - 1 : 2 * n_chip - 2]
        last_ref[v] = blocks[2 * n_chip - 1]


def gradients(n_seq, n_vocab, stats, logits, head):
    rows, shard = logits.shape
    n_chip = n_seq // 2
    block = (n_vocab, ACT_DEV, head.shape[0] // n_vocab)
    return pl.pallas_call(
        functools.partial(gradient_kernel, n_seq),
        out_shape=[
            jax.ShapeDtypeStruct((n_chip,) + block, BF16),
            jax.ShapeDtypeStruct((n_chip - 1,) + block, BF16),
            jax.ShapeDtypeStruct(block, BF16),
        ],
        scratch_shapes=[pltpu.VMEM((rows, 128), F32), pltpu.VMEM((rows, 128), F32)],
        compiler_params=params(),
        name="gradients",
    )(*stats, logits, head)


def body(n_seq, n_vocab, hidden, head, mask):
    n_chip = n_seq // 2
    last = n_chip - 1
    bits = n_chip.bit_length() - 1

    def swap_core(value):
        return lax.ppermute(value, "seq", [(i, i ^ 1) for i in range(n_seq)])

    def swap_chip(value, step):
        flips = (2 << step, 2 << (bits - 1 - step))
        return lax.ppermute(value, "seq", [(i, i ^ flips[i & 1]) for i in range(n_seq)])

    def send_chip(value, chip):
        return lax.ppermute(value, "seq", [(i, i ^ (2 * chip)) for i in range(n_seq)])

    def send_vocab(value, k):
        return lax.ppermute(value, "vocab", [(i, i ^ k) for i in range(n_vocab)])

    own, picker = select(mask, hidden)

    near, far = [own], []
    for a in range(1, n_chip):
        step = a.bit_length() - 1
        source = near[a ^ (1 << step)]
        if a == 2:
            source, far[0] = lax.optimization_barrier((source, far[0]))
        near.append(swap_chip(source, step))
        if a == 1:
            far.append(swap_core(own))
        else:
            far.append(swap_core(near[a - 1]))
    far.append(swap_core(near[last]))

    early = early_logits(near[:last] + far[:last], head)
    logits, stats = late_logits(n_seq, early, near[last], far[last], head, picker)

    stats = merge([stats, swap_core(stats)], lambda: lax.axis_index("seq") & 1)
    stats = merge(
        [stats] + [send_chip(stats, g) for g in range(1, n_chip)], lambda: lax.axis_index("seq") >> 1
    )
    stats = [stats] + [send_vocab(stats, k) for k in range(1, n_vocab)]

    near, far, far_last = gradients(n_seq, n_vocab, stats, logits, head)
    each, average = entropies(stats, picker)

    moved = swap_core(far_last)
    far, moved = lax.optimization_barrier((far, moved))
    far = swap_core(far)
    sums = [near[a].astype(F32) + far[a].astype(F32) for a in range(last)]
    sums.append(near[last].astype(F32) + moved.astype(F32))
    for a in range(last, 0, -1):
        step = a.bit_length() - 1
        sums[a ^ (1 << step)] += swap_chip(sums[a].astype(BF16), step).astype(F32)

    column = lax.axis_index("vocab")

    def piece(k):
        return lax.dynamic_index_in_dim(sums[0], column ^ k, 0, keepdims=False)

    result = piece(0)
    for k in range(n_vocab - 1, 0, -1):
        result = result + send_vocab(piece(k).astype(BF16), k).astype(F32)
    derivative = lax.dot_general(
        picker, result.astype(BF16), (((0,), (0,)), ((), ())), preferred_element_type=F32
    ).astype(BF16)
    return each.reshape(-1), average.reshape(()), derivative


def solution(mesh):
    n_seq, n_vocab = mesh.shape["seq"], mesh.shape["vocab"]

    def run(hidden, head, mask):
        return body(n_seq, n_vocab, hidden, head, mask)

    return jax.shard_map(
        run,
        mesh=mesh,
        in_specs=(P("seq", None), P(None, ("seq", "vocab")), P("seq")),
        out_specs=(P("seq"), P(), P("seq", "vocab")),
        check_vma=False,
    )
```

```python
import functools

import jax
import jax.numpy as jnp
from jax import lax
from jax.experimental import pallas as pl
from jax.experimental.pallas import tpu as pltpu
from jax.sharding import PartitionSpec as P

ACT_DEV = 16
HALVES = 2
ROWS = ACT_DEV // HALVES
LANES = 128
VMEM_BYTES = 16 * 2**20
F32, BF16 = jnp.float32, jnp.bfloat16


def params():
    return pltpu.CompilerParams(vmem_limit_bytes=VMEM_BYTES)


def cost(flops, size):
    return pl.CostEstimate(flops=flops, bytes_accessed=size, transcendentals=0)


def iota(shape, axis):
    return lax.broadcasted_iota(jnp.int32, shape, axis)


def owner_of(q, n_seq):
    n_chip = n_seq // 2
    return lax.axis_index("seq") ^ ((q % n_chip) * 2 + q // n_chip)


def lanes_of(n_seq):
    return -(-n_seq * ROWS // LANES) * LANES


def select_kernel(mask_ref, hidden_ref, *refs):
    *own_refs, picker_ref, mask_here, hidden_here, mask_sem, sems = refs
    parts, tokens, step = hidden_here.shape
    copies = [
        pltpu.make_async_copy(
            hidden_ref.at[:, pl.ds(i * step, step)], hidden_here.at[i], sems.at[i]
        )
        for i in range(parts)
    ]
    mask_copy = pltpu.make_async_copy(mask_ref, mask_here, mask_sem)
    mask_copy.start()
    for copy in copies:
        copy.start()
    mask_copy.wait()
    mask = mask_here[...]
    upper = (iota((tokens, tokens), 0) <= iota((tokens, tokens), 1)).astype(BF16)
    ones = jnp.broadcast_to(mask.astype(F32).astype(BF16), (ACT_DEV, tokens))
    slots = jnp.dot(ones, upper, preferred_element_type=F32).astype(jnp.int32) - 1
    picker = (slots == iota((ACT_DEV, tokens), 0)) & (mask == 1)
    picker = picker.astype(F32).astype(BF16)
    picker_ref[...] = picker
    for i in range(parts):
        copies[i].wait()
        own = jnp.dot(picker, hidden_here[i], preferred_element_type=F32)
        for h, own_ref in enumerate(own_refs):
            own_ref[:, i * step : (i + 1) * step] = own[h * ROWS : (h + 1) * ROWS].astype(BF16)


def select(mask, hidden):
    tokens, width = hidden.shape
    parts = 4
    hbm = functools.partial(pltpu.with_memory_space_constraint, memory_space=pltpu.HBM)
    own = jax.ShapeDtypeStruct((ROWS, width), BF16)
    *own, picker = pl.pallas_call(
        select_kernel,
        in_specs=[pl.BlockSpec(memory_space=pltpu.HBM)] * 2,
        out_shape=[own] * HALVES + [jax.ShapeDtypeStruct((ACT_DEV, tokens), BF16)],
        scratch_shapes=[
            pltpu.VMEM((1, tokens), jnp.int32),
            pltpu.VMEM((parts, tokens, width // parts), BF16),
            pltpu.SemaphoreType.DMA,
            pltpu.SemaphoreType.DMA((parts,)),
        ],
        compiler_params=params(),
        name="select_rows",
    )(hbm(mask.reshape(1, tokens)), hbm(hidden))
    return own, picker


def stage_kernel(head_ref, token_ref, out_ref, sem):
    copy = pltpu.make_async_copy(head_ref, out_ref, sem)
    copy.start()
    copy.wait()


def stage(head, token):
    return pl.pallas_call(
        stage_kernel,
        in_specs=[pl.BlockSpec(memory_space=pltpu.HBM), pl.BlockSpec(memory_space=pl.ANY)],
        out_shape=jax.ShapeDtypeStruct(head.shape, head.dtype),
        scratch_shapes=[pltpu.SemaphoreType.DMA],
        cost_estimate=cost(0, 2 * head.size * 2),
        compiler_params=params(),
        name="stage_head",
    )(pltpu.with_memory_space_constraint(head, pltpu.HBM), token)


def logits_kernel(n_seq, near_ref, far_ref, head_ref, picker_ref, logits_ref, stats_ref, packed):
    width = head_ref.shape[0]
    step = width // 8
    logits = None
    for i in range(8):
        cut = slice(i * step, (i + 1) * step)
        rows = jnp.concatenate([near_ref[:, cut], far_ref[:, cut]], axis=0)
        part = jnp.dot(rows, head_ref[cut, :], preferred_element_type=F32)
        logits = part if logits is None else logits + part
    logits_ref[...] = logits
    top = jnp.max(logits, axis=1, keepdims=True)
    away = logits - top
    ex = jnp.exp(away)
    sums = jnp.sum(ex, axis=1, keepdims=True)
    weighted = jnp.sum(ex * away, axis=1, keepdims=True)
    lane = iota((logits.shape[0], LANES), 1)
    pack = jnp.where(lane == 0, top, jnp.where(lane == 1, sums, weighted))
    packed[...] = jnp.ones(packed.shape, F32)
    for q in range(n_seq):
        place = pl.multiple_of(owner_of(q, n_seq) * ROWS, ROWS)
        packed[pl.ds(place, ROWS), :] = pack[q * ROWS : (q + 1) * ROWS]
    lines = packed[...].T[:8]
    count = jnp.sum(picker_ref[...].astype(F32))
    mine = iota(lines.shape, 1) // ROWS == lax.axis_index("seq")
    lines = jnp.where(iota(lines.shape, 0) == 3, jnp.where(mine, count, 0.0), lines)
    stats_ref[...] = jnp.broadcast_to(lines[None], stats_ref.shape)


def local_logits(n_seq, n_vocab, near, far, head, picker):
    width, shard = head.shape
    rows, lanes = n_seq * ROWS, lanes_of(n_seq)
    return pl.pallas_call(
        functools.partial(logits_kernel, n_seq),
        out_shape=[
            jax.ShapeDtypeStruct((rows, shard), F32),
            jax.ShapeDtypeStruct((n_seq * n_vocab, 8, lanes), F32),
        ],
        scratch_shapes=[pltpu.VMEM((lanes, LANES), F32)],
        cost_estimate=cost(2 * rows * width * shard, 2 * width * (shard + rows)),
        compiler_params=params(),
        name="local_logits",
    )(near, far, head, picker)


def merged(stats):
    tops, sums, weights = stats[:, 0], stats[:, 1], stats[:, 2]
    top = jnp.max(tops, axis=0, keepdims=True)
    offset = tops - top
    scale = jnp.exp(offset)
    total = jnp.sum(scale * sums, axis=0, keepdims=True)
    weighted = jnp.sum(scale * (weights + offset * sums), axis=0, keepdims=True)
    return top, total, weighted / total


def entropy_kernel(n_vocab, *refs):
    *stats_refs, picker_ref, each_ref, average_ref, column = refs
    each, sums, number = 0.0, 0.0, 0.0
    for h, stats_ref in enumerate(stats_refs):
        stats = stats_ref[...]
        _, total, centred = merged(stats)
        entropy = jnp.log(total) - centred
        counts = jnp.sum(stats[:, 3], axis=0, keepdims=True) / n_vocab
        slot = iota(entropy.shape, 1) % ROWS + h * ROWS
        valid = slot.astype(F32) + 0.5 < counts
        sums += jnp.sum(jnp.where(valid, entropy, 0.0), axis=1, keepdims=True)
        number += jnp.sum(valid.astype(F32), axis=1, keepdims=True)
        column[...] = jnp.broadcast_to(entropy, (LANES, entropy.shape[1])).T
        place = pl.multiple_of(lax.axis_index("seq") * ROWS, ROWS)
        mine = column[pl.ds(place, ROWS), :][:, :1]
        picked = picker_ref[...].astype(F32)[h * ROWS : (h + 1) * ROWS] > 0.5
        each += jnp.sum(jnp.where(picked, mine, 0.0), axis=0, keepdims=True)
    each_ref[...] = each
    average_ref[...] = sums / number


def entropies(n_vocab, stats, picker):
    tokens = picker.shape[1]
    return pl.pallas_call(
        functools.partial(entropy_kernel, n_vocab),
        out_shape=[
            jax.ShapeDtypeStruct((1, tokens), F32),
            jax.ShapeDtypeStruct((1, 1), F32),
        ],
        scratch_shapes=[pltpu.VMEM((stats[0].shape[2], LANES), F32)],
        cost_estimate=cost(0, 2**20),
        compiler_params=params(),
        name="entropies",
    )(*stats, picker)


def gradient_kernel(n_seq, stats_ref, logits_ref, head_ref, near_ref, far_ref, columns, ordered):
    top, total, centred = merged(stats_ref[...])
    row = iota((8, top.shape[1]), 0)
    lines = jnp.where(row == 0, top, jnp.where(row == 1, 1.0 / total, top + centred))
    columns[...] = jnp.concatenate([lines] * (LANES // 8), axis=0).T
    for q in range(n_seq):
        place = pl.multiple_of(owner_of(q, n_seq) * ROWS, ROWS)
        ordered[q * ROWS : (q + 1) * ROWS] = columns[pl.ds(place, ROWS), :]
    logits = logits_ref[...]
    prob = jnp.exp(logits - ordered[:, 0:1]) * ordered[:, 1:2]
    score = (prob * (ordered[:, 2:3] - logits)).astype(BF16)
    n_chip, n_vocab, _, wide = near_ref.shape
    for v in range(n_vocab):
        part = lax.dot_general(
            score,
            head_ref[v * wide : (v + 1) * wide, :],
            (((1,), (1,)), ((), ())),
            preferred_element_type=F32,
        )
        for q in range(n_seq):
            out = near_ref if q < n_chip else far_ref
            out[q % n_chip, v] = part[q * ROWS : (q + 1) * ROWS].astype(BF16)


def gradients(n_seq, n_vocab, stats, logits, head):
    rows, shard = logits.shape
    width = head.shape[0]
    out = jax.ShapeDtypeStruct((n_seq // 2, n_vocab, ROWS, width // n_vocab), BF16)
    return pl.pallas_call(
        functools.partial(gradient_kernel, n_seq),
        out_shape=[out, out],
        scratch_shapes=[
            pltpu.VMEM((stats.shape[2], LANES), F32),
            pltpu.VMEM((rows, LANES), F32),
        ],
        cost_estimate=cost(2 * rows * width * shard, 2 * width * (shard + rows)),
        compiler_params=params(),
        name="gradients",
    )(stats, logits, head)


def body(n_seq, n_vocab, hidden, head, mask):
    n_chip = n_seq // 2
    column = lax.axis_index("vocab")

    def swap_core(value):
        return lax.ppermute(value, "seq", [(i, i ^ 1) for i in range(n_seq)])

    def send_chip(value, chip):
        return lax.ppermute(value, "seq", [(i, i ^ (2 * chip)) for i in range(n_seq)])

    def send_vocab(value, k):
        return lax.ppermute(value, "vocab", [(i, i ^ k) for i in range(n_vocab)])

    own, picker = select(mask, hidden)
    head = stage(head, own[0])

    logits, stats = [], []
    for h in range(HALVES):
        near = [own[h]] + [send_chip(own[h], g) for g in range(1, n_chip)]
        near, _ = lax.optimization_barrier((near, logits[-1:]))
        near = jnp.concatenate(near, axis=0)
        part, sent = local_logits(n_seq, n_vocab, near, swap_core(near), head, picker)
        logits.append(part)
        stats.append(lax.all_to_all(sent, ("seq", "vocab"), 0, 0, tiled=True))

    each, average = entropies(n_vocab, stats, picker)

    results = []
    for h in range(HALVES):
        near, far = gradients(n_seq, n_vocab, stats[h], logits[h], head)
        here = near.astype(F32) + swap_core(far).astype(F32)
        sums = here[0]
        for g in range(1, n_chip):
            sums = sums + send_chip(here[g].astype(BF16), g).astype(F32)

        def piece(k):
            return lax.dynamic_index_in_dim(sums, column ^ k, 0, keepdims=False)

        result = piece(0)
        for k in range(1, n_vocab):
            result = result + send_vocab(piece(k).astype(BF16), k).astype(F32)
        results.append(result)
    result = jnp.concatenate(results, axis=0).astype(BF16)
    derivative = lax.dot_general(
        picker, result, (((0,), (0,)), ((), ())), preferred_element_type=F32
    ).astype(BF16)
    return each.reshape(-1), average.reshape(()), derivative


def solution(mesh):
    n_seq, n_vocab = mesh.shape["seq"], mesh.shape["vocab"]

    def run(hidden, head, mask):
        return body(n_seq, n_vocab, hidden, head, mask)

    return jax.shard_map(
        run,
        mesh=mesh,
        in_specs=(P("seq", None), P(None, ("seq", "vocab")), P("seq")),
        out_specs=(P("seq"), P(), P("seq", "vocab")),
        check_vma=False,
    )
```

```python
import functools

import jax
import jax.numpy as jnp
from jax import lax
from jax.experimental import pallas as pl
from jax.experimental.pallas import tpu as pltpu
from jax.sharding import PartitionSpec as P

ACT_DEV = 16
HALVES = 2
ROWS = ACT_DEV // HALVES
LANES = 128
VMEM_BYTES = 16 * 2**20
F32, BF16 = jnp.float32, jnp.bfloat16


def params():
    return pltpu.CompilerParams(vmem_limit_bytes=VMEM_BYTES)


def cost(flops, size):
    return pl.CostEstimate(flops=flops, bytes_accessed=size, transcendentals=0)


def iota(shape, axis):
    return lax.broadcasted_iota(jnp.int32, shape, axis)


def owner_of(q, n_seq):
    n_chip = n_seq // 2
    return lax.axis_index("seq") ^ ((q % n_chip) * 2 + q // n_chip)


def lanes_of(n_seq):
    return -(-n_seq * ROWS // LANES) * LANES


def select_kernel(mask_ref, hidden_ref, *refs):
    *own_refs, picker_ref, mask_here, hidden_here, mask_sem, sems = refs
    parts, tokens, step = hidden_here.shape
    copies = [
        pltpu.make_async_copy(
            hidden_ref.at[:, pl.ds(i * step, step)], hidden_here.at[i], sems.at[i]
        )
        for i in range(parts)
    ]
    mask_copy = pltpu.make_async_copy(mask_ref, mask_here, mask_sem)
    mask_copy.start()
    for copy in copies:
        copy.start()
    mask_copy.wait()
    mask = mask_here[...]
    upper = (iota((tokens, tokens), 0) <= iota((tokens, tokens), 1)).astype(BF16)
    ones = jnp.broadcast_to(mask.astype(F32).astype(BF16), (ACT_DEV, tokens))
    slots = jnp.dot(ones, upper, preferred_element_type=F32).astype(jnp.int32) - 1
    picker = (slots == iota((ACT_DEV, tokens), 0)) & (mask == 1)
    picker = picker.astype(F32).astype(BF16)
    picker_ref[...] = picker
    for i in range(parts):
        copies[i].wait()
        own = jnp.dot(picker, hidden_here[i], preferred_element_type=F32)
        for h, own_ref in enumerate(own_refs):
            own_ref[:, i * step : (i + 1) * step] = own[h * ROWS : (h + 1) * ROWS].astype(BF16)


def select(mask, hidden):
    tokens, width = hidden.shape
    parts = 4
    hbm = functools.partial(pltpu.with_memory_space_constraint, memory_space=pltpu.HBM)
    own = jax.ShapeDtypeStruct((ROWS, width), BF16)
    *own, picker = pl.pallas_call(
        select_kernel,
        in_specs=[pl.BlockSpec(memory_space=pltpu.HBM)] * 2,
        out_shape=[own] * HALVES + [jax.ShapeDtypeStruct((ACT_DEV, tokens), BF16)],
        scratch_shapes=[
            pltpu.VMEM((1, tokens), jnp.int32),
            pltpu.VMEM((parts, tokens, width // parts), BF16),
            pltpu.SemaphoreType.DMA,
            pltpu.SemaphoreType.DMA((parts,)),
        ],
        compiler_params=params(),
        name="select_rows",
    )(hbm(mask.reshape(1, tokens)), hbm(hidden))
    return own, picker


def in_vmem(value):
    return pltpu.with_memory_space_constraint(value, pltpu.VMEM)


def stage_kernel(head_ref, token_ref, out_ref, sem):
    copy = pltpu.make_async_copy(head_ref, out_ref, sem)
    copy.start()
    copy.wait()


def stage(head, token):
    return pl.pallas_call(
        stage_kernel,
        in_specs=[pl.BlockSpec(memory_space=pltpu.HBM), pl.BlockSpec(memory_space=pl.ANY)],
        out_shape=pltpu.VMEM(head.shape, head.dtype),
        scratch_shapes=[pltpu.SemaphoreType.DMA],
        cost_estimate=cost(0, 2 * head.size * 2),
        compiler_params=params(),
        name="stage_head",
    )(pltpu.with_memory_space_constraint(head, pltpu.HBM), token)


def logits_kernel(n_seq, near_ref, far_ref, head_ref, picker_ref, logits_ref, stats_ref, packed):
    width = head_ref.shape[0]
    step = width // 8
    logits = None
    for i in range(8):
        cut = slice(i * step, (i + 1) * step)
        rows = jnp.concatenate([near_ref[:, cut], far_ref[:, cut]], axis=0)
        part = jnp.dot(rows, head_ref[cut, :], preferred_element_type=F32)
        logits = part if logits is None else logits + part
    logits_ref[...] = logits
    top = jnp.max(logits, axis=1, keepdims=True)
    away = logits - top
    ex = jnp.exp(away)
    sums = jnp.sum(ex, axis=1, keepdims=True)
    weighted = jnp.sum(ex * away, axis=1, keepdims=True)
    lane = iota((logits.shape[0], LANES), 1)
    pack = jnp.where(lane == 0, top, jnp.where(lane == 1, sums, weighted))
    packed[...] = jnp.ones(packed.shape, F32)
    for q in range(n_seq):
        place = pl.multiple_of(owner_of(q, n_seq) * ROWS, ROWS)
        packed[pl.ds(place, ROWS), :] = pack[q * ROWS : (q + 1) * ROWS]
    lines = packed[...].T[:8]
    count = jnp.sum(picker_ref[...].astype(F32))
    mine = iota(lines.shape, 1) // ROWS == lax.axis_index("seq")
    lines = jnp.where(iota(lines.shape, 0) == 3, jnp.where(mine, count, 0.0), lines)
    stats_ref[...] = jnp.broadcast_to(lines[None], stats_ref.shape)


def local_logits(n_seq, n_vocab, near, far, head, picker):
    width, shard = head.shape
    rows, lanes = n_seq * ROWS, lanes_of(n_seq)
    return pl.pallas_call(
        functools.partial(logits_kernel, n_seq),
        out_shape=[
            jax.ShapeDtypeStruct((rows, shard), F32),
            jax.ShapeDtypeStruct((n_seq * n_vocab, 8, lanes), F32),
        ],
        scratch_shapes=[pltpu.VMEM((lanes, LANES), F32)],
        cost_estimate=cost(2 * rows * width * shard, 2 * width * (shard + rows)),
        compiler_params=params(),
        name="local_logits",
    )(near, far, in_vmem(head), picker)


def merged(stats):
    tops, sums, weights = stats[:, 0], stats[:, 1], stats[:, 2]
    top = jnp.max(tops, axis=0, keepdims=True)
    offset = tops - top
    scale = jnp.exp(offset)
    total = jnp.sum(scale * sums, axis=0, keepdims=True)
    weighted = jnp.sum(scale * (weights + offset * sums), axis=0, keepdims=True)
    return top, total, weighted / total


def entropy_kernel(n_vocab, *refs):
    *stats_refs, picker_ref, each_ref, average_ref, column = refs
    each, sums, number = 0.0, 0.0, 0.0
    for h, stats_ref in enumerate(stats_refs):
        stats = stats_ref[...]
        _, total, centred = merged(stats)
        entropy = jnp.log(total) - centred
        counts = jnp.sum(stats[:, 3], axis=0, keepdims=True) / n_vocab
        slot = iota(entropy.shape, 1) % ROWS + h * ROWS
        valid = slot.astype(F32) + 0.5 < counts
        sums += jnp.sum(jnp.where(valid, entropy, 0.0), axis=1, keepdims=True)
        number += jnp.sum(valid.astype(F32), axis=1, keepdims=True)
        column[...] = jnp.broadcast_to(entropy, (LANES, entropy.shape[1])).T
        place = pl.multiple_of(lax.axis_index("seq") * ROWS, ROWS)
        mine = column[pl.ds(place, ROWS), :][:, :1]
        picked = picker_ref[...].astype(F32)[h * ROWS : (h + 1) * ROWS] > 0.5
        each += jnp.sum(jnp.where(picked, mine, 0.0), axis=0, keepdims=True)
    each_ref[...] = each
    average_ref[...] = sums / number


def entropies(n_vocab, stats, picker):
    tokens = picker.shape[1]
    return pl.pallas_call(
        functools.partial(entropy_kernel, n_vocab),
        out_shape=[
            jax.ShapeDtypeStruct((1, tokens), F32),
            jax.ShapeDtypeStruct((1, 1), F32),
        ],
        scratch_shapes=[pltpu.VMEM((stats[0].shape[2], LANES), F32)],
        cost_estimate=cost(0, 2**20),
        compiler_params=params(),
        name="entropies",
    )(*stats, picker)


def gradient_kernel(n_seq, stats_ref, logits_ref, head_ref, near_ref, far_ref, columns, ordered):
    top, total, centred = merged(stats_ref[...])
    row = iota((8, top.shape[1]), 0)
    lines = jnp.where(row == 0, top, jnp.where(row == 1, 1.0 / total, top + centred))
    columns[...] = jnp.concatenate([lines] * (LANES // 8), axis=0).T
    for q in range(n_seq):
        place = pl.multiple_of(owner_of(q, n_seq) * ROWS, ROWS)
        ordered[q * ROWS : (q + 1) * ROWS] = columns[pl.ds(place, ROWS), :]
    logits = logits_ref[...]
    prob = jnp.exp(logits - ordered[:, 0:1]) * ordered[:, 1:2]
    score = (prob * (ordered[:, 2:3] - logits)).astype(BF16)
    n_chip, n_vocab, _, wide = near_ref.shape
    for v in range(n_vocab):
        part = lax.dot_general(
            score,
            head_ref[v * wide : (v + 1) * wide, :],
            (((1,), (1,)), ((), ())),
            preferred_element_type=F32,
        )
        for q in range(n_seq):
            out = near_ref if q < n_chip else far_ref
            out[q % n_chip, v] = part[q * ROWS : (q + 1) * ROWS].astype(BF16)


def gradients(n_seq, n_vocab, stats, logits, head):
    rows, shard = logits.shape
    width = head.shape[0]
    out = jax.ShapeDtypeStruct((n_seq // 2, n_vocab, ROWS, width // n_vocab), BF16)
    return pl.pallas_call(
        functools.partial(gradient_kernel, n_seq),
        out_shape=[out, out],
        scratch_shapes=[
            pltpu.VMEM((stats.shape[2], LANES), F32),
            pltpu.VMEM((rows, LANES), F32),
        ],
        cost_estimate=cost(2 * rows * width * shard, 2 * width * (shard + rows)),
        compiler_params=params(),
        name="gradients",
    )(stats, logits, in_vmem(head))


def split_kernel(near_ref, moved_ref, mine_ref, *block_refs):
    mine_ref[...] = near_ref[0].astype(F32) + moved_ref[0].astype(F32)
    for g, block_ref in enumerate(block_refs, 1):
        total = near_ref[g].astype(F32) + moved_ref[g].astype(F32)
        block_ref[...] = total.astype(BF16)


def split(near, moved):
    block = near.shape[1:]
    return pl.pallas_call(
        split_kernel,
        out_shape=[jax.ShapeDtypeStruct(block, F32)]
        + [jax.ShapeDtypeStruct(block, BF16)] * (near.shape[0] - 1),
        cost_estimate=cost(0, 6 * near.size),
        compiler_params=params(),
        name="add_cores",
    )(near, moved)


def plane_kernel(mine_ref, *refs):
    n_vocab = mine_ref.shape[0]
    column = lax.axis_index("vocab")
    moved_refs, out_refs = refs[:-n_vocab], refs[-n_vocab:]
    for k, out_ref in enumerate(out_refs):
        total = mine_ref[column ^ k]
        for moved_ref in moved_refs:
            total = total + moved_ref[column ^ k].astype(F32)
        out_ref[...] = total.astype(out_ref.dtype)


def plane_sum(mine, moved):
    n_vocab, rows, wide = mine.shape
    return pl.pallas_call(
        plane_kernel,
        out_shape=[jax.ShapeDtypeStruct((rows, wide), F32)]
        + [jax.ShapeDtypeStruct((rows, wide), BF16)] * (n_vocab - 1),
        cost_estimate=cost(0, 10 * mine.size),
        compiler_params=params(),
        name="add_chips",
    )(mine, *moved)


def place_kernel(n_vocab, picker_ref, *refs):
    *parts, out_ref = refs
    rows = []
    for h in range(HALVES):
        total = parts[h * n_vocab][...]
        for part in parts[h * n_vocab + 1 : (h + 1) * n_vocab]:
            total = total + part[...].astype(F32)
        rows.append(total)
    result = jnp.concatenate(rows, axis=0).astype(BF16)
    out_ref[...] = lax.dot_general(
        picker_ref[...], result, (((0,), (0,)), ((), ())), preferred_element_type=F32
    ).astype(BF16)


def place(n_vocab, picker, parts):
    return pl.pallas_call(
        functools.partial(place_kernel, n_vocab),
        out_shape=jax.ShapeDtypeStruct((picker.shape[1], parts[0].shape[1]), BF16),
        compiler_params=params(),
        name="place_rows",
    )(picker, *parts)


def body(n_seq, n_vocab, hidden, head, mask):
    n_chip = n_seq // 2

    def swap_core(value):
        return lax.ppermute(value, "seq", [(i, i ^ 1) for i in range(n_seq)])

    def send_chip(value, chip):
        return lax.ppermute(value, "seq", [(i, i ^ (2 * chip)) for i in range(n_seq)])

    def send_vocab(value, k):
        return lax.ppermute(value, "vocab", [(i, i ^ k) for i in range(n_vocab)])

    own, picker = select(mask, hidden)
    head = stage(head, own[0])

    logits, sent, stats = [], [], []
    for h in range(HALVES):
        source = [own[h]] * n_chip
        if h == 0:
            source[-1], head = lax.optimization_barrier((source[-1], head))
        near = [own[h]] + [send_chip(source[g], g) for g in range(1, n_chip)]
        near, _ = lax.optimization_barrier((near, logits[-1:]))
        near = jnp.concatenate(near, axis=0)
        part, lines = local_logits(n_seq, n_vocab, near, swap_core(near), head, picker)
        logits.append(part)
        sent.append(lines)
        stats.append(lax.all_to_all(lines, ("seq", "vocab"), 0, 0, tiled=True))

    parts = []
    for h in range(HALVES):
        lines, _ = lax.optimization_barrier((stats[h], logits))
        near, far = gradients(n_seq, n_vocab, lines, logits[h], head)
        mine, *blocks = split(near, swap_core(far))
        moved = [send_chip(block, g) for g, block in enumerate(blocks, 1)]
        mine, *pieces = plane_sum(mine, moved)
        parts += [mine] + [send_vocab(piece, k) for k, piece in enumerate(pieces, 1)]
    derivative = place(n_vocab, picker, parts)
    each, average = entropies(n_vocab, stats, picker)
    return each.reshape(-1), average.reshape(()), derivative


def solution(mesh):
    n_seq, n_vocab = mesh.shape["seq"], mesh.shape["vocab"]

    def run(hidden, head, mask):
        return body(n_seq, n_vocab, hidden, head, mask)

    return jax.shard_map(
        run,
        mesh=mesh,
        in_specs=(P("seq", None), P(None, ("seq", "vocab")), P("seq")),
        out_specs=(P("seq"), P(), P("seq", "vocab")),
        check_vma=False,
    )
```

```python
import functools

import jax
import jax.numpy as jnp
from jax import lax
from jax.experimental import pallas as pl
from jax.experimental.pallas import tpu as pltpu
from jax.sharding import PartitionSpec as P

ACT_DEV = 16
PARTS = 2
LANES = 128
CHUNKS = 8
VMEM_BYTES = 24 * 2**20
F32, BF16 = jnp.float32, jnp.bfloat16


def params():
    return pltpu.CompilerParams(vmem_limit_bytes=VMEM_BYTES)


def in_hbm(value):
    return pltpu.with_memory_space_constraint(value, pltpu.HBM)


def iota(shape, axis):
    return lax.broadcasted_iota(jnp.int32, shape, axis)


def turn(bits, index):
    return sum(((index >> b) & 1) << (bits - 1 - b) for b in range(bits))


def row_order(n_seq):
    last = n_seq // 2 - 1
    early = [(core, chip) for core in (0, 1) for chip in range(last)]
    return early + [(0, last), (1, last)]


def owner_of(n_seq, core, chip):
    me = lax.axis_index("seq")
    bits = (n_seq // 2).bit_length() - 1
    odd = (me & 1) ^ core
    return me ^ (jnp.where(odd == 1, turn(bits, chip), chip) * 2 + core)


def lanes_of(n_seq):
    return -(-n_seq * ACT_DEV // LANES) * LANES


def select_kernel(mask_ref, hidden_ref, *refs):
    *own_refs, picker_ref, mask_here, hidden_here, mask_sem, sems = refs
    chunks, tokens, step = hidden_here.shape
    copies = [
        pltpu.make_async_copy(
            hidden_ref.at[:, pl.ds(i * step, step)], hidden_here.at[i], sems.at[i]
        )
        for i in range(chunks)
    ]
    mask_copy = pltpu.make_async_copy(mask_ref, mask_here, mask_sem)
    mask_copy.start()
    for copy in copies:
        copy.start()
    mask_copy.wait()
    mask = mask_here[...]
    upper = (iota((tokens, tokens), 0) <= iota((tokens, tokens), 1)).astype(BF16)
    ones = jnp.broadcast_to(mask.astype(F32).astype(BF16), (ACT_DEV, tokens))
    slots = jnp.dot(ones, upper, preferred_element_type=F32).astype(jnp.int32) - 1
    picker = (slots == iota((ACT_DEV, tokens), 0)) & (mask == 1)
    picker = picker.astype(F32).astype(BF16)
    picker_ref[...] = picker
    each = chunks // len(own_refs)
    for i in range(chunks):
        copies[i].wait()
        own = jnp.dot(picker, hidden_here[i], preferred_element_type=F32)
        at = (i % each) * step
        own_refs[i // each][:, at : at + step] = own.astype(BF16)


def select(mask, hidden):
    tokens, width = hidden.shape
    chunks = 4
    own = jax.ShapeDtypeStruct((ACT_DEV, width // PARTS), BF16)
    *own, picker = pl.pallas_call(
        select_kernel,
        in_specs=[pl.BlockSpec(memory_space=pltpu.HBM)] * 2,
        out_shape=[own] * PARTS + [jax.ShapeDtypeStruct((ACT_DEV, tokens), BF16)],
        scratch_shapes=[
            pltpu.VMEM((1, tokens), jnp.int32),
            pltpu.VMEM((chunks, tokens, width // chunks), BF16),
            pltpu.SemaphoreType.DMA,
            pltpu.SemaphoreType.DMA((chunks,)),
        ],
        compiler_params=params(),
        name="select_rows",
    )(in_hbm(mask.reshape(1, tokens)), in_hbm(hidden))
    return own, picker


def head_copies(head_ref, head_here, sems):
    chunks, step, _ = head_here.shape
    copies = [
        pltpu.make_async_copy(head_ref.at[pl.ds(i * step, step), :], head_here.at[i], sems.at[i])
        for i in range(chunks)
    ]
    for copy in copies:
        copy.start()
    return copies


def head_scratch(head):
    width, shard = head.shape
    return [
        pltpu.VMEM((CHUNKS, width // CHUNKS, shard), BF16),
        pltpu.SemaphoreType.DMA((CHUNKS,)),
    ]


def logits_kernel(n_seq, *refs):
    block_refs, head_ref, picker_ref, logits_ref, stats_ref, packed, head_here, sems = (
        refs[:4],
        *refs[4:],
    )
    copies = head_copies(head_ref, head_here, sems)
    step = head_here.shape[1]
    each = CHUNKS // PARTS
    logits = None
    for i in range(CHUNKS):
        at = (i % each) * step
        rows = []
        for ref in block_refs:
            size = ref.shape[0] // PARTS
            start = (i // each) * size
            rows.append(ref[start : start + size, at : at + step])
        rows = jnp.concatenate(rows, axis=0)
        copies[i].wait()
        part = jnp.dot(rows, head_here[i], preferred_element_type=F32)
        logits = part if logits is None else logits + part
    logits_ref[...] = logits
    top = jnp.max(logits, axis=1, keepdims=True)
    away = logits - top
    ex = jnp.exp(away)
    sums = jnp.sum(ex, axis=1, keepdims=True)
    weighted = jnp.sum(ex * away, axis=1, keepdims=True)
    lane = iota((logits.shape[0], LANES), 1)
    pack = jnp.where(lane == 0, top, jnp.where(lane == 1, sums, weighted))
    if packed.shape[0] > n_seq * ACT_DEV:
        packed[...] = jnp.ones(packed.shape, F32)
    for q, (core, chip) in enumerate(row_order(n_seq)):
        place = pl.multiple_of(owner_of(n_seq, core, chip) * ACT_DEV, ACT_DEV)
        packed[pl.ds(place, ACT_DEV), :] = pack[q * ACT_DEV : (q + 1) * ACT_DEV]
    lines = packed[...].T[:8]
    count = jnp.sum(picker_ref[...].astype(F32))
    mine = iota(lines.shape, 1) // ACT_DEV == lax.axis_index("seq")
    lines = jnp.where(iota(lines.shape, 0) == 3, jnp.where(mine, count, 0.0), lines)
    stats_ref[...] = jnp.broadcast_to(lines[None], stats_ref.shape)


def local_logits(n_seq, n_vocab, blocks, head, picker):
    shard = head.shape[1]
    rows, lanes = n_seq * ACT_DEV, lanes_of(n_seq)
    vmem = pl.BlockSpec(memory_space=pltpu.VMEM)
    return pl.pallas_call(
        functools.partial(logits_kernel, n_seq),
        in_specs=[vmem] * 4 + [pl.BlockSpec(memory_space=pltpu.HBM), vmem],
        out_shape=[
            jax.ShapeDtypeStruct((rows, shard), F32),
            jax.ShapeDtypeStruct((n_seq * n_vocab, 8, lanes), F32),
        ],
        scratch_shapes=[pltpu.VMEM((lanes, LANES), F32)] + head_scratch(head),
        compiler_params=params(),
        name="local_logits",
    )(*blocks, in_hbm(head), picker)


def merged(stats):
    tops, sums, weights = stats[:, 0], stats[:, 1], stats[:, 2]
    top = jnp.max(tops, axis=0, keepdims=True)
    offset = tops - top
    scale = jnp.exp(offset)
    total = jnp.sum(scale * sums, axis=0, keepdims=True)
    weighted = jnp.sum(scale * (weights + offset * sums), axis=0, keepdims=True)
    return top, total, weighted / total


def entropy_kernel(n_vocab, stats_ref, picker_ref, each_ref, average_ref, column):
    stats = stats_ref[...]
    _, total, centred = merged(stats)
    entropy = jnp.log(total) - centred
    counts = jnp.sum(stats[:, 3], axis=0, keepdims=True) / n_vocab
    valid = (iota(entropy.shape, 1) % ACT_DEV).astype(F32) + 0.5 < counts
    sums = jnp.sum(jnp.where(valid, entropy, 0.0), axis=1, keepdims=True)
    average_ref[...] = sums / jnp.sum(valid.astype(F32), axis=1, keepdims=True)
    column[...] = jnp.broadcast_to(entropy, (LANES, entropy.shape[1])).T
    place = pl.multiple_of(lax.axis_index("seq") * ACT_DEV, ACT_DEV)
    mine = column[pl.ds(place, ACT_DEV), :][:, :1]
    picked = picker_ref[...].astype(F32) > 0.5
    each_ref[...] = jnp.sum(jnp.where(picked, mine, 0.0), axis=0, keepdims=True)


def entropies(n_vocab, stats, picker):
    tokens = picker.shape[1]
    return pl.pallas_call(
        functools.partial(entropy_kernel, n_vocab),
        out_shape=[
            jax.ShapeDtypeStruct((1, tokens), F32),
            jax.ShapeDtypeStruct((1, 1), F32),
        ],
        scratch_shapes=[pltpu.VMEM((stats.shape[2], LANES), F32)],
        compiler_params=params(),
        name="entropies",
    )(stats, picker)


def gradient_kernel(n_seq, n_vocab, stats_ref, logits_ref, head_ref, *refs):
    *out_refs, last_ref, columns, ordered, head_here, sems = refs
    near_refs, far_refs = out_refs[:PARTS], out_refs[PARTS:]
    copies = head_copies(head_ref, head_here, sems)
    top, total, centred = merged(stats_ref[...])
    row = iota((8, top.shape[1]), 0)
    lines = jnp.where(row == 0, top, jnp.where(row == 1, 1.0 / total, top + centred))
    columns[...] = jnp.concatenate([lines] * (LANES // 8), axis=0).T
    for q, (core, chip) in enumerate(row_order(n_seq)):
        place = pl.multiple_of(owner_of(n_seq, core, chip) * ACT_DEV, ACT_DEV)
        ordered[q * ACT_DEV : (q + 1) * ACT_DEV] = columns[pl.ds(place, ACT_DEV), :]
    logits = logits_ref[...]
    prob = jnp.exp(logits - ordered[:, 0:1]) * ordered[:, 1:2]
    score = (prob * (ordered[:, 2:3] - logits)).astype(BF16)
    n_chip = n_seq // 2
    last = n_chip - 1
    step = head_here.shape[1]
    span = step * CHUNKS // (n_vocab * PARTS)
    size = min(step, span)
    for i in range(CHUNKS):
        copies[i].wait()
        for j in range(step // size):
            start = i * step + j * size
            v, c, at = start // (span * PARTS), start // span % PARTS, start % span
            part = lax.dot_general(
                score,
                head_here[i, j * size : (j + 1) * size, :],
                (((1,), (1,)), ((), ())),
                preferred_element_type=F32,
            ).astype(BF16)
            blocks = part.reshape(n_seq, ACT_DEV, size)
            cut = slice(at, at + size)
            near_refs[c][:last, v, :, cut] = blocks[:last]
            far_refs[c][:, v, :, cut] = blocks[last : 2 * last]
            near_refs[c][last, v, :, cut] = blocks[2 * last]
            last_ref[c, v, :, cut] = blocks[2 * last + 1]


def gradients(n_seq, n_vocab, stats, logits, head):
    rows = logits.shape[0]
    n_chip = n_seq // 2
    block = (n_vocab, ACT_DEV, head.shape[0] // (n_vocab * PARTS))
    vmem = pl.BlockSpec(memory_space=pltpu.VMEM)
    outs = [jax.ShapeDtypeStruct((n_chip,) + block, BF16)] * PARTS
    outs += [jax.ShapeDtypeStruct((n_chip - 1,) + block, BF16)] * PARTS
    outs += [jax.ShapeDtypeStruct((PARTS,) + block, BF16)]
    *outs, far_last = pl.pallas_call(
        functools.partial(gradient_kernel, n_seq, n_vocab),
        in_specs=[vmem, vmem, pl.BlockSpec(memory_space=pltpu.HBM)],
        out_shape=outs,
        scratch_shapes=[
            pltpu.VMEM((stats.shape[2], LANES), F32),
            pltpu.VMEM((rows, LANES), F32),
        ]
        + head_scratch(head),
        compiler_params=params(),
        name="gradients",
    )(stats, logits, in_hbm(head))
    return outs[:PARTS], outs[PARTS:], far_last


def body(n_seq, n_vocab, hidden, head, mask):
    n_chip = n_seq // 2
    last = n_chip - 1
    bits = n_chip.bit_length() - 1

    def swap_core(value):
        return lax.ppermute(value, "seq", [(i, i ^ 1) for i in range(n_seq)])

    def swap_chip(value, step):
        flips = (2 << step, 2 << (bits - 1 - step))
        return lax.ppermute(value, "seq", [(i, i ^ flips[i & 1]) for i in range(n_seq)])

    def send_vocab(value, k):
        return lax.ppermute(value, "vocab", [(i, i ^ k) for i in range(n_vocab)])

    own, picker = select(mask, hidden)

    near = [own]
    for a in range(1, n_chip):
        step = a.bit_length() - 1
        near.append([swap_chip(part, step) for part in near[a ^ (1 << step)]])
    early = jnp.concatenate([near[a][c] for c in range(PARTS) for a in range(last)], axis=0)
    late = jnp.concatenate(near[last], axis=0)
    blocks = [early, swap_core(early), late, swap_core(late)]

    logits, stats = local_logits(n_seq, n_vocab, blocks, head, picker)
    stats = lax.all_to_all(stats, ("seq", "vocab"), 0, 0, tiled=True)
    near, far, far_last = gradients(n_seq, n_vocab, stats, logits, head)
    each, average = entropies(n_vocab, stats, picker)

    moved = swap_core(far_last)
    far, moved = lax.optimization_barrier((far, moved))
    far = [swap_core(part) for part in far]
    sums = [[near[c][a].astype(F32) + far[c][a].astype(F32) for c in range(PARTS)] for a in range(last)]
    sums.append([near[c][last].astype(F32) + moved[c].astype(F32) for c in range(PARTS)])
    for a in range(last, 0, -1):
        step = a.bit_length() - 1
        for c in range(PARTS):
            sums[a ^ (1 << step)][c] += swap_chip(sums[a][c].astype(BF16), step).astype(F32)

    column = lax.axis_index("vocab")

    def piece(k):
        parts = [lax.dynamic_index_in_dim(part, column ^ k, 0, keepdims=False) for part in sums[0]]
        return jnp.concatenate(parts, axis=1)

    result = piece(0)
    for k in range(n_vocab - 1, 0, -1):
        result = result + send_vocab(piece(k).astype(BF16), k).astype(F32)
    derivative = lax.dot_general(
        picker, result.astype(BF16), (((0,), (0,)), ((), ())), preferred_element_type=F32
    ).astype(BF16)
    return each.reshape(-1), average.reshape(()), derivative


def solution(mesh):
    n_seq, n_vocab = mesh.shape["seq"], mesh.shape["vocab"]

    def run(hidden, head, mask):
        return body(n_seq, n_vocab, hidden, head, mask)

    return jax.shard_map(
        run,
        mesh=mesh,
        in_specs=(P("seq", None), P(None, ("seq", "vocab")), P("seq")),
        out_specs=(P("seq"), P(), P("seq", "vocab")),
        check_vma=False,
    )
```

```python
import functools

import jax
import jax.numpy as jnp
from jax import lax
from jax.experimental import pallas as pl
from jax.experimental.pallas import tpu as pltpu
from jax.sharding import PartitionSpec as P

ACT_DEV = 16
PARTS = 2
LANES = 128
CHUNKS = 8
FLIGHT = 3
VMEM_BYTES = 24 * 2**20
F32, BF16 = jnp.float32, jnp.bfloat16


def params():
    return pltpu.CompilerParams(vmem_limit_bytes=VMEM_BYTES)


def in_hbm(value):
    return pltpu.with_memory_space_constraint(value, pltpu.HBM)


def iota(shape, axis):
    return lax.broadcasted_iota(jnp.int32, shape, axis)


def turn(bits, index):
    return sum(((index >> b) & 1) << (bits - 1 - b) for b in range(bits))


def row_order(n_seq):
    last = n_seq // 2 - 1
    early = [(core, chip) for core in (0, 1) for chip in range(last)]
    return early + [(0, last), (1, last)]


def owner_of(n_seq, core, chip):
    me = lax.axis_index("seq")
    bits = (n_seq // 2).bit_length() - 1
    odd = (me & 1) ^ core
    return me ^ (jnp.where(odd == 1, turn(bits, chip), chip) * 2 + core)


def lanes_of(n_seq):
    return -(-n_seq * ACT_DEV // LANES) * LANES


def select_kernel(mask_ref, hidden_ref, *refs):
    *own_refs, picker_ref, mask_here, hidden_here, mask_sem, sems = refs
    chunks, tokens, step = hidden_here.shape
    copies = [
        pltpu.make_async_copy(
            hidden_ref.at[:, pl.ds(i * step, step)], hidden_here.at[i], sems.at[i]
        )
        for i in range(chunks)
    ]
    mask_copy = pltpu.make_async_copy(mask_ref, mask_here, mask_sem)
    mask_copy.start()
    for copy in copies[:FLIGHT]:
        copy.start()
    mask_copy.wait()
    mask = mask_here[...]
    upper = (iota((tokens, tokens), 0) <= iota((tokens, tokens), 1)).astype(BF16)
    ones = jnp.broadcast_to(mask.astype(F32).astype(BF16), (ACT_DEV, tokens))
    slots = jnp.dot(ones, upper, preferred_element_type=F32).astype(jnp.int32) - 1
    picker = (slots == iota((ACT_DEV, tokens), 0)) & (mask == 1)
    picker = picker.astype(F32).astype(BF16)
    picker_ref[...] = picker
    each = chunks // len(own_refs)
    for i in range(chunks):
        arrive(copies, i)
        own = jnp.dot(picker, hidden_here[i], preferred_element_type=F32)
        at = (i % each) * step
        own_refs[i // each][:, at : at + step] = own.astype(BF16)


def select(mask, hidden):
    tokens, width = hidden.shape
    chunks = 4
    own = jax.ShapeDtypeStruct((ACT_DEV, width // PARTS), BF16)
    *own, picker = pl.pallas_call(
        select_kernel,
        in_specs=[pl.BlockSpec(memory_space=pltpu.HBM)] * 2,
        out_shape=[own] * PARTS + [jax.ShapeDtypeStruct((ACT_DEV, tokens), BF16)],
        scratch_shapes=[
            pltpu.VMEM((1, tokens), jnp.int32),
            pltpu.VMEM((chunks, tokens, width // chunks), BF16),
            pltpu.SemaphoreType.DMA,
            pltpu.SemaphoreType.DMA((chunks,)),
        ],
        compiler_params=params(),
        name="select_rows",
    )(in_hbm(mask.reshape(1, tokens)), in_hbm(hidden))
    return own, picker


def head_copies(head_ref, head_here, sems):
    chunks, step, _ = head_here.shape
    copies = [
        pltpu.make_async_copy(head_ref.at[pl.ds(i * step, step), :], head_here.at[i], sems.at[i])
        for i in range(chunks)
    ]
    for copy in copies[:FLIGHT]:
        copy.start()
    return copies


def arrive(copies, i):
    copies[i].wait()
    if i + FLIGHT < len(copies):
        copies[i + FLIGHT].start()


def head_scratch(head):
    width, shard = head.shape
    return [
        pltpu.VMEM((CHUNKS, width // CHUNKS, shard), BF16),
        pltpu.SemaphoreType.DMA((CHUNKS,)),
    ]


def logits_kernel(n_seq, *refs):
    block_refs, head_ref, picker_ref, logits_ref, stats_ref, packed, head_here, sems = (
        refs[:4],
        *refs[4:],
    )
    copies = head_copies(head_ref, head_here, sems)
    step = head_here.shape[1]
    each = CHUNKS // PARTS
    logits = None
    for i in range(CHUNKS):
        at = (i % each) * step
        rows = []
        for ref in block_refs:
            size = ref.shape[0] // PARTS
            start = (i // each) * size
            rows.append(ref[start : start + size, at : at + step])
        rows = jnp.concatenate(rows, axis=0)
        arrive(copies, i)
        part = jnp.dot(rows, head_here[i], preferred_element_type=F32)
        logits = part if logits is None else logits + part
    logits_ref[...] = logits
    top = jnp.max(logits, axis=1, keepdims=True)
    away = logits - top
    ex = jnp.exp(away)
    sums = jnp.sum(ex, axis=1, keepdims=True)
    weighted = jnp.sum(ex * away, axis=1, keepdims=True)
    lane = iota((logits.shape[0], LANES), 1)
    pack = jnp.where(lane == 0, top, jnp.where(lane == 1, sums, weighted))
    if packed.shape[0] > n_seq * ACT_DEV:
        packed[...] = jnp.ones(packed.shape, F32)
    for q, (core, chip) in enumerate(row_order(n_seq)):
        place = pl.multiple_of(owner_of(n_seq, core, chip) * ACT_DEV, ACT_DEV)
        packed[pl.ds(place, ACT_DEV), :] = pack[q * ACT_DEV : (q + 1) * ACT_DEV]
    lines = packed[...].T[:4]
    count = jnp.sum(picker_ref[...].astype(F32))
    mine = iota(lines.shape, 1) // ACT_DEV == lax.axis_index("seq")
    lines = jnp.where(iota(lines.shape, 0) == 3, jnp.where(mine, count, 0.0), lines)
    stats_ref[...] = jnp.broadcast_to(lines[None], stats_ref.shape)


def local_logits(n_seq, n_vocab, blocks, head, picker):
    shard = head.shape[1]
    rows, lanes = n_seq * ACT_DEV, lanes_of(n_seq)
    vmem = pl.BlockSpec(memory_space=pltpu.VMEM)
    return pl.pallas_call(
        functools.partial(logits_kernel, n_seq),
        in_specs=[vmem] * 4 + [pl.BlockSpec(memory_space=pl.ANY), vmem],
        out_shape=[
            jax.ShapeDtypeStruct((rows, shard), F32),
            jax.ShapeDtypeStruct((n_seq * n_vocab, 4, lanes), F32),
        ],
        scratch_shapes=[pltpu.VMEM((lanes, LANES), F32)] + head_scratch(head),
        compiler_params=params(),
        name="local_logits",
    )(*blocks, head, picker)


def merged(stats):
    tops, sums, weights = stats[:, 0], stats[:, 1], stats[:, 2]
    top = jnp.max(tops, axis=0, keepdims=True)
    offset = tops - top
    scale = jnp.exp(offset)
    total = jnp.sum(scale * sums, axis=0, keepdims=True)
    weighted = jnp.sum(scale * (weights + offset * sums), axis=0, keepdims=True)
    return top, total, weighted / total


def entropy_kernel(n_vocab, stats_ref, picker_ref, each_ref, average_ref, column):
    stats = stats_ref[...]
    _, total, centred = merged(stats)
    entropy = jnp.log(total) - centred
    counts = jnp.sum(stats[:, 3], axis=0, keepdims=True) / n_vocab
    valid = (iota(entropy.shape, 1) % ACT_DEV).astype(F32) + 0.5 < counts
    sums = jnp.sum(jnp.where(valid, entropy, 0.0), axis=1, keepdims=True)
    average_ref[...] = sums / jnp.sum(valid.astype(F32), axis=1, keepdims=True)
    column[...] = jnp.broadcast_to(entropy, (LANES, entropy.shape[1])).T
    place = pl.multiple_of(lax.axis_index("seq") * ACT_DEV, ACT_DEV)
    mine = column[pl.ds(place, ACT_DEV), :][:, :1]
    picked = picker_ref[...].astype(F32) > 0.5
    each_ref[...] = jnp.sum(jnp.where(picked, mine, 0.0), axis=0, keepdims=True)


def entropies(n_vocab, stats, picker):
    tokens = picker.shape[1]
    return pl.pallas_call(
        functools.partial(entropy_kernel, n_vocab),
        out_shape=[
            jax.ShapeDtypeStruct((1, tokens), F32),
            jax.ShapeDtypeStruct((1, 1), F32),
        ],
        scratch_shapes=[pltpu.VMEM((stats.shape[2], LANES), F32)],
        compiler_params=params(),
        name="entropies",
    )(stats, picker)


def gradient_kernel(n_seq, n_vocab, stats_ref, logits_ref, head_ref, *refs):
    *out_refs, last_ref, columns, ordered, head_here, sems = refs
    near_refs, far_refs = out_refs[:PARTS], out_refs[PARTS:]
    copies = head_copies(head_ref, head_here, sems)
    top, total, centred = merged(stats_ref[...])
    row = iota((8, top.shape[1]), 0)
    lines = jnp.where(row == 0, top, jnp.where(row == 1, 1.0 / total, top + centred))
    columns[...] = jnp.concatenate([lines] * (LANES // 8), axis=0).T
    for q, (core, chip) in enumerate(row_order(n_seq)):
        place = pl.multiple_of(owner_of(n_seq, core, chip) * ACT_DEV, ACT_DEV)
        ordered[q * ACT_DEV : (q + 1) * ACT_DEV] = columns[pl.ds(place, ACT_DEV), :]
    logits = logits_ref[...]
    prob = jnp.exp(logits - ordered[:, 0:1]) * ordered[:, 1:2]
    score = (prob * (ordered[:, 2:3] - logits)).astype(BF16)
    n_chip = n_seq // 2
    last = n_chip - 1
    step = head_here.shape[1]
    span = step * CHUNKS // (n_vocab * PARTS)
    size = min(step, span)
    for i in range(CHUNKS):
        arrive(copies, i)
        for j in range(step // size):
            start = i * step + j * size
            v, c, at = start // (span * PARTS), start // span % PARTS, start % span
            part = lax.dot_general(
                score,
                head_here[i, j * size : (j + 1) * size, :],
                (((1,), (1,)), ((), ())),
                preferred_element_type=F32,
            ).astype(BF16)
            blocks = part.reshape(n_seq, ACT_DEV, size)
            cut = slice(at, at + size)
            near_refs[c][:last, v, :, cut] = blocks[:last]
            far_refs[c][:, v, :, cut] = blocks[last : 2 * last]
            near_refs[c][last, v, :, cut] = blocks[2 * last]
            last_ref[c, v, :, cut] = blocks[2 * last + 1]


def gradients(n_seq, n_vocab, stats, logits, head):
    rows = logits.shape[0]
    n_chip = n_seq // 2
    block = (n_vocab, ACT_DEV, head.shape[0] // (n_vocab * PARTS))
    vmem = pl.BlockSpec(memory_space=pltpu.VMEM)
    outs = [jax.ShapeDtypeStruct((n_chip,) + block, BF16)] * PARTS
    outs += [jax.ShapeDtypeStruct((n_chip - 1,) + block, BF16)] * PARTS
    outs += [jax.ShapeDtypeStruct((PARTS,) + block, BF16)]
    *outs, far_last = pl.pallas_call(
        functools.partial(gradient_kernel, n_seq, n_vocab),
        in_specs=[vmem, vmem, pl.BlockSpec(memory_space=pl.ANY)],
        out_shape=outs,
        scratch_shapes=[
            pltpu.VMEM((stats.shape[2], LANES), F32),
            pltpu.VMEM((rows, LANES), F32),
        ]
        + head_scratch(head),
        compiler_params=params(),
        name="gradients",
    )(stats, logits, head)
    return outs[:PARTS], outs[PARTS:], far_last


def body(n_seq, n_vocab, hidden, head, mask):
    n_chip = n_seq // 2
    last = n_chip - 1
    bits = n_chip.bit_length() - 1

    def swap_core(value):
        return lax.ppermute(value, "seq", [(i, i ^ 1) for i in range(n_seq)])

    def swap_chip(value, step):
        flips = (2 << step, 2 << (bits - 1 - step))
        return lax.ppermute(value, "seq", [(i, i ^ flips[i & 1]) for i in range(n_seq)])

    def send_vocab(value, k):
        return lax.ppermute(value, "vocab", [(i, i ^ k) for i in range(n_vocab)])

    own, picker = select(mask, hidden)

    near = [own]
    for a in range(1, n_chip):
        step = a.bit_length() - 1
        near.append([swap_chip(part, step) for part in near[a ^ (1 << step)]])
    early = jnp.concatenate([near[a][c] for c in range(PARTS) for a in range(last)], axis=0)
    early, near[last][0] = lax.optimization_barrier((early, near[last][0]))
    late = jnp.concatenate(near[last], axis=0)
    blocks = [early, swap_core(early), late, swap_core(late)]

    logits, stats = local_logits(n_seq, n_vocab, blocks, head, picker)
    stats = lax.all_to_all(stats, ("seq", "vocab"), 0, 0, tiled=True)
    near, far, far_last = gradients(n_seq, n_vocab, stats, logits, head)
    each, average = entropies(n_vocab, stats, picker)

    moved = swap_core(far_last)
    first = [(near[c][last].astype(F32) + moved[c].astype(F32)).astype(BF16) for c in range(PARTS)]
    far, first = lax.optimization_barrier((far, first))
    far = [swap_core(part) for part in far]
    sums = [[near[c][a].astype(F32) + far[c][a].astype(F32) for c in range(PARTS)] for a in range(last)]
    sums.append(first)
    for a in range(last, 0, -1):
        step = a.bit_length() - 1
        for c in range(PARTS):
            sums[a ^ (1 << step)][c] += swap_chip(sums[a][c].astype(BF16), step).astype(F32)

    column = lax.axis_index("vocab")

    def piece(k):
        parts = [lax.dynamic_index_in_dim(part, column ^ k, 0, keepdims=False) for part in sums[0]]
        return jnp.concatenate(parts, axis=1)

    result = piece(0)
    for k in range(n_vocab - 1, 0, -1):
        result = result + send_vocab(piece(k).astype(BF16), k).astype(F32)
    derivative = lax.dot_general(
        picker, result.astype(BF16), (((0,), (0,)), ((), ())), preferred_element_type=F32
    ).astype(BF16)
    return each.reshape(-1), average.reshape(()), derivative


def solution(mesh):
    n_seq, n_vocab = mesh.shape["seq"], mesh.shape["vocab"]

    def run(hidden, head, mask):
        return body(n_seq, n_vocab, hidden, head, mask)

    return jax.shard_map(
        run,
        mesh=mesh,
        in_specs=(P("seq", None), P(None, ("seq", "vocab")), P("seq")),
        out_specs=(P("seq"), P(), P("seq", "vocab")),
        check_vma=False,
    )
```

```python
import functools

import jax
import jax.numpy as jnp
from jax import lax
from jax.experimental import pallas as pl
from jax.experimental.pallas import tpu as pltpu
from jax.sharding import PartitionSpec as P

ACT_DEV = 16
PARTS = 2
LANES = 128
CHUNKS = 8
FLIGHT = 3
VMEM_BYTES = 24 * 2**20
F32, BF16 = jnp.float32, jnp.bfloat16


def params():
    return pltpu.CompilerParams(vmem_limit_bytes=VMEM_BYTES)


def in_hbm(value):
    return pltpu.with_memory_space_constraint(value, pltpu.HBM)


def iota(shape, axis):
    return lax.broadcasted_iota(jnp.int32, shape, axis)


def turn(bits, index):
    return sum(((index >> b) & 1) << (bits - 1 - b) for b in range(bits))


def row_order(n_seq):
    last = n_seq // 2 - 1
    early = [(core, chip) for core in (0, 1) for chip in range(last)]
    return early + [(0, last), (1, last)]


def owner_of(n_seq, core, chip):
    me = lax.axis_index("seq")
    bits = (n_seq // 2).bit_length() - 1
    odd = (me & 1) ^ core
    return me ^ (jnp.where(odd == 1, turn(bits, chip), chip) * 2 + core)


def lanes_of(n_seq):
    return -(-n_seq * ACT_DEV // LANES) * LANES


def arrive(copies, i):
    copies[i].wait()
    if i + FLIGHT < len(copies):
        copies[i + FLIGHT].start()


def select_kernel(mask_ref, hidden_ref, *refs):
    *own_refs, picker_ref, mask_here, hidden_here, mask_sem, sems = refs
    chunks, tokens, step = hidden_here.shape
    copies = [
        pltpu.make_async_copy(
            hidden_ref.at[:, pl.ds(i * step, step)], hidden_here.at[i], sems.at[i]
        )
        for i in range(chunks)
    ]
    mask_copy = pltpu.make_async_copy(mask_ref, mask_here, mask_sem)
    mask_copy.start()
    for copy in copies[:FLIGHT]:
        copy.start()
    mask_copy.wait()
    mask = mask_here[...]
    upper = (iota((tokens, tokens), 0) <= iota((tokens, tokens), 1)).astype(BF16)
    ones = jnp.broadcast_to(mask.astype(F32).astype(BF16), (ACT_DEV, tokens))
    slots = jnp.dot(ones, upper, preferred_element_type=F32).astype(jnp.int32) - 1
    picker = (slots == iota((ACT_DEV, tokens), 0)) & (mask == 1)
    picker = picker.astype(F32).astype(BF16)
    picker_ref[...] = picker
    each = chunks // len(own_refs)
    for i in range(chunks):
        arrive(copies, i)
        own = jnp.dot(picker, hidden_here[i], preferred_element_type=F32)
        at = (i % each) * step
        own_refs[i // each][:, at : at + step] = own.astype(BF16)


def select(mask, hidden):
    tokens, width = hidden.shape
    chunks = 4
    own = jax.ShapeDtypeStruct((ACT_DEV, width // PARTS), BF16)
    *own, picker = pl.pallas_call(
        select_kernel,
        in_specs=[pl.BlockSpec(memory_space=pltpu.HBM)] * 2,
        out_shape=[own] * PARTS + [jax.ShapeDtypeStruct((ACT_DEV, tokens), BF16)],
        scratch_shapes=[
            pltpu.VMEM((1, tokens), jnp.int32),
            pltpu.VMEM((chunks, tokens, width // chunks), BF16),
            pltpu.SemaphoreType.DMA,
            pltpu.SemaphoreType.DMA((chunks,)),
        ],
        compiler_params=params(),
        name="select_rows",
    )(in_hbm(mask.reshape(1, tokens)), in_hbm(hidden))
    return own, picker


def logits_kernel(n_seq, *refs):
    *block_refs, head_ref, picker_ref, logits_ref, stats_ref, packed = refs
    step = head_ref.shape[0] // CHUNKS
    each = CHUNKS // PARTS
    logits = None
    for i in range(CHUNKS):
        at = (i % each) * step
        rows = []
        for ref in block_refs:
            size = ref.shape[0] // PARTS
            start = (i // each) * size
            rows.append(ref[start : start + size, at : at + step])
        rows = jnp.concatenate(rows, axis=0)
        head = head_ref[i * step : (i + 1) * step, :]
        part = jnp.dot(rows, head, preferred_element_type=F32)
        logits = part if logits is None else logits + part
    logits_ref[...] = logits
    top = jnp.max(logits, axis=1, keepdims=True)
    away = logits - top
    ex = jnp.exp(away)
    sums = jnp.sum(ex, axis=1, keepdims=True)
    weighted = jnp.sum(ex * away, axis=1, keepdims=True)
    lane = iota((logits.shape[0], LANES), 1)
    pack = jnp.where(lane == 0, top, jnp.where(lane == 1, sums, weighted))
    if packed.shape[0] > n_seq * ACT_DEV:
        packed[...] = jnp.ones(packed.shape, F32)
    for q, (core, chip) in enumerate(row_order(n_seq)):
        place = pl.multiple_of(owner_of(n_seq, core, chip) * ACT_DEV, ACT_DEV)
        packed[pl.ds(place, ACT_DEV), :] = pack[q * ACT_DEV : (q + 1) * ACT_DEV]
    lines = packed[...].T[:4]
    count = jnp.sum(picker_ref[...].astype(F32))
    mine = iota(lines.shape, 1) // ACT_DEV == lax.axis_index("seq")
    lines = jnp.where(iota(lines.shape, 0) == 3, jnp.where(mine, count, 0.0), lines)
    stats_ref[...] = jnp.broadcast_to(lines[None], stats_ref.shape)


def local_logits(n_seq, n_vocab, blocks, head, picker):
    shard = head.shape[1]
    rows, lanes = n_seq * ACT_DEV, lanes_of(n_seq)
    return pl.pallas_call(
        functools.partial(logits_kernel, n_seq),
        in_specs=[pl.BlockSpec(memory_space=pltpu.VMEM)] * 6,
        out_shape=[
            jax.ShapeDtypeStruct((rows, shard), F32),
            jax.ShapeDtypeStruct((n_seq * n_vocab, 4, lanes), F32),
        ],
        scratch_shapes=[pltpu.VMEM((lanes, LANES), F32)],
        compiler_params=params(),
        name="local_logits",
    )(*blocks, head, picker)


def merged(stats):
    tops, sums, weights = stats[:, 0], stats[:, 1], stats[:, 2]
    top = jnp.max(tops, axis=0, keepdims=True)
    offset = tops - top
    scale = jnp.exp(offset)
    total = jnp.sum(scale * sums, axis=0, keepdims=True)
    weighted = jnp.sum(scale * (weights + offset * sums), axis=0, keepdims=True)
    return top, total, weighted / total


def entropy_kernel(n_vocab, stats_ref, picker_ref, each_ref, average_ref, column):
    stats = stats_ref[...]
    _, total, centred = merged(stats)
    entropy = jnp.log(total) - centred
    counts = jnp.sum(stats[:, 3], axis=0, keepdims=True) / n_vocab
    valid = (iota(entropy.shape, 1) % ACT_DEV).astype(F32) + 0.5 < counts
    sums = jnp.sum(jnp.where(valid, entropy, 0.0), axis=1, keepdims=True)
    average_ref[...] = sums / jnp.sum(valid.astype(F32), axis=1, keepdims=True)
    column[...] = jnp.broadcast_to(entropy, (LANES, entropy.shape[1])).T
    place = pl.multiple_of(lax.axis_index("seq") * ACT_DEV, ACT_DEV)
    mine = column[pl.ds(place, ACT_DEV), :][:, :1]
    picked = picker_ref[...].astype(F32) > 0.5
    each_ref[...] = jnp.sum(jnp.where(picked, mine, 0.0), axis=0, keepdims=True)


def entropies(n_vocab, stats, picker):
    tokens = picker.shape[1]
    return pl.pallas_call(
        functools.partial(entropy_kernel, n_vocab),
        out_shape=[
            jax.ShapeDtypeStruct((1, tokens), F32),
            jax.ShapeDtypeStruct((1, 1), F32),
        ],
        scratch_shapes=[pltpu.VMEM((stats.shape[2], LANES), F32)],
        compiler_params=params(),
        name="entropies",
    )(stats, picker)


def gradient_kernel(n_seq, n_vocab, stats_ref, logits_ref, head_ref, *refs):
    *out_refs, last_ref, columns, ordered = refs
    near_refs, far_refs = out_refs[:PARTS], out_refs[PARTS:]
    top, total, centred = merged(stats_ref[...])
    row = iota((8, top.shape[1]), 0)
    lines = jnp.where(row == 0, top, jnp.where(row == 1, 1.0 / total, top + centred))
    columns[...] = jnp.concatenate([lines] * (LANES // 8), axis=0).T
    for q, (core, chip) in enumerate(row_order(n_seq)):
        place = pl.multiple_of(owner_of(n_seq, core, chip) * ACT_DEV, ACT_DEV)
        ordered[q * ACT_DEV : (q + 1) * ACT_DEV] = columns[pl.ds(place, ACT_DEV), :]
    logits = logits_ref[...]
    prob = jnp.exp(logits - ordered[:, 0:1]) * ordered[:, 1:2]
    score = (prob * (ordered[:, 2:3] - logits)).astype(BF16)
    n_chip = n_seq // 2
    last = n_chip - 1
    size = near_refs[0].shape[3]
    for v in range(n_vocab):
        for c in range(PARTS):
            start = (v * PARTS + c) * size
            part = lax.dot_general(
                score,
                head_ref[start : start + size, :],
                (((1,), (1,)), ((), ())),
                preferred_element_type=F32,
            ).astype(BF16)
            blocks = part.reshape(n_seq, ACT_DEV, size)
            near_refs[c][:last, v] = blocks[:last]
            far_refs[c][:, v] = blocks[last : 2 * last]
            near_refs[c][last, v] = blocks[2 * last]
            last_ref[c, v] = blocks[2 * last + 1]


def gradients(n_seq, n_vocab, stats, logits, head):
    rows = logits.shape[0]
    n_chip = n_seq // 2
    block = (n_vocab, ACT_DEV, head.shape[0] // (n_vocab * PARTS))
    outs = [jax.ShapeDtypeStruct((n_chip,) + block, BF16)] * PARTS
    outs += [jax.ShapeDtypeStruct((n_chip - 1,) + block, BF16)] * PARTS
    outs += [jax.ShapeDtypeStruct((PARTS,) + block, BF16)]
    *outs, far_last = pl.pallas_call(
        functools.partial(gradient_kernel, n_seq, n_vocab),
        in_specs=[pl.BlockSpec(memory_space=pltpu.VMEM)] * 3,
        out_shape=outs,
        scratch_shapes=[
            pltpu.VMEM((stats.shape[2], LANES), F32),
            pltpu.VMEM((rows, LANES), F32),
        ],
        compiler_params=params(),
        name="gradients",
    )(stats, logits, head)
    return outs[:PARTS], outs[PARTS:], far_last


def body(n_seq, n_vocab, hidden, head, mask):
    n_chip = n_seq // 2
    last = n_chip - 1
    bits = n_chip.bit_length() - 1

    def swap_core(value):
        return lax.ppermute(value, "seq", [(i, i ^ 1) for i in range(n_seq)])

    def swap_chip(value, step):
        flips = (2 << step, 2 << (bits - 1 - step))
        return lax.ppermute(value, "seq", [(i, i ^ flips[i & 1]) for i in range(n_seq)])

    def send_vocab(value, k):
        return lax.ppermute(value, "vocab", [(i, i ^ k) for i in range(n_vocab)])

    own, picker = select(mask, hidden)

    near = [own]
    for a in range(1, n_chip):
        step = a.bit_length() - 1
        source = near[a ^ (1 << step)]
        if a > 1 and a == 1 << step:
            moved = swap_chip(jnp.concatenate(source, axis=1), step)
            near.append(jnp.split(moved, PARTS, axis=1))
        else:
            near.append([swap_chip(part, step) for part in source])
    early = jnp.concatenate([near[a][c] for c in range(PARTS) for a in range(last)], axis=0)
    early, near[last][0] = lax.optimization_barrier((early, near[last][0]))
    late = jnp.concatenate(near[last], axis=0)
    blocks = [early, swap_core(early), late, swap_core(late)]

    logits, stats = local_logits(n_seq, n_vocab, blocks, head, picker)
    stats = lax.all_to_all(stats, ("seq", "vocab"), 0, 0, tiled=True)
    near, far, far_last = gradients(n_seq, n_vocab, stats, logits, head)
    moved = swap_core(far_last)
    first = [(near[c][last].astype(F32) + moved[c].astype(F32)).astype(BF16) for c in range(PARTS)]
    far, first = lax.optimization_barrier((far, first))
    far = [swap_core(part) for part in far]
    sums = [[near[c][a].astype(F32) + far[c][a].astype(F32) for c in range(PARTS)] for a in range(last)]
    sums.append(first)
    for a in range(last, 0, -1):
        step = a.bit_length() - 1
        parts = [part.astype(BF16) for part in sums[a]]
        if a > 1 and a == 1 << step:
            moved = jnp.split(swap_chip(jnp.concatenate(parts, axis=2), step), PARTS, axis=2)
        else:
            moved = [swap_chip(part, step) for part in parts]
        target = sums[a ^ (1 << step)]
        for c in range(PARTS):
            target[c] += moved[c].astype(F32)

    stats, _ = lax.optimization_barrier((stats, sums[0]))
    each, average = entropies(n_vocab, stats, picker)
    column = lax.axis_index("vocab")

    def piece(k):
        parts = [lax.dynamic_index_in_dim(part, column ^ k, 0, keepdims=False) for part in sums[0]]
        return jnp.concatenate(parts, axis=1)

    result = piece(0)
    for k in range(n_vocab - 1, 0, -1):
        result = result + send_vocab(piece(k).astype(BF16), k).astype(F32)
    derivative = lax.dot_general(
        picker, result.astype(BF16), (((0,), (0,)), ((), ())), preferred_element_type=F32
    ).astype(BF16)
    return each.reshape(-1), average.reshape(()), derivative


def solution(mesh):
    n_seq, n_vocab = mesh.shape["seq"], mesh.shape["vocab"]

    def run(hidden, head, mask):
        return body(n_seq, n_vocab, hidden, head, mask)

    return jax.shard_map(
        run,
        mesh=mesh,
        in_specs=(P("seq", None), P(None, ("seq", "vocab")), P("seq")),
        out_specs=(P("seq"), P(), P("seq", "vocab")),
        check_vma=False,
    )
```

```python
import functools

import jax
import jax.numpy as jnp
from jax import lax
from jax.experimental import pallas as pl
from jax.experimental.pallas import tpu as pltpu
from jax.sharding import PartitionSpec as P

ACT_DEV = 16
PARTS = 2
LANES = 128
CHUNKS = 8
FLIGHT = 3
VMEM_BYTES = 24 * 2**20
F32, BF16 = jnp.float32, jnp.bfloat16


def params():
    return pltpu.CompilerParams(vmem_limit_bytes=VMEM_BYTES)


def in_hbm(value):
    return pltpu.with_memory_space_constraint(value, pltpu.HBM)


def iota(shape, axis):
    return lax.broadcasted_iota(jnp.int32, shape, axis)


def turn(bits, index):
    return sum(((index >> b) & 1) << (bits - 1 - b) for b in range(bits))


def row_order(n_seq):
    n_chip = n_seq // 2
    cut = n_chip // 2
    groups = [(core, range(low, low + cut)) for low in (0, cut) for core in (0, 1)]
    return [(core, chip) for core, chips in groups for chip in chips]


def owner_of(n_seq, core, chip):
    me = lax.axis_index("seq")
    bits = (n_seq // 2).bit_length() - 1
    odd = (me & 1) ^ core
    return me ^ (jnp.where(odd == 1, turn(bits, chip), chip) * 2 + core)


def lanes_of(n_seq):
    return -(-n_seq * ACT_DEV // LANES) * LANES


def arrive(copies, i):
    copies[i].wait()
    if i + FLIGHT < len(copies):
        copies[i + FLIGHT].start()


def select_kernel(mask_ref, hidden_ref, *refs):
    *own_refs, picker_ref, mask_here, hidden_here, mask_sem, sems = refs
    chunks, tokens, step = hidden_here.shape
    copies = [
        pltpu.make_async_copy(
            hidden_ref.at[:, pl.ds(i * step, step)], hidden_here.at[i], sems.at[i]
        )
        for i in range(chunks)
    ]
    mask_copy = pltpu.make_async_copy(mask_ref, mask_here, mask_sem)
    mask_copy.start()
    for copy in copies[:FLIGHT]:
        copy.start()
    mask_copy.wait()
    mask = mask_here[...]
    upper = (iota((tokens, tokens), 0) <= iota((tokens, tokens), 1)).astype(BF16)
    ones = jnp.broadcast_to(mask.astype(F32).astype(BF16), (ACT_DEV, tokens))
    slots = jnp.dot(ones, upper, preferred_element_type=F32).astype(jnp.int32) - 1
    picker = (slots == iota((ACT_DEV, tokens), 0)) & (mask == 1)
    picker = picker.astype(F32).astype(BF16)
    picker_ref[...] = picker
    each = chunks // len(own_refs)
    for i in range(chunks):
        arrive(copies, i)
        own = jnp.dot(picker, hidden_here[i], preferred_element_type=F32)
        at = (i % each) * step
        own_refs[i // each][:, at : at + step] = own.astype(BF16)


def select(mask, hidden):
    tokens, width = hidden.shape
    chunks = 4
    own = jax.ShapeDtypeStruct((ACT_DEV, width // PARTS), BF16)
    *own, picker = pl.pallas_call(
        select_kernel,
        in_specs=[pl.BlockSpec(memory_space=pltpu.HBM)] * 2,
        out_shape=[own] * PARTS + [jax.ShapeDtypeStruct((ACT_DEV, tokens), BF16)],
        scratch_shapes=[
            pltpu.VMEM((1, tokens), jnp.int32),
            pltpu.VMEM((chunks, tokens, width // chunks), BF16),
            pltpu.SemaphoreType.DMA,
            pltpu.SemaphoreType.DMA((chunks,)),
        ],
        compiler_params=params(),
        name="select_rows",
    )(in_hbm(mask.reshape(1, tokens)), in_hbm(hidden))
    return own, picker


def logits_kernel(n_seq, *refs):
    *block_refs, head_ref, picker_ref, logits_ref, stats_ref, packed = refs
    step = head_ref.shape[0] // CHUNKS
    each = CHUNKS // PARTS
    logits = None
    for i in range(CHUNKS):
        at = (i % each) * step
        rows = []
        for ref in block_refs:
            size = ref.shape[0] // PARTS
            start = (i // each) * size
            rows.append(ref[start : start + size, at : at + step])
        rows = jnp.concatenate(rows, axis=0)
        head = head_ref[i * step : (i + 1) * step, :]
        part = jnp.dot(rows, head, preferred_element_type=F32)
        logits = part if logits is None else logits + part
    logits_ref[...] = logits
    top = jnp.max(logits, axis=1, keepdims=True)
    away = logits - top
    ex = jnp.exp(away)
    sums = jnp.sum(ex, axis=1, keepdims=True)
    weighted = jnp.sum(ex * away, axis=1, keepdims=True)
    lane = iota((logits.shape[0], LANES), 1)
    pack = jnp.where(lane == 0, top, jnp.where(lane == 1, sums, weighted))
    if packed.shape[0] > n_seq * ACT_DEV:
        packed[...] = jnp.ones(packed.shape, F32)
    for q, (core, chip) in enumerate(row_order(n_seq)):
        place = pl.multiple_of(owner_of(n_seq, core, chip) * ACT_DEV, ACT_DEV)
        packed[pl.ds(place, ACT_DEV), :] = pack[q * ACT_DEV : (q + 1) * ACT_DEV]
    lines = packed[...].T[:4]
    count = jnp.sum(picker_ref[...].astype(F32))
    mine = iota(lines.shape, 1) // ACT_DEV == lax.axis_index("seq")
    lines = jnp.where(iota(lines.shape, 0) == 3, jnp.where(mine, count, 0.0), lines)
    stats_ref[...] = jnp.broadcast_to(lines[None], stats_ref.shape)


def local_logits(n_seq, n_vocab, blocks, head, picker):
    shard = head.shape[1]
    rows, lanes = n_seq * ACT_DEV, lanes_of(n_seq)
    return pl.pallas_call(
        functools.partial(logits_kernel, n_seq),
        in_specs=[pl.BlockSpec(memory_space=pltpu.VMEM)] * 6,
        out_shape=[
            jax.ShapeDtypeStruct((rows, shard), F32),
            jax.ShapeDtypeStruct((n_seq * n_vocab, 4, lanes), F32),
        ],
        scratch_shapes=[pltpu.VMEM((lanes, LANES), F32)],
        compiler_params=params(),
        name="local_logits",
    )(*blocks, head, picker)


def merged(stats):
    tops, sums, weights = stats[:, 0], stats[:, 1], stats[:, 2]
    top = jnp.max(tops, axis=0, keepdims=True)
    offset = tops - top
    scale = jnp.exp(offset)
    total = jnp.sum(scale * sums, axis=0, keepdims=True)
    weighted = jnp.sum(scale * (weights + offset * sums), axis=0, keepdims=True)
    return top, total, weighted / total


def entropy_kernel(n_vocab, stats_ref, picker_ref, each_ref, average_ref, column):
    stats = stats_ref[...]
    _, total, centred = merged(stats)
    entropy = jnp.log(total) - centred
    counts = jnp.sum(stats[:, 3], axis=0, keepdims=True) / n_vocab
    valid = (iota(entropy.shape, 1) % ACT_DEV).astype(F32) + 0.5 < counts
    sums = jnp.sum(jnp.where(valid, entropy, 0.0), axis=1, keepdims=True)
    average_ref[...] = sums / jnp.sum(valid.astype(F32), axis=1, keepdims=True)
    column[...] = jnp.broadcast_to(entropy, (LANES, entropy.shape[1])).T
    place = pl.multiple_of(lax.axis_index("seq") * ACT_DEV, ACT_DEV)
    mine = column[pl.ds(place, ACT_DEV), :][:, :1]
    picked = picker_ref[...].astype(F32) > 0.5
    each_ref[...] = jnp.sum(jnp.where(picked, mine, 0.0), axis=0, keepdims=True)


def entropies(n_vocab, stats, picker):
    tokens = picker.shape[1]
    return pl.pallas_call(
        functools.partial(entropy_kernel, n_vocab),
        out_shape=[
            jax.ShapeDtypeStruct((1, tokens), F32),
            jax.ShapeDtypeStruct((1, 1), F32),
        ],
        scratch_shapes=[pltpu.VMEM((stats.shape[2], LANES), F32)],
        compiler_params=params(),
        name="entropies",
    )(stats, picker)


def score_product(score_ref, picks, head_ref, out_refs):
    rows = [score_ref[q * ACT_DEV : (q + 1) * ACT_DEV, :] for q in picks]
    rows = jnp.concatenate(rows, axis=0)
    _, n_vocab, _, size = out_refs[0].shape
    for v in range(n_vocab):
        for c in range(PARTS):
            start = (v * PARTS + c) * size
            part = lax.dot_general(
                rows,
                head_ref[start : start + size, :],
                (((1,), (1,)), ((), ())),
                preferred_element_type=F32,
            ).astype(BF16)
            blocks = part.reshape(len(picks), ACT_DEV, size)
            half = len(picks) // 2
            out_refs[c][:, v] = blocks[:half]
            out_refs[PARTS + c][:, v] = blocks[half:]


def first_kernel(n_seq, stats_ref, logits_ref, head_ref, *refs):
    *out_refs, score, columns, ordered = refs
    top, total, centred = merged(stats_ref[...])
    row = iota((8, top.shape[1]), 0)
    lines = jnp.where(row == 0, top, jnp.where(row == 1, 1.0 / total, top + centred))
    columns[...] = jnp.concatenate([lines] * (LANES // 8), axis=0).T
    for q, (core, chip) in enumerate(row_order(n_seq)):
        place = pl.multiple_of(owner_of(n_seq, core, chip) * ACT_DEV, ACT_DEV)
        ordered[q * ACT_DEV : (q + 1) * ACT_DEV] = columns[pl.ds(place, ACT_DEV), :]
    logits = logits_ref[...]
    prob = jnp.exp(logits - ordered[:, 0:1]) * ordered[:, 1:2]
    score[...] = (prob * (ordered[:, 2:3] - logits)).astype(BF16)
    order = row_order(n_seq)
    last = n_seq // 2 - 1
    score_product(score, [order.index((core, last)) for core in (0, 1)], head_ref, out_refs)


def rest_kernel(n_seq, score_ref, head_ref, *out_refs):
    order = row_order(n_seq)
    last = n_seq // 2 - 1
    picks = [order.index((core, chip)) for core in (0, 1) for chip in range(last)]
    score_product(score_ref, picks, head_ref, out_refs)


def gradients(n_seq, n_vocab, stats, logits, head):
    rows = logits.shape[0]
    last = n_seq // 2 - 1
    block = (n_vocab, ACT_DEV, head.shape[0] // (n_vocab * PARTS))
    vmem = pl.BlockSpec(memory_space=pltpu.VMEM)
    out = jax.ShapeDtypeStruct((1,) + block, BF16)
    *first, score = pl.pallas_call(
        functools.partial(first_kernel, n_seq),
        in_specs=[vmem] * 3,
        out_shape=[out] * 2 * PARTS + [jax.ShapeDtypeStruct(logits.shape, BF16)],
        scratch_shapes=[
            pltpu.VMEM((stats.shape[2], LANES), F32),
            pltpu.VMEM((rows, LANES), F32),
        ],
        compiler_params=params(),
        name="last_gradients",
    )(stats, logits, head)
    out = jax.ShapeDtypeStruct((last,) + block, BF16)
    rest = pl.pallas_call(
        functools.partial(rest_kernel, n_seq),
        in_specs=[vmem] * 2,
        out_shape=[out] * 2 * PARTS,
        cost_estimate=pl.CostEstimate(
            flops=2 * rows * head.size, bytes_accessed=2 * head.size, transcendentals=0
        ),
        compiler_params=params(),
        name="other_gradients",
    )(score, head)
    return first[:PARTS], first[PARTS:], rest[:PARTS], rest[PARTS:]


def body(n_seq, n_vocab, hidden, head, mask):
    n_chip = n_seq // 2
    last = n_chip - 1
    bits = n_chip.bit_length() - 1

    def swap_core(value):
        return lax.ppermute(value, "seq", [(i, i ^ 1) for i in range(n_seq)])

    def swap_chip(value, step):
        flips = (2 << step, 2 << (bits - 1 - step))
        return lax.ppermute(value, "seq", [(i, i ^ flips[i & 1]) for i in range(n_seq)])

    def send_vocab(value, k):
        return lax.ppermute(value, "vocab", [(i, i ^ k) for i in range(n_vocab)])

    own, picker = select(mask, hidden)

    near = [own]
    cut = n_chip // 2
    for a in range(1, n_chip):
        step = a.bit_length() - 1
        source = near[a ^ (1 << step)]
        if a > 1 and a == 1 << step:
            source, near[1][-1] = lax.optimization_barrier((source, near[1][-1]))
            moved = swap_chip(jnp.concatenate(source, axis=1), step)
            near.append(jnp.split(moved, PARTS, axis=1))
        else:
            near.append([swap_chip(part, step) for part in source])

    def gather_rows(chips):
        return jnp.concatenate([near[a][c] for c in range(PARTS) for a in chips], axis=0)

    early, late = gather_rows(range(cut)), gather_rows(range(cut, n_chip))
    blocks = [early, swap_core(early), late, swap_core(late)]

    logits, stats = local_logits(n_seq, n_vocab, blocks, head, picker)
    stats = lax.all_to_all(stats, ("seq", "vocab"), 0, 0, tiled=True)
    near_last, far_last, near, far = gradients(n_seq, n_vocab, stats, logits, head)

    moved = [swap_core(part) for part in far_last]
    first = [(near_last[c][0].astype(F32) + moved[c][0].astype(F32)).astype(BF16) for c in range(PARTS)]
    far, first = lax.optimization_barrier((far, first))
    far = [swap_core(part) for part in far]
    sums = [[near[c][a].astype(F32) + far[c][a].astype(F32) for c in range(PARTS)] for a in range(last)]
    sums.append(first)
    for a in range(last, 0, -1):
        step = a.bit_length() - 1
        parts = [part.astype(BF16) for part in sums[a]]
        if a > 1 and a == 1 << step:
            moved = jnp.split(swap_chip(jnp.concatenate(parts, axis=2), step), PARTS, axis=2)
        else:
            moved = [swap_chip(part, step) for part in parts]
        target = sums[a ^ (1 << step)]
        for c in range(PARTS):
            target[c] += moved[c].astype(F32)

    stats, _ = lax.optimization_barrier((stats, sums[0]))
    each, average = entropies(n_vocab, stats, picker)
    column = lax.axis_index("vocab")

    def piece(k):
        parts = [lax.dynamic_index_in_dim(part, column ^ k, 0, keepdims=False) for part in sums[0]]
        return jnp.concatenate(parts, axis=1)

    result = piece(0)
    for k in range(n_vocab - 1, 0, -1):
        result = result + send_vocab(piece(k).astype(BF16), k).astype(F32)
    derivative = lax.dot_general(
        picker, result.astype(BF16), (((0,), (0,)), ((), ())), preferred_element_type=F32
    ).astype(BF16)
    return each.reshape(-1), average.reshape(()), derivative


def solution(mesh):
    n_seq, n_vocab = mesh.shape["seq"], mesh.shape["vocab"]

    def run(hidden, head, mask):
        return body(n_seq, n_vocab, hidden, head, mask)

    return jax.shard_map(
        run,
        mesh=mesh,
        in_specs=(P("seq", None), P(None, ("seq", "vocab")), P("seq")),
        out_specs=(P("seq"), P(), P("seq", "vocab")),
        check_vma=False,
    )
```

```python
import functools

import jax
import jax.numpy as jnp
from jax import lax
from jax.experimental import pallas as pl
from jax.experimental.pallas import tpu as pltpu
from jax.sharding import PartitionSpec as P

ACT_DEV = 16
PARTS = 2
LANES = 128
CHUNKS = 8
VMEM_BYTES = 24 * 2**20
F32, BF16 = jnp.float32, jnp.bfloat16


def params():
    return pltpu.CompilerParams(vmem_limit_bytes=VMEM_BYTES)


def in_hbm(value):
    return pltpu.with_memory_space_constraint(value, pltpu.HBM)


def iota(shape, axis):
    return lax.broadcasted_iota(jnp.int32, shape, axis)


def turn(bits, index):
    return sum(((index >> b) & 1) << (bits - 1 - b) for b in range(bits))


def row_order(n_seq):
    n_chip = n_seq // 2
    cut = n_chip // 2
    groups = [(core, range(low, low + cut)) for low in (0, cut) for core in (0, 1)]
    return [(core, chip) for core, chips in groups for chip in chips]


def owner_of(n_seq, core, chip):
    me = lax.axis_index("seq")
    bits = (n_seq // 2).bit_length() - 1
    odd = (me & 1) ^ core
    return me ^ (jnp.where(odd == 1, turn(bits, chip), chip) * 2 + core)


def lanes_of(n_seq):
    return -(-n_seq * ACT_DEV // LANES) * LANES


def select_kernel(mask_ref, hidden_ref, *refs):
    *own_refs, picker_ref, mask_here, hidden_here, mask_sem, sems = refs
    chunks, tokens, step = hidden_here.shape
    copies = [
        pltpu.make_async_copy(
            hidden_ref.at[:, pl.ds(i * step, step)], hidden_here.at[i], sems.at[i]
        )
        for i in range(chunks)
    ]
    mask_copy = pltpu.make_async_copy(mask_ref, mask_here, mask_sem)
    mask_copy.start()
    for copy in copies:
        copy.start()
    mask_copy.wait()
    mask = mask_here[...]
    upper = (iota((tokens, tokens), 0) <= iota((tokens, tokens), 1)).astype(BF16)
    ones = jnp.broadcast_to(mask.astype(F32).astype(BF16), (ACT_DEV, tokens))
    slots = jnp.dot(ones, upper, preferred_element_type=F32).astype(jnp.int32) - 1
    picker = (slots == iota((ACT_DEV, tokens), 0)) & (mask == 1)
    picker = picker.astype(F32).astype(BF16)
    picker_ref[...] = picker
    each = chunks // len(own_refs)
    for i in range(chunks):
        copies[i].wait()
        own = jnp.dot(picker, hidden_here[i], preferred_element_type=F32)
        at = (i % each) * step
        own_refs[i // each][:, at : at + step] = own.astype(BF16)


def select(mask, hidden):
    tokens, width = hidden.shape
    chunks = CHUNKS
    own = jax.ShapeDtypeStruct((ACT_DEV, width // PARTS), BF16)
    *own, picker = pl.pallas_call(
        select_kernel,
        in_specs=[pl.BlockSpec(memory_space=pltpu.HBM)] * 2,
        out_shape=[own] * PARTS + [jax.ShapeDtypeStruct((ACT_DEV, tokens), BF16)],
        scratch_shapes=[
            pltpu.VMEM((1, tokens), jnp.int32),
            pltpu.VMEM((chunks, tokens, width // chunks), BF16),
            pltpu.SemaphoreType.DMA,
            pltpu.SemaphoreType.DMA((chunks,)),
        ],
        compiler_params=params(),
        name="select_rows",
    )(in_hbm(mask.reshape(1, tokens)), in_hbm(hidden))
    return own, picker


def logits_kernel(n_seq, *refs):
    *block_refs, head_ref, picker_ref, logits_ref, stats_ref, packed = refs
    step = head_ref.shape[0] // CHUNKS
    each = CHUNKS // PARTS
    logits = None
    for i in range(CHUNKS):
        at = (i % each) * step
        rows = []
        for ref in block_refs:
            size = ref.shape[0] // PARTS
            start = (i // each) * size
            rows.append(ref[start : start + size, at : at + step])
        rows = jnp.concatenate(rows, axis=0)
        head = head_ref[i * step : (i + 1) * step, :]
        part = jnp.dot(rows, head, preferred_element_type=F32)
        logits = part if logits is None else logits + part
    logits_ref[...] = logits
    top = jnp.max(logits, axis=1, keepdims=True)
    away = logits - top
    ex = jnp.exp(away)
    sums = jnp.sum(ex, axis=1, keepdims=True)
    weighted = jnp.sum(ex * away, axis=1, keepdims=True)
    lane = iota((logits.shape[0], LANES), 1)
    pack = jnp.where(lane == 0, top, jnp.where(lane == 1, sums, weighted))
    if packed.shape[0] > n_seq * ACT_DEV:
        packed[...] = jnp.ones(packed.shape, F32)
    for q, (core, chip) in enumerate(row_order(n_seq)):
        place = pl.multiple_of(owner_of(n_seq, core, chip) * ACT_DEV, ACT_DEV)
        packed[pl.ds(place, ACT_DEV), :] = pack[q * ACT_DEV : (q + 1) * ACT_DEV]
    lines = packed[...].T[:4]
    count = jnp.sum(picker_ref[...].astype(F32))
    mine = iota(lines.shape, 1) // ACT_DEV == lax.axis_index("seq")
    lines = jnp.where(iota(lines.shape, 0) == 3, jnp.where(mine, count, 0.0), lines)
    stats_ref[...] = jnp.broadcast_to(lines[None], stats_ref.shape)


def local_logits(n_seq, n_vocab, blocks, head, picker):
    shard = head.shape[1]
    rows, lanes = n_seq * ACT_DEV, lanes_of(n_seq)
    return pl.pallas_call(
        functools.partial(logits_kernel, n_seq),
        in_specs=[pl.BlockSpec(memory_space=pltpu.VMEM)] * 6,
        out_shape=[
            jax.ShapeDtypeStruct((rows, shard), F32),
            jax.ShapeDtypeStruct((n_seq * n_vocab, 4, lanes), F32),
        ],
        scratch_shapes=[pltpu.VMEM((lanes, LANES), F32)],
        compiler_params=params(),
        name="local_logits",
    )(*blocks, head, picker)


def merged(stats):
    tops, sums, weights = stats[:, 0], stats[:, 1], stats[:, 2]
    top = jnp.max(tops, axis=0, keepdims=True)
    offset = tops - top
    scale = jnp.exp(offset)
    total = jnp.sum(scale * sums, axis=0, keepdims=True)
    weighted = jnp.sum(scale * (weights + offset * sums), axis=0, keepdims=True)
    return top, total, weighted / total


def entropy_kernel(n_vocab, stats_ref, picker_ref, each_ref, average_ref, column):
    stats = stats_ref[...]
    _, total, centred = merged(stats)
    entropy = jnp.log(total) - centred
    counts = jnp.sum(stats[:, 3], axis=0, keepdims=True) / n_vocab
    valid = (iota(entropy.shape, 1) % ACT_DEV).astype(F32) + 0.5 < counts
    sums = jnp.sum(jnp.where(valid, entropy, 0.0), axis=1, keepdims=True)
    average_ref[...] = sums / jnp.sum(valid.astype(F32), axis=1, keepdims=True)
    column[...] = jnp.broadcast_to(entropy, (LANES, entropy.shape[1])).T
    place = pl.multiple_of(lax.axis_index("seq") * ACT_DEV, ACT_DEV)
    mine = column[pl.ds(place, ACT_DEV), :][:, :1]
    picked = picker_ref[...].astype(F32) > 0.5
    each_ref[...] = jnp.sum(jnp.where(picked, mine, 0.0), axis=0, keepdims=True)


def entropies(n_vocab, stats, picker):
    tokens = picker.shape[1]
    return pl.pallas_call(
        functools.partial(entropy_kernel, n_vocab),
        out_shape=[
            jax.ShapeDtypeStruct((1, tokens), F32),
            jax.ShapeDtypeStruct((1, 1), F32),
        ],
        scratch_shapes=[pltpu.VMEM((stats.shape[2], LANES), F32)],
        compiler_params=params(),
        name="entropies",
    )(stats, picker)


def gradient_kernel(n_seq, n_vocab, stats_ref, logits_ref, head_ref, *refs):
    *out_refs, last_ref, columns, ordered = refs
    near_refs, far_refs = out_refs[:PARTS], out_refs[PARTS:]
    top, total, centred = merged(stats_ref[...])
    row = iota((8, top.shape[1]), 0)
    lines = jnp.where(row == 0, top, jnp.where(row == 1, 1.0 / total, top + centred))
    columns[...] = jnp.concatenate([lines] * (LANES // 8), axis=0).T
    for q, (core, chip) in enumerate(row_order(n_seq)):
        place = pl.multiple_of(owner_of(n_seq, core, chip) * ACT_DEV, ACT_DEV)
        ordered[q * ACT_DEV : (q + 1) * ACT_DEV] = columns[pl.ds(place, ACT_DEV), :]
    logits = logits_ref[...]
    prob = jnp.exp(logits - ordered[:, 0:1]) * ordered[:, 1:2]
    score = (prob * (ordered[:, 2:3] - logits)).astype(BF16)
    cut = n_seq // 4
    size = near_refs[0].shape[3]
    for v in range(n_vocab):
        for c in range(PARTS):
            start = (v * PARTS + c) * size
            part = lax.dot_general(
                score,
                head_ref[start : start + size, :],
                (((1,), (1,)), ((), ())),
                preferred_element_type=F32,
            ).astype(BF16)
            blocks = part.reshape(n_seq, ACT_DEV, size)
            near_refs[c][:cut, v] = blocks[:cut]
            far_refs[c][:cut, v] = blocks[cut : 2 * cut]
            near_refs[c][cut:, v] = blocks[2 * cut : 3 * cut]
            far_refs[c][cut:, v] = blocks[3 * cut : 4 * cut - 1]
            last_ref[c, v] = blocks[4 * cut - 1]


def gradients(n_seq, n_vocab, stats, logits, head):
    rows = logits.shape[0]
    n_chip = n_seq // 2
    block = (n_vocab, ACT_DEV, head.shape[0] // (n_vocab * PARTS))
    outs = [jax.ShapeDtypeStruct((n_chip,) + block, BF16)] * PARTS
    outs += [jax.ShapeDtypeStruct((n_chip - 1,) + block, BF16)] * PARTS
    outs += [jax.ShapeDtypeStruct((PARTS,) + block, BF16)]
    *outs, far_last = pl.pallas_call(
        functools.partial(gradient_kernel, n_seq, n_vocab),
        in_specs=[pl.BlockSpec(memory_space=pltpu.VMEM)] * 3,
        out_shape=outs,
        scratch_shapes=[
            pltpu.VMEM((stats.shape[2], LANES), F32),
            pltpu.VMEM((rows, LANES), F32),
        ],
        compiler_params=params(),
        name="gradients",
    )(stats, logits, head)
    return outs[:PARTS], outs[PARTS:], far_last


def body(n_seq, n_vocab, hidden, head, mask):
    n_chip = n_seq // 2
    last = n_chip - 1
    bits = n_chip.bit_length() - 1

    def swap_core(value):
        return lax.ppermute(value, "seq", [(i, i ^ 1) for i in range(n_seq)])

    def swap_chip(value, step):
        flips = (2 << step, 2 << (bits - 1 - step))
        return lax.ppermute(value, "seq", [(i, i ^ flips[i & 1]) for i in range(n_seq)])

    def send_vocab(value, k):
        return lax.ppermute(value, "vocab", [(i, i ^ k) for i in range(n_vocab)])

    own, picker = select(mask, hidden)

    near = [own]
    cut = n_chip // 2
    for a in range(1, n_chip):
        step = a.bit_length() - 1
        source = near[a ^ (1 << step)]
        if a > 1 and a == 1 << step:
            source, _ = lax.optimization_barrier((source, near[1]))
        near.append([swap_chip(part, step) for part in source])

    def gather_rows(chips):
        return jnp.concatenate([near[a][c] for c in range(PARTS) for a in chips], axis=0)

    early, late = gather_rows(range(cut)), gather_rows(range(cut, n_chip))
    blocks = [early, swap_core(early), late, swap_core(late)]

    logits, stats = local_logits(n_seq, n_vocab, blocks, head, picker)
    stats = lax.all_to_all(stats, ("seq", "vocab"), 0, 0, tiled=True)
    near, far, far_last = gradients(n_seq, n_vocab, stats, logits, head)
    moved = swap_core(far_last)
    first = [(near[c][last].astype(F32) + moved[c].astype(F32)).astype(BF16) for c in range(PARTS)]
    far, first = lax.optimization_barrier((far, first))
    far = [swap_core(part) for part in far]
    sums = [[near[c][a].astype(F32) + far[c][a].astype(F32) for c in range(PARTS)] for a in range(last)]
    sums.append(first)
    for a in range(last, 0, -1):
        step = a.bit_length() - 1
        parts = [part.astype(BF16) for part in sums[a]]
        if a > 1 and a == 1 << step:
            moved = jnp.split(swap_chip(jnp.concatenate(parts, axis=2), step), PARTS, axis=2)
        else:
            moved = [swap_chip(part, step) for part in parts]
        target = sums[a ^ (1 << step)]
        for c in range(PARTS):
            target[c] += moved[c].astype(F32)

    stats, _ = lax.optimization_barrier((stats, sums[0]))
    each, average = entropies(n_vocab, stats, picker)
    column = lax.axis_index("vocab")

    def piece(k):
        parts = [lax.dynamic_index_in_dim(part, column ^ k, 0, keepdims=False) for part in sums[0]]
        return jnp.concatenate(parts, axis=1)

    result = piece(0)
    for k in range(n_vocab - 1, 0, -1):
        result = result + send_vocab(piece(k).astype(BF16), k).astype(F32)
    derivative = lax.dot_general(
        picker, result.astype(BF16), (((0,), (0,)), ((), ())), preferred_element_type=F32
    ).astype(BF16)
    return each.reshape(-1), average.reshape(()), derivative


def solution(mesh):
    n_seq, n_vocab = mesh.shape["seq"], mesh.shape["vocab"]

    def run(hidden, head, mask):
        return body(n_seq, n_vocab, hidden, head, mask)

    return jax.shard_map(
        run,
        mesh=mesh,
        in_specs=(P("seq", None), P(None, ("seq", "vocab")), P("seq")),
        out_specs=(P("seq"), P(), P("seq", "vocab")),
        check_vma=False,
    )
```

```python
import functools

import jax
import jax.numpy as jnp
from jax import lax
from jax.experimental import pallas as pl
from jax.experimental.pallas import tpu as pltpu
from jax.sharding import PartitionSpec as P

ACT_DEV = 16
PARTS = 2
LANES = 128
CHUNKS = 8
FLIGHT = 3
VMEM_BYTES = 24 * 2**20
F32, BF16 = jnp.float32, jnp.bfloat16


def params():
    return pltpu.CompilerParams(vmem_limit_bytes=VMEM_BYTES)


def in_hbm(value):
    return pltpu.with_memory_space_constraint(value, pltpu.HBM)


def iota(shape, axis):
    return lax.broadcasted_iota(jnp.int32, shape, axis)


def turn(bits, index):
    return sum(((index >> b) & 1) << (bits - 1 - b) for b in range(bits))


def row_order(n_seq):
    last = n_seq // 2 - 1
    early = [(core, chip) for core in (0, 1) for chip in range(last)]
    return early + [(0, last), (1, last)]


def owner_of(n_seq, core, chip):
    me = lax.axis_index("seq")
    bits = (n_seq // 2).bit_length() - 1
    odd = (me & 1) ^ core
    return me ^ (jnp.where(odd == 1, turn(bits, chip), chip) * 2 + core)


def lanes_of(n_seq):
    return -(-n_seq * ACT_DEV // LANES) * LANES


def arrive(copies, i):
    copies[i].wait()
    if i + FLIGHT < len(copies):
        copies[i + FLIGHT].start()


def select_kernel(mask_ref, hidden_ref, *refs):
    *own_refs, picker_ref, mask_here, hidden_here, mask_sem, sems = refs
    chunks, tokens, step = hidden_here.shape
    copies = [
        pltpu.make_async_copy(
            hidden_ref.at[:, pl.ds(i * step, step)], hidden_here.at[i], sems.at[i]
        )
        for i in range(chunks)
    ]
    mask_copy = pltpu.make_async_copy(mask_ref, mask_here, mask_sem)
    mask_copy.start()
    for copy in copies[:FLIGHT]:
        copy.start()
    mask_copy.wait()
    mask = mask_here[...]
    upper = (iota((tokens, tokens), 0) <= iota((tokens, tokens), 1)).astype(BF16)
    ones = jnp.broadcast_to(mask.astype(F32).astype(BF16), (ACT_DEV, tokens))
    slots = jnp.dot(ones, upper, preferred_element_type=F32).astype(jnp.int32) - 1
    picker = (slots == iota((ACT_DEV, tokens), 0)) & (mask == 1)
    picker = picker.astype(F32).astype(BF16)
    picker_ref[...] = picker
    each = chunks // len(own_refs)
    for i in range(chunks):
        arrive(copies, i)
        own = jnp.dot(picker, hidden_here[i], preferred_element_type=F32)
        at = (i % each) * step
        own_refs[i // each][:, at : at + step] = own.astype(BF16)


def select(mask, hidden):
    tokens, width = hidden.shape
    chunks = 4
    own = jax.ShapeDtypeStruct((ACT_DEV, width // PARTS), BF16)
    *own, picker = pl.pallas_call(
        select_kernel,
        in_specs=[pl.BlockSpec(memory_space=pltpu.HBM)] * 2,
        out_shape=[own] * PARTS + [jax.ShapeDtypeStruct((ACT_DEV, tokens), BF16)],
        scratch_shapes=[
            pltpu.VMEM((1, tokens), jnp.int32),
            pltpu.VMEM((chunks, tokens, width // chunks), BF16),
            pltpu.SemaphoreType.DMA,
            pltpu.SemaphoreType.DMA((chunks,)),
        ],
        compiler_params=params(),
        name="select_rows",
    )(in_hbm(mask.reshape(1, tokens)), in_hbm(hidden))
    return own, picker


def logits_kernel(n_seq, *refs):
    *block_refs, head_ref, picker_ref, logits_ref, stats_ref, packed = refs
    step = head_ref.shape[0] // CHUNKS
    each = CHUNKS // PARTS
    logits = None
    for i in range(CHUNKS):
        at = (i % each) * step
        rows = []
        for ref in block_refs:
            size = ref.shape[0] // PARTS
            start = (i // each) * size
            rows.append(ref[start : start + size, at : at + step])
        rows = jnp.concatenate(rows, axis=0)
        head = head_ref[i * step : (i + 1) * step, :]
        part = jnp.dot(rows, head, preferred_element_type=F32)
        logits = part if logits is None else logits + part
    logits_ref[...] = logits
    top = jnp.max(logits, axis=1, keepdims=True)
    away = logits - top
    ex = jnp.exp(away)
    sums = jnp.sum(ex, axis=1, keepdims=True)
    weighted = jnp.sum(ex * away, axis=1, keepdims=True)
    lane = iota((logits.shape[0], LANES), 1)
    pack = jnp.where(lane == 0, top, jnp.where(lane == 1, sums, weighted))
    if packed.shape[0] > n_seq * ACT_DEV:
        packed[...] = jnp.ones(packed.shape, F32)
    for q, (core, chip) in enumerate(row_order(n_seq)):
        place = pl.multiple_of(owner_of(n_seq, core, chip) * ACT_DEV, ACT_DEV)
        packed[pl.ds(place, ACT_DEV), :] = pack[q * ACT_DEV : (q + 1) * ACT_DEV]
    lines = packed[...].T[:4]
    count = jnp.sum(picker_ref[...].astype(F32))
    mine = iota(lines.shape, 1) // ACT_DEV == lax.axis_index("seq")
    lines = jnp.where(iota(lines.shape, 0) == 3, jnp.where(mine, count, 0.0), lines)
    stats_ref[...] = jnp.broadcast_to(lines[None], stats_ref.shape)


def local_logits(n_seq, n_vocab, blocks, head, picker):
    shard = head.shape[1]
    rows, lanes = n_seq * ACT_DEV, lanes_of(n_seq)
    return pl.pallas_call(
        functools.partial(logits_kernel, n_seq),
        in_specs=[pl.BlockSpec(memory_space=pltpu.VMEM)] * 6,
        out_shape=[
            jax.ShapeDtypeStruct((rows, shard), F32),
            jax.ShapeDtypeStruct((n_seq * n_vocab, 4, lanes), F32),
        ],
        scratch_shapes=[pltpu.VMEM((lanes, LANES), F32)],
        compiler_params=params(),
        name="local_logits",
    )(*blocks, head, picker)


def merged(stats):
    tops, sums, weights = stats[:, 0], stats[:, 1], stats[:, 2]
    top = jnp.max(tops, axis=0, keepdims=True)
    offset = tops - top
    scale = jnp.exp(offset)
    total = jnp.sum(scale * sums, axis=0, keepdims=True)
    weighted = jnp.sum(scale * (weights + offset * sums), axis=0, keepdims=True)
    return top, total, weighted / total


def entropy_kernel(n_vocab, stats_ref, picker_ref, each_ref, average_ref, column):
    stats = stats_ref[...]
    _, total, centred = merged(stats)
    entropy = jnp.log(total) - centred
    counts = jnp.sum(stats[:, 3], axis=0, keepdims=True) / n_vocab
    valid = (iota(entropy.shape, 1) % ACT_DEV).astype(F32) + 0.5 < counts
    sums = jnp.sum(jnp.where(valid, entropy, 0.0), axis=1, keepdims=True)
    average_ref[...] = sums / jnp.sum(valid.astype(F32), axis=1, keepdims=True)
    column[...] = jnp.broadcast_to(entropy, (LANES, entropy.shape[1])).T
    place = pl.multiple_of(lax.axis_index("seq") * ACT_DEV, ACT_DEV)
    mine = column[pl.ds(place, ACT_DEV), :][:, :1]
    picked = picker_ref[...].astype(F32) > 0.5
    each_ref[...] = jnp.sum(jnp.where(picked, mine, 0.0), axis=0, keepdims=True)


def entropies(n_vocab, stats, picker):
    tokens = picker.shape[1]
    return pl.pallas_call(
        functools.partial(entropy_kernel, n_vocab),
        out_shape=[
            jax.ShapeDtypeStruct((1, tokens), F32),
            jax.ShapeDtypeStruct((1, 1), F32),
        ],
        scratch_shapes=[pltpu.VMEM((stats.shape[2], LANES), F32)],
        compiler_params=params(),
        name="entropies",
    )(stats, picker)


def gradient_kernel(n_seq, n_vocab, stats_ref, logits_ref, head_ref, *refs):
    *out_refs, columns, ordered = refs
    near_refs, far_refs, last_refs = (out_refs[k * PARTS : (k + 1) * PARTS] for k in range(3))
    top, total, centred = merged(stats_ref[...])
    row = iota((8, top.shape[1]), 0)
    lines = jnp.where(row == 0, top, jnp.where(row == 1, 1.0 / total, top + centred))
    columns[...] = jnp.concatenate([lines] * (LANES // 8), axis=0).T
    for q, (core, chip) in enumerate(row_order(n_seq)):
        place = pl.multiple_of(owner_of(n_seq, core, chip) * ACT_DEV, ACT_DEV)
        ordered[q * ACT_DEV : (q + 1) * ACT_DEV] = columns[pl.ds(place, ACT_DEV), :]
    logits = logits_ref[...]
    prob = jnp.exp(logits - ordered[:, 0:1]) * ordered[:, 1:2]
    score = (prob * (ordered[:, 2:3] - logits)).astype(BF16)
    n_chip = n_seq // 2
    last = n_chip - 1
    size = near_refs[0].shape[3]
    for v in range(n_vocab):
        for c in range(PARTS):
            start = (v * PARTS + c) * size
            part = lax.dot_general(
                score,
                head_ref[start : start + size, :],
                (((1,), (1,)), ((), ())),
                preferred_element_type=F32,
            ).astype(BF16)
            blocks = part.reshape(n_seq, ACT_DEV, size)
            near_refs[c][:last, v] = blocks[:last]
            far_refs[c][:, v] = blocks[last : 2 * last]
            near_refs[c][last, v] = blocks[2 * last]
            last_refs[c][v] = blocks[2 * last + 1]


def gradients(n_seq, n_vocab, stats, logits, head):
    rows = logits.shape[0]
    n_chip = n_seq // 2
    block = (n_vocab, ACT_DEV, head.shape[0] // (n_vocab * PARTS))
    outs = [jax.ShapeDtypeStruct((n_chip,) + block, BF16)] * PARTS
    outs += [jax.ShapeDtypeStruct((n_chip - 1,) + block, BF16)] * PARTS
    outs += [jax.ShapeDtypeStruct(block, BF16)] * PARTS
    outs = pl.pallas_call(
        functools.partial(gradient_kernel, n_seq, n_vocab),
        in_specs=[pl.BlockSpec(memory_space=pltpu.VMEM)] * 3,
        out_shape=outs,
        scratch_shapes=[
            pltpu.VMEM((stats.shape[2], LANES), F32),
            pltpu.VMEM((rows, LANES), F32),
        ],
        compiler_params=params(),
        name="gradients",
    )(stats, logits, head)
    return [outs[k * PARTS : (k + 1) * PARTS] for k in range(3)]


def body(n_seq, n_vocab, hidden, head, mask):
    n_chip = n_seq // 2
    last = n_chip - 1
    bits = n_chip.bit_length() - 1

    def swap_core(value):
        return lax.ppermute(value, "seq", [(i, i ^ 1) for i in range(n_seq)])

    def swap_chip(value, step):
        flips = (2 << step, 2 << (bits - 1 - step))
        return lax.ppermute(value, "seq", [(i, i ^ flips[i & 1]) for i in range(n_seq)])

    def send_vocab(value, k):
        return lax.ppermute(value, "vocab", [(i, i ^ k) for i in range(n_vocab)])

    own, picker = select(mask, hidden)

    near = [own]
    for a in range(1, n_chip):
        step = a.bit_length() - 1
        source = near[a ^ (1 << step)]
        if a > 1 and a == 1 << step:
            moved = swap_chip(jnp.concatenate(source, axis=1), step)
            near.append(jnp.split(moved, PARTS, axis=1))
        else:
            near.append([swap_chip(part, step) for part in source])
    early = jnp.concatenate([near[a][c] for c in range(PARTS) for a in range(last)], axis=0)
    early, near[last][0] = lax.optimization_barrier((early, near[last][0]))
    late = jnp.concatenate(near[last], axis=0)
    blocks = [early, swap_core(early), late, swap_core(late)]

    logits, stats = local_logits(n_seq, n_vocab, blocks, head, picker)
    stats = lax.all_to_all(stats, ("seq", "vocab"), 0, 0, tiled=True)
    near, far, far_last = gradients(n_seq, n_vocab, stats, logits, head)
    moved = [swap_core(part) for part in far_last]
    far, _ = lax.optimization_barrier((far, moved))
    far = [swap_core(part) for part in far]
    sums = [[near[c][a].astype(F32) + far[c][a].astype(F32) for c in range(PARTS)] for a in range(last)]
    sums.append([near[c][last].astype(F32) + moved[c].astype(F32) for c in range(PARTS)])
    direct = {
        a: jnp.concatenate([part.astype(BF16) for part in sums[a]], axis=2)
        for a in range(2, n_chip)
        if a & (a - 1) == 0 and a > n_chip // 4
    }
    for a in range(last, 0, -1):
        step = a.bit_length() - 1
        target = sums[a ^ (1 << step)]
        if a in direct:
            moved = jnp.split(swap_chip(direct[a], step), PARTS, axis=2)
        else:
            moved = [swap_chip(part.astype(BF16), step) for part in sums[a]]
        for c in range(PARTS):
            if a == last:
                moved[c], _ = lax.optimization_barrier((moved[c], direct))
            target[c] += moved[c].astype(F32)

    stats, _ = lax.optimization_barrier((stats, sums[0]))
    each, average = entropies(n_vocab, stats, picker)
    column = lax.axis_index("vocab")

    def piece(k):
        parts = [lax.dynamic_index_in_dim(part, column ^ k, 0, keepdims=False) for part in sums[0]]
        return jnp.concatenate(parts, axis=1)

    result = piece(0)
    for k in range(n_vocab - 1, 0, -1):
        result = result + send_vocab(piece(k).astype(BF16), k).astype(F32)
    derivative = lax.dot_general(
        picker, result.astype(BF16), (((0,), (0,)), ((), ())), preferred_element_type=F32
    ).astype(BF16)
    return each.reshape(-1), average.reshape(()), derivative


def solution(mesh):
    n_seq, n_vocab = mesh.shape["seq"], mesh.shape["vocab"]

    def run(hidden, head, mask):
        return body(n_seq, n_vocab, hidden, head, mask)

    return jax.shard_map(
        run,
        mesh=mesh,
        in_specs=(P("seq", None), P(None, ("seq", "vocab")), P("seq")),
        out_specs=(P("seq"), P(), P("seq", "vocab")),
        check_vma=False,
    )
```

```python
import functools

import jax
import jax.numpy as jnp
from jax import lax
from jax.experimental import pallas as pl
from jax.experimental.pallas import tpu as pltpu
from jax.sharding import PartitionSpec as P

ACT_DEV = 16
PARTS = 2
LANES = 128
CHUNKS = 8
FLIGHT = 3
VMEM_BYTES = 24 * 2**20
F32, BF16 = jnp.float32, jnp.bfloat16


def params():
    return pltpu.CompilerParams(vmem_limit_bytes=VMEM_BYTES)


def in_hbm(value):
    return pltpu.with_memory_space_constraint(value, pltpu.HBM)


def iota(shape, axis):
    return lax.broadcasted_iota(jnp.int32, shape, axis)


def turn(bits, index):
    return sum(((index >> b) & 1) << (bits - 1 - b) for b in range(bits))


def row_order(n_seq):
    n_chip = n_seq // 2
    cut = n_chip // 2
    groups = [(core, range(low, low + cut)) for low in (0, cut) for core in (0, 1)]
    return [(core, chip) for core, chips in groups for chip in chips]


def owner_of(n_seq, core, chip):
    me = lax.axis_index("seq")
    bits = (n_seq // 2).bit_length() - 1
    odd = (me & 1) ^ core
    return me ^ (jnp.where(odd == 1, turn(bits, chip), chip) * 2 + core)


def lanes_of(n_seq):
    return -(-n_seq * ACT_DEV // LANES) * LANES


def arrive(copies, i):
    copies[i].wait()
    if i + FLIGHT < len(copies):
        copies[i + FLIGHT].start()


def select_kernel(mask_ref, hidden_ref, *refs):
    *own_refs, picker_ref, mask_here, hidden_here, mask_sem, sems = refs
    chunks, tokens, step = hidden_here.shape
    copies = [
        pltpu.make_async_copy(
            hidden_ref.at[:, pl.ds(i * step, step)], hidden_here.at[i], sems.at[i]
        )
        for i in range(chunks)
    ]
    mask_copy = pltpu.make_async_copy(mask_ref, mask_here, mask_sem)
    mask_copy.start()
    for copy in copies[:FLIGHT]:
        copy.start()
    mask_copy.wait()
    mask = mask_here[...]
    upper = (iota((tokens, tokens), 0) <= iota((tokens, tokens), 1)).astype(BF16)
    ones = jnp.broadcast_to(mask.astype(F32).astype(BF16), (ACT_DEV, tokens))
    slots = jnp.dot(ones, upper, preferred_element_type=F32).astype(jnp.int32) - 1
    picker = (slots == iota((ACT_DEV, tokens), 0)) & (mask == 1)
    picker = picker.astype(F32).astype(BF16)
    picker_ref[...] = picker
    each = chunks // len(own_refs)
    for i in range(chunks):
        arrive(copies, i)
        own = jnp.dot(picker, hidden_here[i], preferred_element_type=F32)
        at = (i % each) * step
        own_refs[i // each][:, at : at + step] = own.astype(BF16)


def select(mask, hidden):
    tokens, width = hidden.shape
    chunks = 4
    own = jax.ShapeDtypeStruct((ACT_DEV, width // PARTS), BF16)
    *own, picker = pl.pallas_call(
        select_kernel,
        in_specs=[pl.BlockSpec(memory_space=pltpu.HBM)] * 2,
        out_shape=[own] * PARTS + [jax.ShapeDtypeStruct((ACT_DEV, tokens), BF16)],
        scratch_shapes=[
            pltpu.VMEM((1, tokens), jnp.int32),
            pltpu.VMEM((chunks, tokens, width // chunks), BF16),
            pltpu.SemaphoreType.DMA,
            pltpu.SemaphoreType.DMA((chunks,)),
        ],
        compiler_params=params(),
        name="select_rows",
    )(in_hbm(mask.reshape(1, tokens)), in_hbm(hidden))
    return own, picker


def logits_kernel(n_seq, *refs):
    *block_refs, head_ref, picker_ref, logits_ref, stats_ref, packed = refs
    step = head_ref.shape[0] // CHUNKS
    each = CHUNKS // PARTS
    logits = None
    for i in range(CHUNKS):
        at = (i % each) * step
        rows = []
        for ref in block_refs:
            size = ref.shape[0] // PARTS
            start = (i // each) * size
            rows.append(ref[start : start + size, at : at + step])
        rows = jnp.concatenate(rows, axis=0)
        head = head_ref[i * step : (i + 1) * step, :]
        part = jnp.dot(rows, head, preferred_element_type=F32)
        logits = part if logits is None else logits + part
    logits_ref[...] = logits
    top = jnp.max(logits, axis=1, keepdims=True)
    away = logits - top
    ex = jnp.exp(away)
    sums = jnp.sum(ex, axis=1, keepdims=True)
    weighted = jnp.sum(ex * away, axis=1, keepdims=True)
    lane = iota((logits.shape[0], LANES), 1)
    pack = jnp.where(lane == 0, top, jnp.where(lane == 1, sums, weighted))
    if packed.shape[0] > n_seq * ACT_DEV:
        packed[...] = jnp.ones(packed.shape, F32)
    for q, (core, chip) in enumerate(row_order(n_seq)):
        place = pl.multiple_of(owner_of(n_seq, core, chip) * ACT_DEV, ACT_DEV)
        packed[pl.ds(place, ACT_DEV), :] = pack[q * ACT_DEV : (q + 1) * ACT_DEV]
    lines = packed[...].T[:4]
    count = jnp.sum(picker_ref[...].astype(F32))
    mine = iota(lines.shape, 1) // ACT_DEV == lax.axis_index("seq")
    lines = jnp.where(iota(lines.shape, 0) == 3, jnp.where(mine, count, 0.0), lines)
    stats_ref[...] = jnp.broadcast_to(lines[None], stats_ref.shape)


def local_logits(n_seq, n_vocab, blocks, head, picker):
    shard = head.shape[1]
    rows, lanes = n_seq * ACT_DEV, lanes_of(n_seq)
    return pl.pallas_call(
        functools.partial(logits_kernel, n_seq),
        in_specs=[pl.BlockSpec(memory_space=pltpu.VMEM)] * 6,
        out_shape=[
            jax.ShapeDtypeStruct((rows, shard), F32),
            jax.ShapeDtypeStruct((n_seq * n_vocab, 4, lanes), F32),
        ],
        scratch_shapes=[pltpu.VMEM((lanes, LANES), F32)],
        compiler_params=params(),
        name="local_logits",
    )(*blocks, head, picker)


def merged(stats):
    tops, sums, weights = stats[:, 0], stats[:, 1], stats[:, 2]
    top = jnp.max(tops, axis=0, keepdims=True)
    offset = tops - top
    scale = jnp.exp(offset)
    total = jnp.sum(scale * sums, axis=0, keepdims=True)
    weighted = jnp.sum(scale * (weights + offset * sums), axis=0, keepdims=True)
    return top, total, weighted / total


def entropy_kernel(n_vocab, stats_ref, picker_ref, each_ref, average_ref, column):
    stats = stats_ref[...]
    _, total, centred = merged(stats)
    entropy = jnp.log(total) - centred
    counts = jnp.sum(stats[:, 3], axis=0, keepdims=True) / n_vocab
    valid = (iota(entropy.shape, 1) % ACT_DEV).astype(F32) + 0.5 < counts
    sums = jnp.sum(jnp.where(valid, entropy, 0.0), axis=1, keepdims=True)
    average_ref[...] = sums / jnp.sum(valid.astype(F32), axis=1, keepdims=True)
    column[...] = jnp.broadcast_to(entropy, (LANES, entropy.shape[1])).T
    place = pl.multiple_of(lax.axis_index("seq") * ACT_DEV, ACT_DEV)
    mine = column[pl.ds(place, ACT_DEV), :][:, :1]
    picked = picker_ref[...].astype(F32) > 0.5
    each_ref[...] = jnp.sum(jnp.where(picked, mine, 0.0), axis=0, keepdims=True)


def entropies(n_vocab, stats, picker):
    tokens = picker.shape[1]
    return pl.pallas_call(
        functools.partial(entropy_kernel, n_vocab),
        out_shape=[
            jax.ShapeDtypeStruct((1, tokens), F32),
            jax.ShapeDtypeStruct((1, 1), F32),
        ],
        scratch_shapes=[pltpu.VMEM((stats.shape[2], LANES), F32)],
        compiler_params=params(),
        name="entropies",
    )(stats, picker)


def gradient_kernel(n_seq, n_vocab, stats_ref, logits_ref, head_ref, *refs):
    *out_refs, columns, ordered = refs
    near_refs, far_refs, last_refs = (out_refs[k * PARTS : (k + 1) * PARTS] for k in range(3))
    top, total, centred = merged(stats_ref[...])
    row = iota((8, top.shape[1]), 0)
    lines = jnp.where(row == 0, top, jnp.where(row == 1, 1.0 / total, top + centred))
    columns[...] = jnp.concatenate([lines] * (LANES // 8), axis=0).T
    for q, (core, chip) in enumerate(row_order(n_seq)):
        place = pl.multiple_of(owner_of(n_seq, core, chip) * ACT_DEV, ACT_DEV)
        ordered[q * ACT_DEV : (q + 1) * ACT_DEV] = columns[pl.ds(place, ACT_DEV), :]
    logits = logits_ref[...]
    prob = jnp.exp(logits - ordered[:, 0:1]) * ordered[:, 1:2]
    score = (prob * (ordered[:, 2:3] - logits)).astype(BF16)
    cut = n_seq // 4
    size = near_refs[0].shape[3]
    for v in range(n_vocab):
        for c in range(PARTS):
            start = (v * PARTS + c) * size
            part = lax.dot_general(
                score,
                head_ref[start : start + size, :],
                (((1,), (1,)), ((), ())),
                preferred_element_type=F32,
            ).astype(BF16)
            blocks = part.reshape(n_seq, ACT_DEV, size)
            near_refs[c][:cut, v] = blocks[:cut]
            far_refs[c][:cut, v] = blocks[cut : 2 * cut]
            near_refs[c][cut:, v] = blocks[2 * cut : 3 * cut]
            far_refs[c][cut:, v] = blocks[3 * cut : 4 * cut - 1]
            last_refs[c][v] = blocks[4 * cut - 1]


def gradients(n_seq, n_vocab, stats, logits, head):
    rows = logits.shape[0]
    n_chip = n_seq // 2
    block = (n_vocab, ACT_DEV, head.shape[0] // (n_vocab * PARTS))
    outs = [jax.ShapeDtypeStruct((n_chip,) + block, BF16)] * PARTS
    outs += [jax.ShapeDtypeStruct((n_chip - 1,) + block, BF16)] * PARTS
    outs += [jax.ShapeDtypeStruct(block, BF16)] * PARTS
    outs = pl.pallas_call(
        functools.partial(gradient_kernel, n_seq, n_vocab),
        in_specs=[pl.BlockSpec(memory_space=pltpu.VMEM)] * 3,
        out_shape=outs,
        scratch_shapes=[
            pltpu.VMEM((stats.shape[2], LANES), F32),
            pltpu.VMEM((rows, LANES), F32),
        ],
        compiler_params=params(),
        name="gradients",
    )(stats, logits, head)
    return [outs[k * PARTS : (k + 1) * PARTS] for k in range(3)]


def body(n_seq, n_vocab, hidden, head, mask):
    n_chip = n_seq // 2
    last = n_chip - 1
    bits = n_chip.bit_length() - 1

    def swap_core(value):
        return lax.ppermute(value, "seq", [(i, i ^ 1) for i in range(n_seq)])

    def swap_chip(value, step):
        flips = (2 << step, 2 << (bits - 1 - step))
        return lax.ppermute(value, "seq", [(i, i ^ flips[i & 1]) for i in range(n_seq)])

    def send_vocab(value, k):
        return lax.ppermute(value, "vocab", [(i, i ^ k) for i in range(n_vocab)])

    own, picker = select(mask, hidden)

    near = [own]
    for a in range(1, n_chip):
        step = a.bit_length() - 1
        source = near[a ^ (1 << step)]
        if a > 1 and a == 1 << step:
            whole = lax.optimization_barrier(jnp.concatenate(source, axis=1))
            source = jnp.split(whole, PARTS, axis=1)
        near.append([swap_chip(part, step) for part in source])

    def gather_rows(chips):
        return jnp.concatenate([near[a][c] for c in range(PARTS) for a in chips], axis=0)

    cut = n_chip // 2
    early, late = gather_rows(range(cut)), gather_rows(range(cut, n_chip))
    blocks = [early, swap_core(early), late, swap_core(late)]

    logits, stats = local_logits(n_seq, n_vocab, blocks, head, picker)
    stats = lax.all_to_all(stats, ("seq", "vocab"), 0, 0, tiled=True)
    near, far, far_last = gradients(n_seq, n_vocab, stats, logits, head)
    moved = [swap_core(part) for part in far_last]
    far, _ = lax.optimization_barrier((far, moved))
    far = [swap_core(part) for part in far]
    sums = [[near[c][a].astype(F32) + far[c][a].astype(F32) for c in range(PARTS)] for a in range(last)]
    sums.append([near[c][last].astype(F32) + moved[c].astype(F32) for c in range(PARTS)])
    direct = {
        a: jnp.concatenate([part.astype(BF16) for part in sums[a]], axis=2)
        for a in range(2, n_chip)
        if a & (a - 1) == 0 and a > n_chip // 4
    }
    for a in range(last, 0, -1):
        step = a.bit_length() - 1
        target = sums[a ^ (1 << step)]
        if a in direct:
            moved = jnp.split(swap_chip(direct[a], step), PARTS, axis=2)
        else:
            moved = [swap_chip(part.astype(BF16), step) for part in sums[a]]
        for c in range(PARTS):
            if a == last:
                moved[c], _ = lax.optimization_barrier((moved[c], direct))
            target[c] += moved[c].astype(F32)

    stats, _ = lax.optimization_barrier((stats, sums[0]))
    each, average = entropies(n_vocab, stats, picker)
    column = lax.axis_index("vocab")

    def piece(k):
        parts = [lax.dynamic_index_in_dim(part, column ^ k, 0, keepdims=False) for part in sums[0]]
        return jnp.concatenate(parts, axis=1)

    result = piece(0)
    for k in range(n_vocab - 1, 0, -1):
        result = result + send_vocab(piece(k).astype(BF16), k).astype(F32)
    derivative = lax.dot_general(
        picker, result.astype(BF16), (((0,), (0,)), ((), ())), preferred_element_type=F32
    ).astype(BF16)
    return each.reshape(-1), average.reshape(()), derivative


def solution(mesh):
    n_seq, n_vocab = mesh.shape["seq"], mesh.shape["vocab"]

    def run(hidden, head, mask):
        return body(n_seq, n_vocab, hidden, head, mask)

    return jax.shard_map(
        run,
        mesh=mesh,
        in_specs=(P("seq", None), P(None, ("seq", "vocab")), P("seq")),
        out_specs=(P("seq"), P(), P("seq", "vocab")),
        check_vma=False,
    )
```

```python
import functools

import jax
import jax.numpy as jnp
from jax import lax
from jax.experimental import pallas as pl
from jax.experimental.pallas import tpu as pltpu
from jax.sharding import PartitionSpec as P

ACT_DEV = 16
PARTS = 2
LANES = 128
CHUNKS = 8
FLIGHT = 3
VMEM_BYTES = 24 * 2**20
F32, BF16 = jnp.float32, jnp.bfloat16


def params():
    return pltpu.CompilerParams(vmem_limit_bytes=VMEM_BYTES)


def in_hbm(value):
    return pltpu.with_memory_space_constraint(value, pltpu.HBM)


def iota(shape, axis):
    return lax.broadcasted_iota(jnp.int32, shape, axis)


def turn(bits, index):
    return sum(((index >> b) & 1) << (bits - 1 - b) for b in range(bits))


def row_order(n_seq):
    last = n_seq // 2 - 1
    early = [(core, chip) for core in (0, 1) for chip in range(last)]
    return early + [(0, last), (1, last)]


def owner_of(n_seq, core, chip):
    me = lax.axis_index("seq")
    bits = (n_seq // 2).bit_length() - 1
    odd = (me & 1) ^ core
    return me ^ (jnp.where(odd == 1, turn(bits, chip), chip) * 2 + core)


def lanes_of(n_seq):
    return -(-n_seq * ACT_DEV // LANES) * LANES


def arrive(copies, i):
    copies[i].wait()
    if i + FLIGHT < len(copies):
        copies[i + FLIGHT].start()


def select_kernel(mask_ref, hidden_ref, *refs):
    *own_refs, picker_ref, mask_here, hidden_here, mask_sem, sems = refs
    chunks, tokens, step = hidden_here.shape
    copies = [
        pltpu.make_async_copy(
            hidden_ref.at[:, pl.ds(i * step, step)], hidden_here.at[i], sems.at[i]
        )
        for i in range(chunks)
    ]
    mask_copy = pltpu.make_async_copy(mask_ref, mask_here, mask_sem)
    mask_copy.start()
    for copy in copies[:FLIGHT]:
        copy.start()
    mask_copy.wait()
    mask = mask_here[...]
    upper = (iota((tokens, tokens), 0) <= iota((tokens, tokens), 1)).astype(BF16)
    ones = jnp.broadcast_to(mask.astype(F32).astype(BF16), (ACT_DEV, tokens))
    slots = jnp.dot(ones, upper, preferred_element_type=F32).astype(jnp.int32) - 1
    picker = (slots == iota((ACT_DEV, tokens), 0)) & (mask == 1)
    picker = picker.astype(F32).astype(BF16)
    picker_ref[...] = picker
    each = chunks // len(own_refs)
    for i in range(chunks):
        arrive(copies, i)
        own = jnp.dot(picker, hidden_here[i], preferred_element_type=F32)
        at = (i % each) * step
        own_refs[i // each][:, at : at + step] = own.astype(BF16)


def select(mask, hidden):
    tokens, width = hidden.shape
    chunks = 4
    own = jax.ShapeDtypeStruct((ACT_DEV, width // PARTS), BF16)
    *own, picker = pl.pallas_call(
        select_kernel,
        in_specs=[pl.BlockSpec(memory_space=pltpu.HBM)] * 2,
        out_shape=[own] * PARTS + [jax.ShapeDtypeStruct((ACT_DEV, tokens), BF16)],
        scratch_shapes=[
            pltpu.VMEM((1, tokens), jnp.int32),
            pltpu.VMEM((chunks, tokens, width // chunks), BF16),
            pltpu.SemaphoreType.DMA,
            pltpu.SemaphoreType.DMA((chunks,)),
        ],
        compiler_params=params(),
        name="select_rows",
    )(in_hbm(mask.reshape(1, tokens)), in_hbm(hidden))
    return own, picker


def logits_kernel(n_seq, *refs):
    *block_refs, head_ref, picker_ref, logits_ref, stats_ref, packed = refs
    step = head_ref.shape[0] // CHUNKS
    each = CHUNKS // PARTS
    logits = None
    for i in range(CHUNKS):
        at = (i % each) * step
        rows = []
        for ref in block_refs:
            size = ref.shape[0] // PARTS
            start = (i // each) * size
            rows.append(ref[start : start + size, at : at + step])
        rows = jnp.concatenate(rows, axis=0)
        head = head_ref[i * step : (i + 1) * step, :]
        part = jnp.dot(rows, head, preferred_element_type=F32)
        logits = part if logits is None else logits + part
    logits_ref[...] = logits
    top = jnp.max(logits, axis=1, keepdims=True)
    away = logits - top
    ex = jnp.exp(away)
    sums = jnp.sum(ex, axis=1, keepdims=True)
    weighted = jnp.sum(ex * away, axis=1, keepdims=True)
    lane = iota((logits.shape[0], LANES), 1)
    pack = jnp.where(lane == 0, top, jnp.where(lane == 1, sums, weighted))
    if packed.shape[0] > n_seq * ACT_DEV:
        packed[...] = jnp.ones(packed.shape, F32)
    for q, (core, chip) in enumerate(row_order(n_seq)):
        place = pl.multiple_of(owner_of(n_seq, core, chip) * ACT_DEV, ACT_DEV)
        packed[pl.ds(place, ACT_DEV), :] = pack[q * ACT_DEV : (q + 1) * ACT_DEV]
    lines = packed[...].T[:4]
    count = jnp.sum(picker_ref[...].astype(F32))
    mine = iota(lines.shape, 1) // ACT_DEV == lax.axis_index("seq")
    lines = jnp.where(iota(lines.shape, 0) == 3, jnp.where(mine, count, 0.0), lines)
    stats_ref[...] = jnp.broadcast_to(lines[None], stats_ref.shape)


def local_logits(n_seq, n_vocab, blocks, head, picker):
    shard = head.shape[1]
    rows, lanes = n_seq * ACT_DEV, lanes_of(n_seq)
    return pl.pallas_call(
        functools.partial(logits_kernel, n_seq),
        in_specs=[pl.BlockSpec(memory_space=pltpu.VMEM)] * 6,
        out_shape=[
            jax.ShapeDtypeStruct((rows, shard), F32),
            jax.ShapeDtypeStruct((n_seq * n_vocab, 4, lanes), F32),
        ],
        scratch_shapes=[pltpu.VMEM((lanes, LANES), F32)],
        compiler_params=params(),
        name="local_logits",
    )(*blocks, head, picker)


def merged(stats):
    tops, sums, weights = stats[:, 0], stats[:, 1], stats[:, 2]
    top = jnp.max(tops, axis=0, keepdims=True)
    offset = tops - top
    scale = jnp.exp(offset)
    total = jnp.sum(scale * sums, axis=0, keepdims=True)
    weighted = jnp.sum(scale * (weights + offset * sums), axis=0, keepdims=True)
    return top, total, weighted / total


def entropy_kernel(n_vocab, stats_ref, picker_ref, each_ref, average_ref, column):
    stats = stats_ref[...]
    _, total, centred = merged(stats)
    entropy = jnp.log(total) - centred
    counts = jnp.sum(stats[:, 3], axis=0, keepdims=True) / n_vocab
    valid = (iota(entropy.shape, 1) % ACT_DEV).astype(F32) + 0.5 < counts
    sums = jnp.sum(jnp.where(valid, entropy, 0.0), axis=1, keepdims=True)
    average_ref[...] = sums / jnp.sum(valid.astype(F32), axis=1, keepdims=True)
    column[...] = jnp.broadcast_to(entropy, (LANES, entropy.shape[1])).T
    place = pl.multiple_of(lax.axis_index("seq") * ACT_DEV, ACT_DEV)
    mine = column[pl.ds(place, ACT_DEV), :][:, :1]
    picked = picker_ref[...].astype(F32) > 0.5
    each_ref[...] = jnp.sum(jnp.where(picked, mine, 0.0), axis=0, keepdims=True)


def entropies(n_vocab, stats, picker):
    tokens = picker.shape[1]
    return pl.pallas_call(
        functools.partial(entropy_kernel, n_vocab),
        out_shape=[
            jax.ShapeDtypeStruct((1, tokens), F32),
            jax.ShapeDtypeStruct((1, 1), F32),
        ],
        scratch_shapes=[pltpu.VMEM((stats.shape[2], LANES), F32)],
        compiler_params=params(),
        name="entropies",
    )(stats, picker)


def gradient_kernel(n_seq, n_vocab, stats_ref, logits_ref, head_ref, *refs):
    *out_refs, columns, ordered = refs
    near_refs, far_refs, last_refs = (out_refs[k * PARTS : (k + 1) * PARTS] for k in range(3))
    top, total, centred = merged(stats_ref[...])
    row = iota((8, top.shape[1]), 0)
    lines = jnp.where(row == 0, top, jnp.where(row == 1, 1.0 / total, top + centred))
    columns[...] = jnp.concatenate([lines] * (LANES // 8), axis=0).T
    for q, (core, chip) in enumerate(row_order(n_seq)):
        place = pl.multiple_of(owner_of(n_seq, core, chip) * ACT_DEV, ACT_DEV)
        ordered[q * ACT_DEV : (q + 1) * ACT_DEV] = columns[pl.ds(place, ACT_DEV), :]
    logits = logits_ref[...]
    prob = jnp.exp(logits - ordered[:, 0:1]) * ordered[:, 1:2]
    score = (prob * (ordered[:, 2:3] - logits)).astype(BF16)
    n_chip = n_seq // 2
    last = n_chip - 1
    size = near_refs[0].shape[3]
    for v in range(n_vocab):
        for c in range(PARTS):
            start = (v * PARTS + c) * size
            part = lax.dot_general(
                score,
                head_ref[start : start + size, :],
                (((1,), (1,)), ((), ())),
                preferred_element_type=F32,
            ).astype(BF16)
            blocks = part.reshape(n_seq, ACT_DEV, size)
            near_refs[c][:last, v] = blocks[:last]
            far_refs[c][:, v] = blocks[last : 2 * last]
            near_refs[c][last, v] = blocks[2 * last]
            last_refs[c][v] = blocks[2 * last + 1]


def gradients(n_seq, n_vocab, stats, logits, head):
    rows = logits.shape[0]
    n_chip = n_seq // 2
    block = (n_vocab, ACT_DEV, head.shape[0] // (n_vocab * PARTS))
    outs = [jax.ShapeDtypeStruct((n_chip,) + block, BF16)] * PARTS
    outs += [jax.ShapeDtypeStruct((n_chip - 1,) + block, BF16)] * PARTS
    outs += [jax.ShapeDtypeStruct(block, BF16)] * PARTS
    outs = pl.pallas_call(
        functools.partial(gradient_kernel, n_seq, n_vocab),
        in_specs=[pl.BlockSpec(memory_space=pltpu.VMEM)] * 3,
        out_shape=outs,
        scratch_shapes=[
            pltpu.VMEM((stats.shape[2], LANES), F32),
            pltpu.VMEM((rows, LANES), F32),
        ],
        compiler_params=params(),
        name="gradients",
    )(stats, logits, head)
    return [outs[k * PARTS : (k + 1) * PARTS] for k in range(3)]


def place_kernel(picker_ref, *refs):
    *part_refs, out_ref, rows, sems = refs
    picker = picker_ref[...]
    chunks, _, step = rows.shape
    copies = []
    for i in range(chunks):
        cut = slice(i * step, (i + 1) * step)
        total = part_refs[0][:, cut]
        for ref in part_refs[1:]:
            total = total + ref[:, cut].astype(F32)
        rows[i] = lax.dot_general(
            picker, total.astype(BF16), (((0,), (0,)), ((), ())), preferred_element_type=F32
        ).astype(BF16)
        copy = pltpu.make_async_copy(rows.at[i], out_ref.at[:, pl.ds(i * step, step)], sems.at[i])
        copy.start()
        copies.append(copy)
    for copy in copies:
        copy.wait()


def place(picker, parts):
    tokens, wide = picker.shape[1], parts[0].shape[1]
    chunks = 4
    return pl.pallas_call(
        place_kernel,
        out_specs=pl.BlockSpec(memory_space=pltpu.HBM),
        out_shape=jax.ShapeDtypeStruct((tokens, wide), BF16),
        scratch_shapes=[
            pltpu.VMEM((chunks, tokens, wide // chunks), BF16),
            pltpu.SemaphoreType.DMA((chunks,)),
        ],
        compiler_params=params(),
        name="place_rows",
    )(picker, *parts)


def body(n_seq, n_vocab, hidden, head, mask):
    n_chip = n_seq // 2
    last = n_chip - 1
    bits = n_chip.bit_length() - 1

    def swap_core(value):
        return lax.ppermute(value, "seq", [(i, i ^ 1) for i in range(n_seq)])

    def swap_chip(value, step):
        flips = (2 << step, 2 << (bits - 1 - step))
        return lax.ppermute(value, "seq", [(i, i ^ flips[i & 1]) for i in range(n_seq)])

    def send_vocab(value, k):
        return lax.ppermute(value, "vocab", [(i, i ^ k) for i in range(n_vocab)])

    own, picker = select(mask, hidden)

    near = [own]
    for a in range(1, n_chip):
        step = a.bit_length() - 1
        source = near[a ^ (1 << step)]
        if a > 1 and a == 1 << step:
            moved = swap_chip(jnp.concatenate(source, axis=1), step)
            near.append(jnp.split(moved, PARTS, axis=1))
        else:
            near.append([swap_chip(part, step) for part in source])
    early = jnp.concatenate([near[a][c] for c in range(PARTS) for a in range(last)], axis=0)
    early, near[last][0] = lax.optimization_barrier((early, near[last][0]))
    late = jnp.concatenate(near[last], axis=0)
    blocks = [early, swap_core(early), late, swap_core(late)]

    logits, stats = local_logits(n_seq, n_vocab, blocks, head, picker)
    stats = lax.all_to_all(stats, ("seq", "vocab"), 0, 0, tiled=True)
    near, far, far_last = gradients(n_seq, n_vocab, stats, logits, head)
    moved = [swap_core(part) for part in far_last]
    far, _ = lax.optimization_barrier((far, moved))
    far = [swap_core(part) for part in far]
    sums = [[near[c][a].astype(F32) + far[c][a].astype(F32) for c in range(PARTS)] for a in range(last)]
    sums.append([near[c][last].astype(F32) + moved[c].astype(F32) for c in range(PARTS)])
    direct = {
        a: jnp.concatenate([part.astype(BF16) for part in sums[a]], axis=2)
        for a in range(2, n_chip)
        if a & (a - 1) == 0 and a > n_chip // 4
    }
    for a in range(last, 0, -1):
        step = a.bit_length() - 1
        target = sums[a ^ (1 << step)]
        if a in direct:
            moved = jnp.split(swap_chip(direct[a], step), PARTS, axis=2)
        else:
            moved = [swap_chip(part.astype(BF16), step) for part in sums[a]]
        for c in range(PARTS):
            if a == last:
                moved[c], _ = lax.optimization_barrier((moved[c], direct))
            target[c] += moved[c].astype(F32)

    stats, _ = lax.optimization_barrier((stats, sums[0]))
    each, average = entropies(n_vocab, stats, picker)
    column = lax.axis_index("vocab")

    def piece(k):
        parts = [lax.dynamic_index_in_dim(part, column ^ k, 0, keepdims=False) for part in sums[0]]
        return jnp.concatenate(parts, axis=1)

    parts = [piece(0)]
    for k in range(n_vocab - 1, 0, -1):
        parts.append(send_vocab(piece(k).astype(BF16), k))
    derivative = place(picker, parts)
    return each.reshape(-1), average.reshape(()), derivative


def solution(mesh):
    n_seq, n_vocab = mesh.shape["seq"], mesh.shape["vocab"]

    def run(hidden, head, mask):
        return body(n_seq, n_vocab, hidden, head, mask)

    return jax.shard_map(
        run,
        mesh=mesh,
        in_specs=(P("seq", None), P(None, ("seq", "vocab")), P("seq")),
        out_specs=(P("seq"), P(), P("seq", "vocab")),
        check_vma=False,
    )
```

```python
import functools

import jax
import jax.numpy as jnp
from jax import lax
from jax.experimental import pallas as pl
from jax.experimental.pallas import tpu as pltpu
from jax.sharding import PartitionSpec as P

ACT_DEV = 16
PARTS = 2
LANES = 128
CHUNKS = 8
FLIGHT = 3
VMEM_BYTES = 24 * 2**20
F32, BF16 = jnp.float32, jnp.bfloat16


def params():
    return pltpu.CompilerParams(vmem_limit_bytes=VMEM_BYTES)


def in_hbm(value):
    return pltpu.with_memory_space_constraint(value, pltpu.HBM)


def iota(shape, axis):
    return lax.broadcasted_iota(jnp.int32, shape, axis)


def turn(bits, index):
    return sum(((index >> b) & 1) << (bits - 1 - b) for b in range(bits))


def row_order(n_seq):
    last = n_seq // 2 - 1
    early = [(core, chip) for core in (0, 1) for chip in range(last)]
    return early + [(0, last), (1, last)]


def owner_of(n_seq, core, chip):
    me = lax.axis_index("seq")
    bits = (n_seq // 2).bit_length() - 1
    odd = (me & 1) ^ core
    return me ^ (jnp.where(odd == 1, turn(bits, chip), chip) * 2 + core)


def lanes_of(n_seq):
    return -(-n_seq * ACT_DEV // LANES) * LANES


def arrive(copies, i):
    copies[i].wait()
    if i + FLIGHT < len(copies):
        copies[i + FLIGHT].start()


def select_kernel(mask_ref, hidden_ref, *refs):
    *own_refs, picker_ref, mask_here, hidden_here, mask_sem, sems = refs
    chunks, tokens, step = hidden_here.shape
    copies = [
        pltpu.make_async_copy(
            hidden_ref.at[:, pl.ds(i * step, step)], hidden_here.at[i], sems.at[i]
        )
        for i in range(chunks)
    ]
    mask_copy = pltpu.make_async_copy(mask_ref, mask_here, mask_sem)
    mask_copy.start()
    for copy in copies[:FLIGHT]:
        copy.start()
    mask_copy.wait()
    mask = mask_here[...]
    upper = (iota((tokens, tokens), 0) <= iota((tokens, tokens), 1)).astype(BF16)
    ones = jnp.broadcast_to(mask.astype(F32).astype(BF16), (ACT_DEV, tokens))
    slots = jnp.dot(ones, upper, preferred_element_type=F32).astype(jnp.int32) - 1
    picker = (slots == iota((ACT_DEV, tokens), 0)) & (mask == 1)
    picker = picker.astype(F32).astype(BF16)
    picker_ref[...] = picker
    each = chunks // len(own_refs)
    for i in range(chunks):
        arrive(copies, i)
        own = jnp.dot(picker, hidden_here[i], preferred_element_type=F32)
        at = (i % each) * step
        own_refs[i // each][:, at : at + step] = own.astype(BF16)


def select(mask, hidden):
    tokens, width = hidden.shape
    chunks = 4
    own = jax.ShapeDtypeStruct((ACT_DEV, width // PARTS), BF16)
    *own, picker = pl.pallas_call(
        select_kernel,
        in_specs=[pl.BlockSpec(memory_space=pltpu.HBM)] * 2,
        out_shape=[own] * PARTS + [jax.ShapeDtypeStruct((ACT_DEV, tokens), BF16)],
        scratch_shapes=[
            pltpu.VMEM((1, tokens), jnp.int32),
            pltpu.VMEM((chunks, tokens, width // chunks), BF16),
            pltpu.SemaphoreType.DMA,
            pltpu.SemaphoreType.DMA((chunks,)),
        ],
        compiler_params=params(),
        name="select_rows",
    )(in_hbm(mask.reshape(1, tokens)), in_hbm(hidden))
    return own, picker


def join_kernel(*refs):
    *part_refs, out_ref, sems = refs
    size = part_refs[0].shape[1]
    copies = [
        pltpu.make_async_copy(ref, out_ref.at[:, pl.ds(c * size, size)], sems.at[c])
        for c, ref in enumerate(part_refs)
    ]
    for copy in copies:
        copy.start()
    for copy in copies:
        copy.wait()


def join(parts):
    rows, size = parts[0].shape
    vmem = pl.BlockSpec(memory_space=pltpu.VMEM)
    return pl.pallas_call(
        join_kernel,
        in_specs=[vmem] * len(parts),
        out_specs=vmem,
        out_shape=jax.ShapeDtypeStruct((rows, size * len(parts)), parts[0].dtype),
        scratch_shapes=[pltpu.SemaphoreType.DMA((len(parts),))],
        compiler_params=params(),
        name="join_parts",
    )(*parts)


def logits_kernel(n_seq, *refs):
    *block_refs, head_ref, picker_ref, logits_ref, stats_ref, packed = refs
    step = head_ref.shape[0] // CHUNKS
    each = CHUNKS // PARTS
    logits = None
    for i in range(CHUNKS):
        at = (i % each) * step
        rows = []
        for ref in block_refs:
            size = ref.shape[0] // PARTS
            start = (i // each) * size
            rows.append(ref[start : start + size, at : at + step])
        rows = jnp.concatenate(rows, axis=0)
        head = head_ref[i * step : (i + 1) * step, :]
        part = jnp.dot(rows, head, preferred_element_type=F32)
        logits = part if logits is None else logits + part
    logits_ref[...] = logits
    top = jnp.max(logits, axis=1, keepdims=True)
    away = logits - top
    ex = jnp.exp(away)
    sums = jnp.sum(ex, axis=1, keepdims=True)
    weighted = jnp.sum(ex * away, axis=1, keepdims=True)
    lane = iota((logits.shape[0], LANES), 1)
    pack = jnp.where(lane == 0, top, jnp.where(lane == 1, sums, weighted))
    if packed.shape[0] > n_seq * ACT_DEV:
        packed[...] = jnp.ones(packed.shape, F32)
    for q, (core, chip) in enumerate(row_order(n_seq)):
        place = pl.multiple_of(owner_of(n_seq, core, chip) * ACT_DEV, ACT_DEV)
        packed[pl.ds(place, ACT_DEV), :] = pack[q * ACT_DEV : (q + 1) * ACT_DEV]
    lines = packed[...].T[:4]
    count = jnp.sum(picker_ref[...].astype(F32))
    mine = iota(lines.shape, 1) // ACT_DEV == lax.axis_index("seq")
    lines = jnp.where(iota(lines.shape, 0) == 3, jnp.where(mine, count, 0.0), lines)
    stats_ref[...] = jnp.broadcast_to(lines[None], stats_ref.shape)


def local_logits(n_seq, n_vocab, blocks, head, picker):
    shard = head.shape[1]
    rows, lanes = n_seq * ACT_DEV, lanes_of(n_seq)
    return pl.pallas_call(
        functools.partial(logits_kernel, n_seq),
        in_specs=[pl.BlockSpec(memory_space=pltpu.VMEM)] * 6,
        out_shape=[
            jax.ShapeDtypeStruct((rows, shard), F32),
            jax.ShapeDtypeStruct((n_seq * n_vocab, 4, lanes), F32),
        ],
        scratch_shapes=[pltpu.VMEM((lanes, LANES), F32)],
        compiler_params=params(),
        name="local_logits",
    )(*blocks, head, picker)


def merged(stats):
    tops, sums, weights = stats[:, 0], stats[:, 1], stats[:, 2]
    top = jnp.max(tops, axis=0, keepdims=True)
    offset = tops - top
    scale = jnp.exp(offset)
    total = jnp.sum(scale * sums, axis=0, keepdims=True)
    weighted = jnp.sum(scale * (weights + offset * sums), axis=0, keepdims=True)
    return top, total, weighted / total


def entropy_kernel(n_vocab, stats_ref, picker_ref, each_ref, average_ref, column):
    stats = stats_ref[...]
    _, total, centred = merged(stats)
    entropy = jnp.log(total) - centred
    counts = jnp.sum(stats[:, 3], axis=0, keepdims=True) / n_vocab
    valid = (iota(entropy.shape, 1) % ACT_DEV).astype(F32) + 0.5 < counts
    sums = jnp.sum(jnp.where(valid, entropy, 0.0), axis=1, keepdims=True)
    average_ref[...] = sums / jnp.sum(valid.astype(F32), axis=1, keepdims=True)
    column[...] = jnp.broadcast_to(entropy, (LANES, entropy.shape[1])).T
    place = pl.multiple_of(lax.axis_index("seq") * ACT_DEV, ACT_DEV)
    mine = column[pl.ds(place, ACT_DEV), :][:, :1]
    picked = picker_ref[...].astype(F32) > 0.5
    each_ref[...] = jnp.sum(jnp.where(picked, mine, 0.0), axis=0, keepdims=True)


def entropies(n_vocab, stats, picker):
    tokens = picker.shape[1]
    return pl.pallas_call(
        functools.partial(entropy_kernel, n_vocab),
        out_shape=[
            jax.ShapeDtypeStruct((1, tokens), F32),
            jax.ShapeDtypeStruct((1, 1), F32),
        ],
        scratch_shapes=[pltpu.VMEM((stats.shape[2], LANES), F32)],
        compiler_params=params(),
        name="entropies",
    )(stats, picker)


def gradient_kernel(n_seq, n_vocab, stats_ref, logits_ref, head_ref, *refs):
    *out_refs, columns, ordered = refs
    near_refs, far_refs, last_refs = (out_refs[k * PARTS : (k + 1) * PARTS] for k in range(3))
    top, total, centred = merged(stats_ref[...])
    row = iota((8, top.shape[1]), 0)
    lines = jnp.where(row == 0, top, jnp.where(row == 1, 1.0 / total, top + centred))
    columns[...] = jnp.concatenate([lines] * (LANES // 8), axis=0).T
    for q, (core, chip) in enumerate(row_order(n_seq)):
        place = pl.multiple_of(owner_of(n_seq, core, chip) * ACT_DEV, ACT_DEV)
        ordered[q * ACT_DEV : (q + 1) * ACT_DEV] = columns[pl.ds(place, ACT_DEV), :]
    logits = logits_ref[...]
    prob = jnp.exp(logits - ordered[:, 0:1]) * ordered[:, 1:2]
    score = (prob * (ordered[:, 2:3] - logits)).astype(BF16)
    n_chip = n_seq // 2
    last = n_chip - 1
    size = near_refs[0].shape[3]
    for v in range(n_vocab):
        for c in range(PARTS):
            start = (v * PARTS + c) * size
            part = lax.dot_general(
                score,
                head_ref[start : start + size, :],
                (((1,), (1,)), ((), ())),
                preferred_element_type=F32,
            ).astype(BF16)
            blocks = part.reshape(n_seq, ACT_DEV, size)
            near_refs[c][:last, v] = blocks[:last]
            far_refs[c][:, v] = blocks[last : 2 * last]
            near_refs[c][last, v] = blocks[2 * last]
            last_refs[c][v] = blocks[2 * last + 1]


def gradients(n_seq, n_vocab, stats, logits, head):
    rows = logits.shape[0]
    n_chip = n_seq // 2
    block = (n_vocab, ACT_DEV, head.shape[0] // (n_vocab * PARTS))
    outs = [jax.ShapeDtypeStruct((n_chip,) + block, BF16)] * PARTS
    outs += [jax.ShapeDtypeStruct((n_chip - 1,) + block, BF16)] * PARTS
    outs += [jax.ShapeDtypeStruct(block, BF16)] * PARTS
    outs = pl.pallas_call(
        functools.partial(gradient_kernel, n_seq, n_vocab),
        in_specs=[pl.BlockSpec(memory_space=pltpu.VMEM)] * 3,
        out_shape=outs,
        scratch_shapes=[
            pltpu.VMEM((stats.shape[2], LANES), F32),
            pltpu.VMEM((rows, LANES), F32),
        ],
        compiler_params=params(),
        name="gradients",
    )(stats, logits, head)
    return [outs[k * PARTS : (k + 1) * PARTS] for k in range(3)]


def body(n_seq, n_vocab, hidden, head, mask):
    n_chip = n_seq // 2
    last = n_chip - 1
    bits = n_chip.bit_length() - 1

    def swap_core(value):
        return lax.ppermute(value, "seq", [(i, i ^ 1) for i in range(n_seq)])

    def swap_chip(value, step):
        flips = (2 << step, 2 << (bits - 1 - step))
        return lax.ppermute(value, "seq", [(i, i ^ flips[i & 1]) for i in range(n_seq)])

    def send_vocab(value, k):
        return lax.ppermute(value, "vocab", [(i, i ^ k) for i in range(n_vocab)])

    own, picker = select(mask, hidden)

    near = [own]
    for a in range(1, n_chip):
        step = a.bit_length() - 1
        source = near[a ^ (1 << step)]
        if a > 1 and a == 1 << step:
            moved = swap_chip(join(source), step)
            near.append(jnp.split(moved, PARTS, axis=1))
        else:
            near.append([swap_chip(part, step) for part in source])
    early = jnp.concatenate([near[a][c] for c in range(PARTS) for a in range(last)], axis=0)
    early, near[last][0] = lax.optimization_barrier((early, near[last][0]))
    late = jnp.concatenate(near[last], axis=0)
    blocks = [early, swap_core(early), late, swap_core(late)]

    logits, stats = local_logits(n_seq, n_vocab, blocks, head, picker)
    stats = lax.all_to_all(stats, ("seq", "vocab"), 0, 0, tiled=True)
    near, far, far_last = gradients(n_seq, n_vocab, stats, logits, head)
    moved = [swap_core(part) for part in far_last]
    far, _ = lax.optimization_barrier((far, moved))
    far = [swap_core(part) for part in far]
    sums = [[near[c][a].astype(F32) + far[c][a].astype(F32) for c in range(PARTS)] for a in range(last)]
    sums.append([near[c][last].astype(F32) + moved[c].astype(F32) for c in range(PARTS)])
    direct = {
        a: jnp.concatenate([part.astype(BF16) for part in sums[a]], axis=2)
        for a in range(2, n_chip)
        if a & (a - 1) == 0 and a > n_chip // 4
    }
    for a in range(last, 0, -1):
        step = a.bit_length() - 1
        target = sums[a ^ (1 << step)]
        if a in direct:
            moved = jnp.split(swap_chip(direct[a], step), PARTS, axis=2)
        else:
            moved = [swap_chip(part.astype(BF16), step) for part in sums[a]]
        for c in range(PARTS):
            if a == last:
                moved[c], _ = lax.optimization_barrier((moved[c], direct))
            target[c] += moved[c].astype(F32)

    stats, _ = lax.optimization_barrier((stats, sums[0]))
    each, average = entropies(n_vocab, stats, picker)
    column = lax.axis_index("vocab")

    def piece(k):
        parts = [lax.dynamic_index_in_dim(part, column ^ k, 0, keepdims=False) for part in sums[0]]
        return jnp.concatenate(parts, axis=1)

    result = piece(0)
    for k in range(n_vocab - 1, 0, -1):
        result = result + send_vocab(piece(k).astype(BF16), k).astype(F32)
    derivative = lax.dot_general(
        picker, result.astype(BF16), (((0,), (0,)), ((), ())), preferred_element_type=F32
    ).astype(BF16)
    return each.reshape(-1), average.reshape(()), derivative


def solution(mesh):
    n_seq, n_vocab = mesh.shape["seq"], mesh.shape["vocab"]

    def run(hidden, head, mask):
        return body(n_seq, n_vocab, hidden, head, mask)

    return jax.shard_map(
        run,
        mesh=mesh,
        in_specs=(P("seq", None), P(None, ("seq", "vocab")), P("seq")),
        out_specs=(P("seq"), P(), P("seq", "vocab")),
        check_vma=False,
    )
```

```python
import functools

import jax
import jax.numpy as jnp
from jax import lax
from jax.experimental import pallas as pl
from jax.experimental.pallas import tpu as pltpu
from jax.sharding import PartitionSpec as P

ACT_DEV = 16
PARTS = 2
LANES = 128
CHUNKS = 8
FLIGHT = 3
VMEM_BYTES = 24 * 2**20
F32, BF16 = jnp.float32, jnp.bfloat16


def params():
    return pltpu.CompilerParams(vmem_limit_bytes=VMEM_BYTES)


def in_hbm(value):
    return pltpu.with_memory_space_constraint(value, pltpu.HBM)


def iota(shape, axis):
    return lax.broadcasted_iota(jnp.int32, shape, axis)


def turn(bits, index):
    return sum(((index >> b) & 1) << (bits - 1 - b) for b in range(bits))


def row_order(n_seq):
    last = n_seq // 2 - 1
    early = [(core, chip) for core in (0, 1) for chip in range(last)]
    return early + [(0, last), (1, last)]


def owner_of(n_seq, core, chip):
    me = lax.axis_index("seq")
    bits = (n_seq // 2).bit_length() - 1
    odd = (me & 1) ^ core
    return me ^ (jnp.where(odd == 1, turn(bits, chip), chip) * 2 + core)


def lanes_of(n_seq):
    return -(-n_seq * ACT_DEV // LANES) * LANES


def arrive(copies, i):
    copies[i].wait()
    if i + FLIGHT < len(copies):
        copies[i + FLIGHT].start()


def select_kernel(mask_ref, hidden_ref, *refs):
    *own_refs, picker_ref, mask_here, hidden_here, mask_sem, sems = refs
    chunks, tokens, step = hidden_here.shape
    copies = [
        pltpu.make_async_copy(
            hidden_ref.at[:, pl.ds(i * step, step)], hidden_here.at[i], sems.at[i]
        )
        for i in range(chunks)
    ]
    mask_copy = pltpu.make_async_copy(mask_ref, mask_here, mask_sem)
    mask_copy.start()
    for copy in copies[:FLIGHT]:
        copy.start()
    mask_copy.wait()
    mask = mask_here[...]
    upper = (iota((tokens, tokens), 0) <= iota((tokens, tokens), 1)).astype(BF16)
    ones = jnp.broadcast_to(mask.astype(F32).astype(BF16), (ACT_DEV, tokens))
    slots = jnp.dot(ones, upper, preferred_element_type=F32).astype(jnp.int32) - 1
    picker = (slots == iota((ACT_DEV, tokens), 0)) & (mask == 1)
    picker = picker.astype(F32).astype(BF16)
    picker_ref[...] = picker
    each = chunks // len(own_refs)
    for i in range(chunks):
        arrive(copies, i)
        own = jnp.dot(picker, hidden_here[i], preferred_element_type=F32)
        at = (i % each) * step
        own_refs[i // each][:, at : at + step] = own.astype(BF16)


def select(mask, hidden):
    tokens, width = hidden.shape
    chunks = 4
    own = jax.ShapeDtypeStruct((ACT_DEV, width // PARTS), BF16)
    *own, picker = pl.pallas_call(
        select_kernel,
        in_specs=[pl.BlockSpec(memory_space=pltpu.HBM)] * 2,
        out_shape=[own] * PARTS + [jax.ShapeDtypeStruct((ACT_DEV, tokens), BF16)],
        scratch_shapes=[
            pltpu.VMEM((1, tokens), jnp.int32),
            pltpu.VMEM((chunks, tokens, width // chunks), BF16),
            pltpu.SemaphoreType.DMA,
            pltpu.SemaphoreType.DMA((chunks,)),
        ],
        compiler_params=params(),
        name="select_rows",
    )(in_hbm(mask.reshape(1, tokens)), in_hbm(hidden))
    return own, picker


def own_kernel(*refs):
    *part_refs, head_ref, out_ref = refs
    total = None
    size = part_refs[0].shape[1]
    for c, ref in enumerate(part_refs):
        head = head_ref[c * size : (c + 1) * size, :]
        part = jnp.dot(ref[...], head, preferred_element_type=F32)
        total = part if total is None else total + part
    out_ref[...] = total


def own_logits(own, head):
    return pl.pallas_call(
        own_kernel,
        in_specs=[pl.BlockSpec(memory_space=pltpu.VMEM)] * (len(own) + 1),
        out_shape=jax.ShapeDtypeStruct((ACT_DEV, head.shape[1]), F32),
        compiler_params=params(),
        name="own_logits",
    )(*own, head)


def logits_kernel(n_seq, *refs):
    own_ref, *block_refs, head_ref, picker_ref, logits_ref, stats_ref, packed = refs
    step = head_ref.shape[0] // CHUNKS
    each = CHUNKS // PARTS
    logits = None
    for i in range(CHUNKS):
        at = (i % each) * step
        rows = []
        for k, ref in enumerate(block_refs):
            size = ref.shape[0] // PARTS
            start = (i // each) * size
            first = start + ACT_DEV if k == 0 else start
            rows.append(ref[first : start + size, at : at + step])
        rows = jnp.concatenate(rows, axis=0)
        head = head_ref[i * step : (i + 1) * step, :]
        part = jnp.dot(rows, head, preferred_element_type=F32)
        logits = part if logits is None else logits + part
    logits = jnp.concatenate([own_ref[...], logits], axis=0)
    logits_ref[...] = logits
    top = jnp.max(logits, axis=1, keepdims=True)
    away = logits - top
    ex = jnp.exp(away)
    sums = jnp.sum(ex, axis=1, keepdims=True)
    weighted = jnp.sum(ex * away, axis=1, keepdims=True)
    lane = iota((logits.shape[0], LANES), 1)
    pack = jnp.where(lane == 0, top, jnp.where(lane == 1, sums, weighted))
    if packed.shape[0] > n_seq * ACT_DEV:
        packed[...] = jnp.ones(packed.shape, F32)
    for q, (core, chip) in enumerate(row_order(n_seq)):
        place = pl.multiple_of(owner_of(n_seq, core, chip) * ACT_DEV, ACT_DEV)
        packed[pl.ds(place, ACT_DEV), :] = pack[q * ACT_DEV : (q + 1) * ACT_DEV]
    lines = packed[...].T[:4]
    count = jnp.sum(picker_ref[...].astype(F32))
    mine = iota(lines.shape, 1) // ACT_DEV == lax.axis_index("seq")
    lines = jnp.where(iota(lines.shape, 0) == 3, jnp.where(mine, count, 0.0), lines)
    stats_ref[...] = jnp.broadcast_to(lines[None], stats_ref.shape)


def local_logits(n_seq, n_vocab, mine, blocks, head, picker):
    shard = head.shape[1]
    rows, lanes = n_seq * ACT_DEV, lanes_of(n_seq)
    return pl.pallas_call(
        functools.partial(logits_kernel, n_seq),
        in_specs=[pl.BlockSpec(memory_space=pltpu.VMEM)] * 7,
        out_shape=[
            jax.ShapeDtypeStruct((rows, shard), F32),
            jax.ShapeDtypeStruct((n_seq * n_vocab, 4, lanes), F32),
        ],
        scratch_shapes=[pltpu.VMEM((lanes, LANES), F32)],
        compiler_params=params(),
        name="local_logits",
    )(mine, *blocks, head, picker)


def merged(stats):
    tops, sums, weights = stats[:, 0], stats[:, 1], stats[:, 2]
    top = jnp.max(tops, axis=0, keepdims=True)
    offset = tops - top
    scale = jnp.exp(offset)
    total = jnp.sum(scale * sums, axis=0, keepdims=True)
    weighted = jnp.sum(scale * (weights + offset * sums), axis=0, keepdims=True)
    return top, total, weighted / total


def entropy_kernel(n_vocab, stats_ref, picker_ref, each_ref, average_ref, column):
    stats = stats_ref[...]
    _, total, centred = merged(stats)
    entropy = jnp.log(total) - centred
    counts = jnp.sum(stats[:, 3], axis=0, keepdims=True) / n_vocab
    valid = (iota(entropy.shape, 1) % ACT_DEV).astype(F32) + 0.5 < counts
    sums = jnp.sum(jnp.where(valid, entropy, 0.0), axis=1, keepdims=True)
    average_ref[...] = sums / jnp.sum(valid.astype(F32), axis=1, keepdims=True)
    column[...] = jnp.broadcast_to(entropy, (LANES, entropy.shape[1])).T
    place = pl.multiple_of(lax.axis_index("seq") * ACT_DEV, ACT_DEV)
    mine = column[pl.ds(place, ACT_DEV), :][:, :1]
    picked = picker_ref[...].astype(F32) > 0.5
    each_ref[...] = jnp.sum(jnp.where(picked, mine, 0.0), axis=0, keepdims=True)


def entropies(n_vocab, stats, picker):
    tokens = picker.shape[1]
    return pl.pallas_call(
        functools.partial(entropy_kernel, n_vocab),
        out_shape=[
            jax.ShapeDtypeStruct((1, tokens), F32),
            jax.ShapeDtypeStruct((1, 1), F32),
        ],
        scratch_shapes=[pltpu.VMEM((stats.shape[2], LANES), F32)],
        compiler_params=params(),
        name="entropies",
    )(stats, picker)


def gradient_kernel(n_seq, n_vocab, stats_ref, logits_ref, head_ref, *refs):
    *out_refs, columns, ordered = refs
    near_refs, far_refs, last_refs = (out_refs[k * PARTS : (k + 1) * PARTS] for k in range(3))
    top, total, centred = merged(stats_ref[...])
    row = iota((8, top.shape[1]), 0)
    lines = jnp.where(row == 0, top, jnp.where(row == 1, 1.0 / total, top + centred))
    columns[...] = jnp.concatenate([lines] * (LANES // 8), axis=0).T
    for q, (core, chip) in enumerate(row_order(n_seq)):
        place = pl.multiple_of(owner_of(n_seq, core, chip) * ACT_DEV, ACT_DEV)
        ordered[q * ACT_DEV : (q + 1) * ACT_DEV] = columns[pl.ds(place, ACT_DEV), :]
    logits = logits_ref[...]
    prob = jnp.exp(logits - ordered[:, 0:1]) * ordered[:, 1:2]
    score = (prob * (ordered[:, 2:3] - logits)).astype(BF16)
    n_chip = n_seq // 2
    last = n_chip - 1
    size = near_refs[0].shape[3]
    for v in range(n_vocab):
        for c in range(PARTS):
            start = (v * PARTS + c) * size
            part = lax.dot_general(
                score,
                head_ref[start : start + size, :],
                (((1,), (1,)), ((), ())),
                preferred_element_type=F32,
            ).astype(BF16)
            blocks = part.reshape(n_seq, ACT_DEV, size)
            near_refs[c][:last, v] = blocks[:last]
            far_refs[c][:, v] = blocks[last : 2 * last]
            near_refs[c][last, v] = blocks[2 * last]
            last_refs[c][v] = blocks[2 * last + 1]


def gradients(n_seq, n_vocab, stats, logits, head):
    rows = logits.shape[0]
    n_chip = n_seq // 2
    block = (n_vocab, ACT_DEV, head.shape[0] // (n_vocab * PARTS))
    outs = [jax.ShapeDtypeStruct((n_chip,) + block, BF16)] * PARTS
    outs += [jax.ShapeDtypeStruct((n_chip - 1,) + block, BF16)] * PARTS
    outs += [jax.ShapeDtypeStruct(block, BF16)] * PARTS
    outs = pl.pallas_call(
        functools.partial(gradient_kernel, n_seq, n_vocab),
        in_specs=[pl.BlockSpec(memory_space=pltpu.VMEM)] * 3,
        out_shape=outs,
        scratch_shapes=[
            pltpu.VMEM((stats.shape[2], LANES), F32),
            pltpu.VMEM((rows, LANES), F32),
        ],
        compiler_params=params(),
        name="gradients",
    )(stats, logits, head)
    return [outs[k * PARTS : (k + 1) * PARTS] for k in range(3)]


def body(n_seq, n_vocab, hidden, head, mask):
    n_chip = n_seq // 2
    last = n_chip - 1
    bits = n_chip.bit_length() - 1

    def swap_core(value):
        return lax.ppermute(value, "seq", [(i, i ^ 1) for i in range(n_seq)])

    def swap_chip(value, step):
        flips = (2 << step, 2 << (bits - 1 - step))
        return lax.ppermute(value, "seq", [(i, i ^ flips[i & 1]) for i in range(n_seq)])

    def send_vocab(value, k):
        return lax.ppermute(value, "vocab", [(i, i ^ k) for i in range(n_vocab)])

    own, picker = select(mask, hidden)

    near = [own]
    mine = own_logits(own, head)
    for a in range(1, n_chip):
        step = a.bit_length() - 1
        source = near[a ^ (1 << step)]
        if a > 1 and a == 1 << step:
            source, mine = lax.optimization_barrier((jnp.concatenate(source, axis=1), mine))
            moved = swap_chip(source, step)
            near.append(jnp.split(moved, PARTS, axis=1))
        else:
            near.append([swap_chip(part, step) for part in source])
    early = jnp.concatenate([near[a][c] for c in range(PARTS) for a in range(last)], axis=0)
    early, near[last][0] = lax.optimization_barrier((early, near[last][0]))
    late = jnp.concatenate(near[last], axis=0)
    blocks = [early, swap_core(early), late, swap_core(late)]

    logits, stats = local_logits(n_seq, n_vocab, mine, blocks, head, picker)
    stats = lax.all_to_all(stats, ("seq", "vocab"), 0, 0, tiled=True)
    near, far, far_last = gradients(n_seq, n_vocab, stats, logits, head)
    moved = [swap_core(part) for part in far_last]
    far, _ = lax.optimization_barrier((far, moved))
    far = [swap_core(part) for part in far]
    sums = [[near[c][a].astype(F32) + far[c][a].astype(F32) for c in range(PARTS)] for a in range(last)]
    sums.append([near[c][last].astype(F32) + moved[c].astype(F32) for c in range(PARTS)])
    direct = {
        a: jnp.concatenate([part.astype(BF16) for part in sums[a]], axis=2)
        for a in range(2, n_chip)
        if a & (a - 1) == 0 and a > n_chip // 4
    }
    for a in range(last, 0, -1):
        step = a.bit_length() - 1
        target = sums[a ^ (1 << step)]
        if a in direct:
            moved = jnp.split(swap_chip(direct[a], step), PARTS, axis=2)
        else:
            moved = [swap_chip(part.astype(BF16), step) for part in sums[a]]
        for c in range(PARTS):
            if a == last:
                moved[c], _ = lax.optimization_barrier((moved[c], direct))
            target[c] += moved[c].astype(F32)

    stats, _ = lax.optimization_barrier((stats, sums[0]))
    each, average = entropies(n_vocab, stats, picker)
    column = lax.axis_index("vocab")

    def piece(k):
        parts = [lax.dynamic_index_in_dim(part, column ^ k, 0, keepdims=False) for part in sums[0]]
        return jnp.concatenate(parts, axis=1)

    result = piece(0)
    for k in range(n_vocab - 1, 0, -1):
        result = result + send_vocab(piece(k).astype(BF16), k).astype(F32)
    derivative = lax.dot_general(
        picker, result.astype(BF16), (((0,), (0,)), ((), ())), preferred_element_type=F32
    ).astype(BF16)
    return each.reshape(-1), average.reshape(()), derivative


def solution(mesh):
    n_seq, n_vocab = mesh.shape["seq"], mesh.shape["vocab"]

    def run(hidden, head, mask):
        return body(n_seq, n_vocab, hidden, head, mask)

    return jax.shard_map(
        run,
        mesh=mesh,
        in_specs=(P("seq", None), P(None, ("seq", "vocab")), P("seq")),
        out_specs=(P("seq"), P(), P("seq", "vocab")),
        check_vma=False,
    )
```

```python
import functools

import jax
import jax.numpy as jnp
from jax import lax
from jax.experimental import pallas as pl
from jax.experimental.pallas import tpu as pltpu
from jax.sharding import PartitionSpec as P

ACT_DEV = 16
PARTS = 2
LANES = 128
CHUNKS = 8
OWN_CHUNKS = 2
FLIGHT = 3
VMEM_BYTES = 24 * 2**20
F32, BF16 = jnp.float32, jnp.bfloat16


def params():
    return pltpu.CompilerParams(vmem_limit_bytes=VMEM_BYTES)


def in_hbm(value):
    return pltpu.with_memory_space_constraint(value, pltpu.HBM)


def iota(shape, axis):
    return lax.broadcasted_iota(jnp.int32, shape, axis)


def turn(bits, index):
    return sum(((index >> b) & 1) << (bits - 1 - b) for b in range(bits))


def row_order(n_seq):
    last = n_seq // 2 - 1
    early = [(core, chip) for core in (0, 1) for chip in range(last)]
    return early + [(0, last), (1, last)]


def owner_of(n_seq, core, chip):
    me = lax.axis_index("seq")
    bits = (n_seq // 2).bit_length() - 1
    odd = (me & 1) ^ core
    return me ^ (jnp.where(odd == 1, turn(bits, chip), chip) * 2 + core)


def lanes_of(n_seq):
    return -(-n_seq * ACT_DEV // LANES) * LANES


def arrive(copies, i):
    copies[i].wait()
    if i + FLIGHT < len(copies):
        copies[i + FLIGHT].start()


def select_kernel(mask_ref, hidden_ref, *refs):
    *own_refs, picker_ref, mask_here, hidden_here, mask_sem, sems = refs
    chunks, tokens, step = hidden_here.shape
    copies = [
        pltpu.make_async_copy(
            hidden_ref.at[:, pl.ds(i * step, step)], hidden_here.at[i], sems.at[i]
        )
        for i in range(chunks)
    ]
    mask_copy = pltpu.make_async_copy(mask_ref, mask_here, mask_sem)
    mask_copy.start()
    for copy in copies[:FLIGHT]:
        copy.start()
    mask_copy.wait()
    mask = mask_here[...]
    upper = (iota((tokens, tokens), 0) <= iota((tokens, tokens), 1)).astype(BF16)
    ones = jnp.broadcast_to(mask.astype(F32).astype(BF16), (ACT_DEV, tokens))
    slots = jnp.dot(ones, upper, preferred_element_type=F32).astype(jnp.int32) - 1
    picker = (slots == iota((ACT_DEV, tokens), 0)) & (mask == 1)
    picker = picker.astype(F32).astype(BF16)
    picker_ref[...] = picker
    each = chunks // len(own_refs)
    for i in range(chunks):
        arrive(copies, i)
        own = jnp.dot(picker, hidden_here[i], preferred_element_type=F32)
        at = (i % each) * step
        own_refs[i // each][:, at : at + step] = own.astype(BF16)


def select(mask, hidden):
    tokens, width = hidden.shape
    chunks = 4
    own = jax.ShapeDtypeStruct((ACT_DEV, width // PARTS), BF16)
    *own, picker = pl.pallas_call(
        select_kernel,
        in_specs=[pl.BlockSpec(memory_space=pltpu.HBM)] * 2,
        out_shape=[own] * PARTS + [jax.ShapeDtypeStruct((ACT_DEV, tokens), BF16)],
        scratch_shapes=[
            pltpu.VMEM((1, tokens), jnp.int32),
            pltpu.VMEM((chunks, tokens, width // chunks), BF16),
            pltpu.SemaphoreType.DMA,
            pltpu.SemaphoreType.DMA((chunks,)),
        ],
        compiler_params=params(),
        name="select_rows",
    )(in_hbm(mask.reshape(1, tokens)), in_hbm(hidden))
    return own, picker


def own_kernel(own_ref, head_ref, out_ref, head_here, sems):
    chunks, step, _ = head_here.shape
    copies = [
        pltpu.make_async_copy(head_ref.at[pl.ds(i * step, step), :], head_here.at[i], sems.at[i])
        for i in range(chunks)
    ]
    for copy in copies:
        copy.start()
    total = None
    for i in range(chunks):
        copies[i].wait()
        rows = own_ref[:, i * step : (i + 1) * step]
        part = jnp.dot(rows, head_here[i], preferred_element_type=F32)
        total = part if total is None else total + part
    out_ref[...] = total


def own_logits(own, head):
    width, shard = head.shape
    return pl.pallas_call(
        own_kernel,
        in_specs=[pl.BlockSpec(memory_space=pltpu.VMEM), pl.BlockSpec(memory_space=pltpu.HBM)],
        out_shape=jax.ShapeDtypeStruct((ACT_DEV, shard), F32),
        scratch_shapes=[
            pltpu.VMEM((OWN_CHUNKS, width // CHUNKS, shard), BF16),
            pltpu.SemaphoreType.DMA((OWN_CHUNKS,)),
        ],
        compiler_params=params(),
        name="own_logits",
    )(own[0], in_hbm(head))


def logits_kernel(n_seq, *refs):
    own_ref, *block_refs, head_ref, picker_ref, logits_ref, stats_ref, packed = refs
    step = head_ref.shape[0] // CHUNKS
    each = CHUNKS // PARTS
    logits = None
    for i in range(CHUNKS):
        at = (i % each) * step
        rows = []
        for k, ref in enumerate(block_refs):
            size = ref.shape[0] // PARTS
            start = (i // each) * size
            first = start + ACT_DEV if k == 0 and i < OWN_CHUNKS else start
            rows.append(ref[first : start + size, at : at + step])
        rows = jnp.concatenate(rows, axis=0)
        head = head_ref[i * step : (i + 1) * step, :]
        part = jnp.dot(rows, head, preferred_element_type=F32)
        if i < OWN_CHUNKS:
            mine = own_ref[...] if i == 0 else jnp.zeros(own_ref.shape, F32)
            part = jnp.concatenate([mine, part], axis=0)
        logits = part if logits is None else logits + part
    logits_ref[...] = logits
    top = jnp.max(logits, axis=1, keepdims=True)
    away = logits - top
    ex = jnp.exp(away)
    sums = jnp.sum(ex, axis=1, keepdims=True)
    weighted = jnp.sum(ex * away, axis=1, keepdims=True)
    lane = iota((logits.shape[0], LANES), 1)
    pack = jnp.where(lane == 0, top, jnp.where(lane == 1, sums, weighted))
    if packed.shape[0] > n_seq * ACT_DEV:
        packed[...] = jnp.ones(packed.shape, F32)
    for q, (core, chip) in enumerate(row_order(n_seq)):
        place = pl.multiple_of(owner_of(n_seq, core, chip) * ACT_DEV, ACT_DEV)
        packed[pl.ds(place, ACT_DEV), :] = pack[q * ACT_DEV : (q + 1) * ACT_DEV]
    lines = packed[...].T[:4]
    count = jnp.sum(picker_ref[...].astype(F32))
    mine = iota(lines.shape, 1) // ACT_DEV == lax.axis_index("seq")
    lines = jnp.where(iota(lines.shape, 0) == 3, jnp.where(mine, count, 0.0), lines)
    stats_ref[...] = jnp.broadcast_to(lines[None], stats_ref.shape)


def local_logits(n_seq, n_vocab, mine, blocks, head, picker):
    shard = head.shape[1]
    rows, lanes = n_seq * ACT_DEV, lanes_of(n_seq)
    return pl.pallas_call(
        functools.partial(logits_kernel, n_seq),
        in_specs=[pl.BlockSpec(memory_space=pltpu.VMEM)] * 7,
        out_shape=[
            jax.ShapeDtypeStruct((rows, shard), F32),
            jax.ShapeDtypeStruct((n_seq * n_vocab, 4, lanes), F32),
        ],
        scratch_shapes=[pltpu.VMEM((lanes, LANES), F32)],
        compiler_params=params(),
        name="local_logits",
    )(mine, *blocks, head, picker)


def merged(stats):
    tops, sums, weights = stats[:, 0], stats[:, 1], stats[:, 2]
    top = jnp.max(tops, axis=0, keepdims=True)
    offset = tops - top
    scale = jnp.exp(offset)
    total = jnp.sum(scale * sums, axis=0, keepdims=True)
    weighted = jnp.sum(scale * (weights + offset * sums), axis=0, keepdims=True)
    return top, total, weighted / total


def entropy_kernel(n_vocab, stats_ref, picker_ref, each_ref, average_ref, column):
    stats = stats_ref[...]
    _, total, centred = merged(stats)
    entropy = jnp.log(total) - centred
    counts = jnp.sum(stats[:, 3], axis=0, keepdims=True) / n_vocab
    valid = (iota(entropy.shape, 1) % ACT_DEV).astype(F32) + 0.5 < counts
    sums = jnp.sum(jnp.where(valid, entropy, 0.0), axis=1, keepdims=True)
    average_ref[...] = sums / jnp.sum(valid.astype(F32), axis=1, keepdims=True)
    column[...] = jnp.broadcast_to(entropy, (LANES, entropy.shape[1])).T
    place = pl.multiple_of(lax.axis_index("seq") * ACT_DEV, ACT_DEV)
    mine = column[pl.ds(place, ACT_DEV), :][:, :1]
    picked = picker_ref[...].astype(F32) > 0.5
    each_ref[...] = jnp.sum(jnp.where(picked, mine, 0.0), axis=0, keepdims=True)


def entropies(n_vocab, stats, picker):
    tokens = picker.shape[1]
    return pl.pallas_call(
        functools.partial(entropy_kernel, n_vocab),
        out_shape=[
            jax.ShapeDtypeStruct((1, tokens), F32),
            jax.ShapeDtypeStruct((1, 1), F32),
        ],
        scratch_shapes=[pltpu.VMEM((stats.shape[2], LANES), F32)],
        compiler_params=params(),
        name="entropies",
    )(stats, picker)


def gradient_kernel(n_seq, n_vocab, stats_ref, logits_ref, head_ref, *refs):
    *out_refs, columns, ordered = refs
    near_refs, far_refs, last_refs = (out_refs[k * PARTS : (k + 1) * PARTS] for k in range(3))
    top, total, centred = merged(stats_ref[...])
    row = iota((8, top.shape[1]), 0)
    lines = jnp.where(row == 0, top, jnp.where(row == 1, 1.0 / total, top + centred))
    columns[...] = jnp.concatenate([lines] * (LANES // 8), axis=0).T
    for q, (core, chip) in enumerate(row_order(n_seq)):
        place = pl.multiple_of(owner_of(n_seq, core, chip) * ACT_DEV, ACT_DEV)
        ordered[q * ACT_DEV : (q + 1) * ACT_DEV] = columns[pl.ds(place, ACT_DEV), :]
    logits = logits_ref[...]
    prob = jnp.exp(logits - ordered[:, 0:1]) * ordered[:, 1:2]
    score = (prob * (ordered[:, 2:3] - logits)).astype(BF16)
    n_chip = n_seq // 2
    last = n_chip - 1
    size = near_refs[0].shape[3]
    for v in range(n_vocab):
        for c in range(PARTS):
            start = (v * PARTS + c) * size
            part = lax.dot_general(
                score,
                head_ref[start : start + size, :],
                (((1,), (1,)), ((), ())),
                preferred_element_type=F32,
            ).astype(BF16)
            blocks = part.reshape(n_seq, ACT_DEV, size)
            near_refs[c][:last, v] = blocks[:last]
            far_refs[c][:, v] = blocks[last : 2 * last]
            near_refs[c][last, v] = blocks[2 * last]
            last_refs[c][v] = blocks[2 * last + 1]


def gradients(n_seq, n_vocab, stats, logits, head):
    rows = logits.shape[0]
    n_chip = n_seq // 2
    block = (n_vocab, ACT_DEV, head.shape[0] // (n_vocab * PARTS))
    outs = [jax.ShapeDtypeStruct((n_chip,) + block, BF16)] * PARTS
    outs += [jax.ShapeDtypeStruct((n_chip - 1,) + block, BF16)] * PARTS
    outs += [jax.ShapeDtypeStruct(block, BF16)] * PARTS
    outs = pl.pallas_call(
        functools.partial(gradient_kernel, n_seq, n_vocab),
        in_specs=[pl.BlockSpec(memory_space=pltpu.VMEM)] * 3,
        out_shape=outs,
        scratch_shapes=[
            pltpu.VMEM((stats.shape[2], LANES), F32),
            pltpu.VMEM((rows, LANES), F32),
        ],
        compiler_params=params(),
        name="gradients",
    )(stats, logits, head)
    return [outs[k * PARTS : (k + 1) * PARTS] for k in range(3)]


def body(n_seq, n_vocab, hidden, head, mask):
    n_chip = n_seq // 2
    last = n_chip - 1
    bits = n_chip.bit_length() - 1

    def swap_core(value):
        return lax.ppermute(value, "seq", [(i, i ^ 1) for i in range(n_seq)])

    def swap_chip(value, step):
        flips = (2 << step, 2 << (bits - 1 - step))
        return lax.ppermute(value, "seq", [(i, i ^ flips[i & 1]) for i in range(n_seq)])

    def send_vocab(value, k):
        return lax.ppermute(value, "vocab", [(i, i ^ k) for i in range(n_vocab)])

    own, picker = select(mask, hidden)

    near = [own]
    mine = own_logits(own, head)
    for a in range(1, n_chip):
        step = a.bit_length() - 1
        source = near[a ^ (1 << step)]
        if a > 1 and a == 1 << step:
            source, mine = lax.optimization_barrier((jnp.concatenate(source, axis=1), mine))
            moved = swap_chip(source, step)
            near.append(jnp.split(moved, PARTS, axis=1))
        else:
            near.append([swap_chip(part, step) for part in source])
    early = jnp.concatenate([near[a][c] for c in range(PARTS) for a in range(last)], axis=0)
    early, near[last][0] = lax.optimization_barrier((early, near[last][0]))
    late = jnp.concatenate(near[last], axis=0)
    blocks = [early, swap_core(early), late, swap_core(late)]

    logits, stats = local_logits(n_seq, n_vocab, mine, blocks, head, picker)
    stats = lax.all_to_all(stats, ("seq", "vocab"), 0, 0, tiled=True)
    near, far, far_last = gradients(n_seq, n_vocab, stats, logits, head)
    moved = [swap_core(part) for part in far_last]
    far, _ = lax.optimization_barrier((far, moved))
    far = [swap_core(part) for part in far]
    sums = [[near[c][a].astype(F32) + far[c][a].astype(F32) for c in range(PARTS)] for a in range(last)]
    sums.append([near[c][last].astype(F32) + moved[c].astype(F32) for c in range(PARTS)])
    direct = {
        a: jnp.concatenate([part.astype(BF16) for part in sums[a]], axis=2)
        for a in range(2, n_chip)
        if a & (a - 1) == 0 and a > n_chip // 4
    }
    for a in range(last, 0, -1):
        step = a.bit_length() - 1
        target = sums[a ^ (1 << step)]
        if a in direct:
            moved = jnp.split(swap_chip(direct[a], step), PARTS, axis=2)
        else:
            moved = [swap_chip(part.astype(BF16), step) for part in sums[a]]
        for c in range(PARTS):
            if a == last:
                moved[c], _ = lax.optimization_barrier((moved[c], direct))
            target[c] += moved[c].astype(F32)

    stats, _ = lax.optimization_barrier((stats, sums[0]))
    each, average = entropies(n_vocab, stats, picker)
    column = lax.axis_index("vocab")

    def piece(k):
        parts = [lax.dynamic_index_in_dim(part, column ^ k, 0, keepdims=False) for part in sums[0]]
        return jnp.concatenate(parts, axis=1)

    result = piece(0)
    for k in range(n_vocab - 1, 0, -1):
        result = result + send_vocab(piece(k).astype(BF16), k).astype(F32)
    derivative = lax.dot_general(
        picker, result.astype(BF16), (((0,), (0,)), ((), ())), preferred_element_type=F32
    ).astype(BF16)
    return each.reshape(-1), average.reshape(()), derivative


def solution(mesh):
    n_seq, n_vocab = mesh.shape["seq"], mesh.shape["vocab"]

    def run(hidden, head, mask):
        return body(n_seq, n_vocab, hidden, head, mask)

    return jax.shard_map(
        run,
        mesh=mesh,
        in_specs=(P("seq", None), P(None, ("seq", "vocab")), P("seq")),
        out_specs=(P("seq"), P(), P("seq", "vocab")),
        check_vma=False,
    )
```

```python
import functools

import jax
import jax.numpy as jnp
from jax import lax
from jax.experimental import pallas as pl
from jax.experimental.pallas import tpu as pltpu
from jax.sharding import PartitionSpec as P

ACT_DEV = 16
PARTS = 2
LANES = 128
CHUNKS = 8
OWN_CHUNKS = 1
FLIGHT = 3
VMEM_BYTES = 24 * 2**20
F32, BF16 = jnp.float32, jnp.bfloat16


def params():
    return pltpu.CompilerParams(vmem_limit_bytes=VMEM_BYTES)


def in_hbm(value):
    return pltpu.with_memory_space_constraint(value, pltpu.HBM)


def iota(shape, axis):
    return lax.broadcasted_iota(jnp.int32, shape, axis)


def turn(bits, index):
    return sum(((index >> b) & 1) << (bits - 1 - b) for b in range(bits))


def row_order(n_seq):
    last = n_seq // 2 - 1
    early = [(core, chip) for core in (0, 1) for chip in range(last)]
    return early + [(0, last), (1, last)]


def owner_of(n_seq, core, chip):
    me = lax.axis_index("seq")
    bits = (n_seq // 2).bit_length() - 1
    odd = (me & 1) ^ core
    return me ^ (jnp.where(odd == 1, turn(bits, chip), chip) * 2 + core)


def lanes_of(n_seq):
    return -(-n_seq * ACT_DEV // LANES) * LANES


def arrive(copies, i):
    copies[i].wait()
    if i + FLIGHT < len(copies):
        copies[i + FLIGHT].start()


def select_kernel(mask_ref, hidden_ref, *refs):
    *own_refs, picker_ref, mask_here, hidden_here, mask_sem, sems = refs
    chunks, tokens, step = hidden_here.shape
    copies = [
        pltpu.make_async_copy(
            hidden_ref.at[:, pl.ds(i * step, step)], hidden_here.at[i], sems.at[i]
        )
        for i in range(chunks)
    ]
    mask_copy = pltpu.make_async_copy(mask_ref, mask_here, mask_sem)
    mask_copy.start()
    for copy in copies[:FLIGHT]:
        copy.start()
    mask_copy.wait()
    mask = mask_here[...]
    upper = (iota((tokens, tokens), 0) <= iota((tokens, tokens), 1)).astype(BF16)
    ones = jnp.broadcast_to(mask.astype(F32).astype(BF16), (ACT_DEV, tokens))
    slots = jnp.dot(ones, upper, preferred_element_type=F32).astype(jnp.int32) - 1
    picker = (slots == iota((ACT_DEV, tokens), 0)) & (mask == 1)
    picker = picker.astype(F32).astype(BF16)
    picker_ref[...] = picker
    each = chunks // len(own_refs)
    for i in range(chunks):
        arrive(copies, i)
        own = jnp.dot(picker, hidden_here[i], preferred_element_type=F32)
        at = (i % each) * step
        own_refs[i // each][:, at : at + step] = own.astype(BF16)


def select(mask, hidden):
    tokens, width = hidden.shape
    chunks = 4
    own = jax.ShapeDtypeStruct((ACT_DEV, width // PARTS), BF16)
    *own, picker = pl.pallas_call(
        select_kernel,
        in_specs=[pl.BlockSpec(memory_space=pltpu.HBM)] * 2,
        out_shape=[own] * PARTS + [jax.ShapeDtypeStruct((ACT_DEV, tokens), BF16)],
        scratch_shapes=[
            pltpu.VMEM((1, tokens), jnp.int32),
            pltpu.VMEM((chunks, tokens, width // chunks), BF16),
            pltpu.SemaphoreType.DMA,
            pltpu.SemaphoreType.DMA((chunks,)),
        ],
        compiler_params=params(),
        name="select_rows",
    )(in_hbm(mask.reshape(1, tokens)), in_hbm(hidden))
    return own, picker


def own_kernel(own_ref, head_ref, out_ref, head_here, sems):
    chunks, step, _ = head_here.shape
    copies = [
        pltpu.make_async_copy(head_ref.at[pl.ds(i * step, step), :], head_here.at[i], sems.at[i])
        for i in range(chunks)
    ]
    for copy in copies:
        copy.start()
    total = None
    for i in range(chunks):
        copies[i].wait()
        rows = own_ref[:, i * step : (i + 1) * step]
        part = jnp.dot(rows, head_here[i], preferred_element_type=F32)
        total = part if total is None else total + part
    out_ref[...] = total


def own_logits(own, head):
    width, shard = head.shape
    return pl.pallas_call(
        own_kernel,
        in_specs=[pl.BlockSpec(memory_space=pltpu.VMEM), pl.BlockSpec(memory_space=pltpu.HBM)],
        out_shape=jax.ShapeDtypeStruct((ACT_DEV, shard), F32),
        scratch_shapes=[
            pltpu.VMEM((OWN_CHUNKS, width // CHUNKS, shard), BF16),
            pltpu.SemaphoreType.DMA((OWN_CHUNKS,)),
        ],
        compiler_params=params(),
        name="own_logits",
    )(own[0], in_hbm(head))


def logits_kernel(n_seq, *refs):
    own_ref, *block_refs, head_ref, picker_ref, logits_ref, stats_ref, packed = refs
    step = head_ref.shape[0] // CHUNKS
    each = CHUNKS // PARTS
    logits = None
    for i in range(CHUNKS):
        at = (i % each) * step
        rows = []
        for k, ref in enumerate(block_refs):
            size = ref.shape[0] // PARTS
            start = (i // each) * size
            first = start + ACT_DEV if k == 0 and i < OWN_CHUNKS else start
            rows.append(ref[first : start + size, at : at + step])
        rows = jnp.concatenate(rows, axis=0)
        head = head_ref[i * step : (i + 1) * step, :]
        part = jnp.dot(rows, head, preferred_element_type=F32)
        if i < OWN_CHUNKS:
            mine = own_ref[...] if i == 0 else jnp.zeros(own_ref.shape, F32)
            part = jnp.concatenate([mine, part], axis=0)
        logits = part if logits is None else logits + part
    logits_ref[...] = logits
    top = jnp.max(logits, axis=1, keepdims=True)
    away = logits - top
    ex = jnp.exp(away)
    sums = jnp.sum(ex, axis=1, keepdims=True)
    weighted = jnp.sum(ex * away, axis=1, keepdims=True)
    lane = iota((logits.shape[0], LANES), 1)
    pack = jnp.where(lane == 0, top, jnp.where(lane == 1, sums, weighted))
    if packed.shape[0] > n_seq * ACT_DEV:
        packed[...] = jnp.ones(packed.shape, F32)
    for q, (core, chip) in enumerate(row_order(n_seq)):
        place = pl.multiple_of(owner_of(n_seq, core, chip) * ACT_DEV, ACT_DEV)
        packed[pl.ds(place, ACT_DEV), :] = pack[q * ACT_DEV : (q + 1) * ACT_DEV]
    lines = packed[...].T[:4]
    count = jnp.sum(picker_ref[...].astype(F32))
    mine = iota(lines.shape, 1) // ACT_DEV == lax.axis_index("seq")
    lines = jnp.where(iota(lines.shape, 0) == 3, jnp.where(mine, count, 0.0), lines)
    stats_ref[...] = jnp.broadcast_to(lines[None], stats_ref.shape)


def local_logits(n_seq, n_vocab, mine, blocks, head, picker):
    shard = head.shape[1]
    rows, lanes = n_seq * ACT_DEV, lanes_of(n_seq)
    return pl.pallas_call(
        functools.partial(logits_kernel, n_seq),
        in_specs=[pl.BlockSpec(memory_space=pltpu.VMEM)] * 7,
        out_shape=[
            jax.ShapeDtypeStruct((rows, shard), F32),
            jax.ShapeDtypeStruct((n_seq * n_vocab, 4, lanes), F32),
        ],
        scratch_shapes=[pltpu.VMEM((lanes, LANES), F32)],
        compiler_params=params(),
        name="local_logits",
    )(mine, *blocks, head, picker)


def merged(stats):
    tops, sums, weights = stats[:, 0], stats[:, 1], stats[:, 2]
    top = jnp.max(tops, axis=0, keepdims=True)
    offset = tops - top
    scale = jnp.exp(offset)
    total = jnp.sum(scale * sums, axis=0, keepdims=True)
    weighted = jnp.sum(scale * (weights + offset * sums), axis=0, keepdims=True)
    return top, total, weighted / total


def entropy_kernel(n_vocab, stats_ref, picker_ref, each_ref, average_ref, column):
    stats = stats_ref[...]
    _, total, centred = merged(stats)
    entropy = jnp.log(total) - centred
    counts = jnp.sum(stats[:, 3], axis=0, keepdims=True) / n_vocab
    valid = (iota(entropy.shape, 1) % ACT_DEV).astype(F32) + 0.5 < counts
    sums = jnp.sum(jnp.where(valid, entropy, 0.0), axis=1, keepdims=True)
    average_ref[...] = sums / jnp.sum(valid.astype(F32), axis=1, keepdims=True)
    column[...] = jnp.broadcast_to(entropy, (LANES, entropy.shape[1])).T
    place = pl.multiple_of(lax.axis_index("seq") * ACT_DEV, ACT_DEV)
    mine = column[pl.ds(place, ACT_DEV), :][:, :1]
    picked = picker_ref[...].astype(F32) > 0.5
    each_ref[...] = jnp.sum(jnp.where(picked, mine, 0.0), axis=0, keepdims=True)


def entropies(n_vocab, stats, picker):
    tokens = picker.shape[1]
    return pl.pallas_call(
        functools.partial(entropy_kernel, n_vocab),
        out_shape=[
            jax.ShapeDtypeStruct((1, tokens), F32),
            jax.ShapeDtypeStruct((1, 1), F32),
        ],
        scratch_shapes=[pltpu.VMEM((stats.shape[2], LANES), F32)],
        compiler_params=params(),
        name="entropies",
    )(stats, picker)


def gradient_kernel(n_seq, n_vocab, stats_ref, logits_ref, head_ref, *refs):
    *out_refs, columns, ordered = refs
    near_refs, far_refs, last_refs = (out_refs[k * PARTS : (k + 1) * PARTS] for k in range(3))
    top, total, centred = merged(stats_ref[...])
    row = iota((8, top.shape[1]), 0)
    lines = jnp.where(row == 0, top, jnp.where(row == 1, 1.0 / total, top + centred))
    columns[...] = jnp.concatenate([lines] * (LANES // 8), axis=0).T
    for q, (core, chip) in enumerate(row_order(n_seq)):
        place = pl.multiple_of(owner_of(n_seq, core, chip) * ACT_DEV, ACT_DEV)
        ordered[q * ACT_DEV : (q + 1) * ACT_DEV] = columns[pl.ds(place, ACT_DEV), :]
    logits = logits_ref[...]
    prob = jnp.exp(logits - ordered[:, 0:1]) * ordered[:, 1:2]
    score = (prob * (ordered[:, 2:3] - logits)).astype(BF16)
    n_chip = n_seq // 2
    last = n_chip - 1
    size = near_refs[0].shape[3]
    for v in range(n_vocab):
        for c in range(PARTS):
            start = (v * PARTS + c) * size
            part = lax.dot_general(
                score,
                head_ref[start : start + size, :],
                (((1,), (1,)), ((), ())),
                preferred_element_type=F32,
            ).astype(BF16)
            blocks = part.reshape(n_seq, ACT_DEV, size)
            near_refs[c][:last, v] = blocks[:last]
            far_refs[c][:, v] = blocks[last : 2 * last]
            near_refs[c][last, v] = blocks[2 * last]
            last_refs[c][v] = blocks[2 * last + 1]


def gradients(n_seq, n_vocab, stats, logits, head):
    rows = logits.shape[0]
    n_chip = n_seq // 2
    block = (n_vocab, ACT_DEV, head.shape[0] // (n_vocab * PARTS))
    outs = [jax.ShapeDtypeStruct((n_chip,) + block, BF16)] * PARTS
    outs += [jax.ShapeDtypeStruct((n_chip - 1,) + block, BF16)] * PARTS
    outs += [jax.ShapeDtypeStruct(block, BF16)] * PARTS
    outs = pl.pallas_call(
        functools.partial(gradient_kernel, n_seq, n_vocab),
        in_specs=[pl.BlockSpec(memory_space=pltpu.VMEM)] * 3,
        out_shape=outs,
        scratch_shapes=[
            pltpu.VMEM((stats.shape[2], LANES), F32),
            pltpu.VMEM((rows, LANES), F32),
        ],
        compiler_params=params(),
        name="gradients",
    )(stats, logits, head)
    return [outs[k * PARTS : (k + 1) * PARTS] for k in range(3)]


def body(n_seq, n_vocab, hidden, head, mask):
    n_chip = n_seq // 2
    last = n_chip - 1
    bits = n_chip.bit_length() - 1

    def swap_core(value):
        return lax.ppermute(value, "seq", [(i, i ^ 1) for i in range(n_seq)])

    def swap_chip(value, step):
        flips = (2 << step, 2 << (bits - 1 - step))
        return lax.ppermute(value, "seq", [(i, i ^ flips[i & 1]) for i in range(n_seq)])

    def send_vocab(value, k):
        return lax.ppermute(value, "vocab", [(i, i ^ k) for i in range(n_vocab)])

    own, picker = select(mask, hidden)

    near = [own]
    mine = own_logits(own, head)
    for a in range(1, n_chip):
        step = a.bit_length() - 1
        source = near[a ^ (1 << step)]
        if a > 1 and a == 1 << step:
            source, mine = lax.optimization_barrier((jnp.concatenate(source, axis=1), mine))
            moved = swap_chip(source, step)
            near.append(jnp.split(moved, PARTS, axis=1))
        else:
            near.append([swap_chip(part, step) for part in source])
    early = jnp.concatenate([near[a][c] for c in range(PARTS) for a in range(last)], axis=0)
    early, near[last][0] = lax.optimization_barrier((early, near[last][0]))
    late = jnp.concatenate(near[last], axis=0)
    blocks = [early, swap_core(early), late, swap_core(late)]

    logits, stats = local_logits(n_seq, n_vocab, mine, blocks, head, picker)
    stats = lax.all_to_all(stats, ("seq", "vocab"), 0, 0, tiled=True)
    near, far, far_last = gradients(n_seq, n_vocab, stats, logits, head)
    moved = [swap_core(part) for part in far_last]
    far, _ = lax.optimization_barrier((far, moved))
    far = [swap_core(part) for part in far]
    sums = [[near[c][a].astype(F32) + far[c][a].astype(F32) for c in range(PARTS)] for a in range(last)]
    sums.append([near[c][last].astype(F32) + moved[c].astype(F32) for c in range(PARTS)])
    direct = {
        a: jnp.concatenate([part.astype(BF16) for part in sums[a]], axis=2)
        for a in range(2, n_chip)
        if a & (a - 1) == 0 and a > n_chip // 4
    }
    for a in range(last, 0, -1):
        step = a.bit_length() - 1
        target = sums[a ^ (1 << step)]
        if a in direct:
            moved = jnp.split(swap_chip(direct[a], step), PARTS, axis=2)
        else:
            moved = [swap_chip(part.astype(BF16), step) for part in sums[a]]
        for c in range(PARTS):
            if a == last:
                moved[c], _ = lax.optimization_barrier((moved[c], direct))
            target[c] += moved[c].astype(F32)

    stats, _ = lax.optimization_barrier((stats, sums[0]))
    each, average = entropies(n_vocab, stats, picker)
    column = lax.axis_index("vocab")

    def piece(k):
        parts = [lax.dynamic_index_in_dim(part, column ^ k, 0, keepdims=False) for part in sums[0]]
        return jnp.concatenate(parts, axis=1)

    result = piece(0)
    for k in range(n_vocab - 1, 0, -1):
        result = result + send_vocab(piece(k).astype(BF16), k).astype(F32)
    derivative = lax.dot_general(
        picker, result.astype(BF16), (((0,), (0,)), ((), ())), preferred_element_type=F32
    ).astype(BF16)
    return each.reshape(-1), average.reshape(()), derivative


def solution(mesh):
    n_seq, n_vocab = mesh.shape["seq"], mesh.shape["vocab"]

    def run(hidden, head, mask):
        return body(n_seq, n_vocab, hidden, head, mask)

    return jax.shard_map(
        run,
        mesh=mesh,
        in_specs=(P("seq", None), P(None, ("seq", "vocab")), P("seq")),
        out_specs=(P("seq"), P(), P("seq", "vocab")),
        check_vma=False,
    )
```

```python
import functools

import jax
import jax.numpy as jnp
from jax import lax
from jax.experimental import pallas as pl
from jax.experimental.pallas import tpu as pltpu
from jax.sharding import PartitionSpec as P

ACT_DEV = 16
PARTS = 2
LANES = 128
CHUNKS = 8
OWN_CHUNKS = 1
FLIGHT = 3
VMEM_BYTES = 24 * 2**20
F32, BF16 = jnp.float32, jnp.bfloat16


def params(size=VMEM_BYTES):
    return pltpu.CompilerParams(vmem_limit_bytes=size)


def in_hbm(value):
    return pltpu.with_memory_space_constraint(value, pltpu.HBM)


def iota(shape, axis):
    return lax.broadcasted_iota(jnp.int32, shape, axis)


def turn(bits, index):
    return sum(((index >> b) & 1) << (bits - 1 - b) for b in range(bits))


def row_order(n_seq):
    last = n_seq // 2 - 1
    early = [(core, chip) for core in (0, 1) for chip in range(last)]
    return early + [(0, last), (1, last)]


def owner_of(n_seq, core, chip):
    me = lax.axis_index("seq")
    bits = (n_seq // 2).bit_length() - 1
    odd = (me & 1) ^ core
    return me ^ (jnp.where(odd == 1, turn(bits, chip), chip) * 2 + core)


def lanes_of(n_seq):
    return -(-n_seq * ACT_DEV // LANES) * LANES


def arrive(copies, i):
    copies[i].wait()
    if i + FLIGHT < len(copies):
        copies[i + FLIGHT].start()


def select_kernel(mask_ref, hidden_ref, *refs):
    *own_refs, picker_ref, mask_here, hidden_here, mask_sem, sems = refs
    chunks, tokens, step = hidden_here.shape
    copies = [
        pltpu.make_async_copy(
            hidden_ref.at[:, pl.ds(i * step, step)], hidden_here.at[i], sems.at[i]
        )
        for i in range(chunks)
    ]
    mask_copy = pltpu.make_async_copy(mask_ref, mask_here, mask_sem)
    mask_copy.start()
    for copy in copies[:FLIGHT]:
        copy.start()
    mask_copy.wait()
    mask = mask_here[...]
    upper = (iota((tokens, tokens), 0) <= iota((tokens, tokens), 1)).astype(BF16)
    ones = jnp.broadcast_to(mask.astype(F32).astype(BF16), (ACT_DEV, tokens))
    slots = jnp.dot(ones, upper, preferred_element_type=F32).astype(jnp.int32) - 1
    picker = (slots == iota((ACT_DEV, tokens), 0)) & (mask == 1)
    picker = picker.astype(F32).astype(BF16)
    picker_ref[...] = picker
    each = chunks // len(own_refs)
    for i in range(chunks):
        arrive(copies, i)
        own = jnp.dot(picker, hidden_here[i], preferred_element_type=F32)
        at = (i % each) * step
        own_refs[i // each][:, at : at + step] = own.astype(BF16)


def select(mask, hidden):
    tokens, width = hidden.shape
    chunks = 4
    own = jax.ShapeDtypeStruct((ACT_DEV, width // PARTS), BF16)
    *own, picker = pl.pallas_call(
        select_kernel,
        in_specs=[pl.BlockSpec(memory_space=pltpu.HBM)] * 2,
        out_shape=[own] * PARTS + [jax.ShapeDtypeStruct((ACT_DEV, tokens), BF16)],
        scratch_shapes=[
            pltpu.VMEM((1, tokens), jnp.int32),
            pltpu.VMEM((chunks, tokens, width // chunks), BF16),
            pltpu.SemaphoreType.DMA,
            pltpu.SemaphoreType.DMA((chunks,)),
        ],
        compiler_params=params(60 * 2**20),
        name="select_rows",
    )(in_hbm(mask.reshape(1, tokens)), in_hbm(hidden))
    return own, picker


def own_kernel(own_ref, head_ref, out_ref, head_here, sems):
    chunks, step, _ = head_here.shape
    copies = [
        pltpu.make_async_copy(head_ref.at[pl.ds(i * step, step), :], head_here.at[i], sems.at[i])
        for i in range(chunks)
    ]
    for copy in copies:
        copy.start()
    total = None
    for i in range(chunks):
        copies[i].wait()
        rows = own_ref[:, i * step : (i + 1) * step]
        part = jnp.dot(rows, head_here[i], preferred_element_type=F32)
        total = part if total is None else total + part
    out_ref[...] = total


def own_logits(own, head):
    width, shard = head.shape
    return pl.pallas_call(
        own_kernel,
        in_specs=[pl.BlockSpec(memory_space=pltpu.VMEM), pl.BlockSpec(memory_space=pltpu.HBM)],
        out_shape=jax.ShapeDtypeStruct((ACT_DEV, shard), F32),
        scratch_shapes=[
            pltpu.VMEM((OWN_CHUNKS, width // CHUNKS, shard), BF16),
            pltpu.SemaphoreType.DMA((OWN_CHUNKS,)),
        ],
        compiler_params=params(),
        name="own_logits",
    )(own[0], in_hbm(head))


def logits_kernel(n_seq, *refs):
    own_ref, *block_refs, head_ref, picker_ref, logits_ref, stats_ref, packed = refs
    step = head_ref.shape[0] // CHUNKS
    each = CHUNKS // PARTS
    logits = None
    for i in range(CHUNKS):
        at = (i % each) * step
        rows = []
        for k, ref in enumerate(block_refs):
            size = ref.shape[0] // PARTS
            start = (i // each) * size
            first = start + ACT_DEV if k == 0 and i < OWN_CHUNKS else start
            rows.append(ref[first : start + size, at : at + step])
        rows = jnp.concatenate(rows, axis=0)
        head = head_ref[i * step : (i + 1) * step, :]
        part = jnp.dot(rows, head, preferred_element_type=F32)
        if i < OWN_CHUNKS:
            mine = own_ref[...] if i == 0 else jnp.zeros(own_ref.shape, F32)
            part = jnp.concatenate([mine, part], axis=0)
        logits = part if logits is None else logits + part
    logits_ref[...] = logits
    top = jnp.max(logits, axis=1, keepdims=True)
    away = logits - top
    ex = jnp.exp(away)
    sums = jnp.sum(ex, axis=1, keepdims=True)
    weighted = jnp.sum(ex * away, axis=1, keepdims=True)
    lane = iota((logits.shape[0], LANES), 1)
    pack = jnp.where(lane == 0, top, jnp.where(lane == 1, sums, weighted))
    if packed.shape[0] > n_seq * ACT_DEV:
        packed[...] = jnp.ones(packed.shape, F32)
    for q, (core, chip) in enumerate(row_order(n_seq)):
        place = pl.multiple_of(owner_of(n_seq, core, chip) * ACT_DEV, ACT_DEV)
        packed[pl.ds(place, ACT_DEV), :] = pack[q * ACT_DEV : (q + 1) * ACT_DEV]
    lines = packed[...].T[:4]
    count = jnp.sum(picker_ref[...].astype(F32))
    mine = iota(lines.shape, 1) // ACT_DEV == lax.axis_index("seq")
    lines = jnp.where(iota(lines.shape, 0) == 3, jnp.where(mine, count, 0.0), lines)
    stats_ref[...] = jnp.broadcast_to(lines[None], stats_ref.shape)


def local_logits(n_seq, n_vocab, mine, blocks, head, picker):
    shard = head.shape[1]
    rows, lanes = n_seq * ACT_DEV, lanes_of(n_seq)
    return pl.pallas_call(
        functools.partial(logits_kernel, n_seq),
        in_specs=[pl.BlockSpec(memory_space=pltpu.VMEM)] * 7,
        out_shape=[
            jax.ShapeDtypeStruct((rows, shard), F32),
            jax.ShapeDtypeStruct((n_seq * n_vocab, 4, lanes), F32),
        ],
        scratch_shapes=[pltpu.VMEM((lanes, LANES), F32)],
        compiler_params=params(),
        name="local_logits",
    )(mine, *blocks, head, picker)


def merged(stats):
    tops, sums, weights = stats[:, 0], stats[:, 1], stats[:, 2]
    top = jnp.max(tops, axis=0, keepdims=True)
    offset = tops - top
    scale = jnp.exp(offset)
    total = jnp.sum(scale * sums, axis=0, keepdims=True)
    weighted = jnp.sum(scale * (weights + offset * sums), axis=0, keepdims=True)
    return top, total, weighted / total


def entropy_kernel(n_vocab, stats_ref, picker_ref, each_ref, average_ref, column):
    stats = stats_ref[...]
    _, total, centred = merged(stats)
    entropy = jnp.log(total) - centred
    counts = jnp.sum(stats[:, 3], axis=0, keepdims=True) / n_vocab
    valid = (iota(entropy.shape, 1) % ACT_DEV).astype(F32) + 0.5 < counts
    sums = jnp.sum(jnp.where(valid, entropy, 0.0), axis=1, keepdims=True)
    average_ref[...] = sums / jnp.sum(valid.astype(F32), axis=1, keepdims=True)
    column[...] = jnp.broadcast_to(entropy, (LANES, entropy.shape[1])).T
    place = pl.multiple_of(lax.axis_index("seq") * ACT_DEV, ACT_DEV)
    mine = column[pl.ds(place, ACT_DEV), :][:, :1]
    picked = picker_ref[...].astype(F32) > 0.5
    each_ref[...] = jnp.sum(jnp.where(picked, mine, 0.0), axis=0, keepdims=True)


def entropies(n_vocab, stats, picker):
    tokens = picker.shape[1]
    return pl.pallas_call(
        functools.partial(entropy_kernel, n_vocab),
        out_shape=[
            jax.ShapeDtypeStruct((1, tokens), F32),
            jax.ShapeDtypeStruct((1, 1), F32),
        ],
        scratch_shapes=[pltpu.VMEM((stats.shape[2], LANES), F32)],
        compiler_params=params(),
        name="entropies",
    )(stats, picker)


def gradient_kernel(n_seq, n_vocab, stats_ref, logits_ref, head_ref, *refs):
    *out_refs, columns, ordered = refs
    near_refs, far_refs, last_refs = (out_refs[k * PARTS : (k + 1) * PARTS] for k in range(3))
    top, total, centred = merged(stats_ref[...])
    row = iota((8, top.shape[1]), 0)
    lines = jnp.where(row == 0, top, jnp.where(row == 1, 1.0 / total, top + centred))
    columns[...] = jnp.concatenate([lines] * (LANES // 8), axis=0).T
    for q, (core, chip) in enumerate(row_order(n_seq)):
        place = pl.multiple_of(owner_of(n_seq, core, chip) * ACT_DEV, ACT_DEV)
        ordered[q * ACT_DEV : (q + 1) * ACT_DEV] = columns[pl.ds(place, ACT_DEV), :]
    logits = logits_ref[...]
    prob = jnp.exp(logits - ordered[:, 0:1]) * ordered[:, 1:2]
    score = (prob * (ordered[:, 2:3] - logits)).astype(BF16)
    n_chip = n_seq // 2
    last = n_chip - 1
    size = near_refs[0].shape[3]
    for v in range(n_vocab):
        for c in range(PARTS):
            start = (v * PARTS + c) * size
            part = lax.dot_general(
                score,
                head_ref[start : start + size, :],
                (((1,), (1,)), ((), ())),
                preferred_element_type=F32,
            ).astype(BF16)
            blocks = part.reshape(n_seq, ACT_DEV, size)
            near_refs[c][:last, v] = blocks[:last]
            far_refs[c][:, v] = blocks[last : 2 * last]
            near_refs[c][last, v] = blocks[2 * last]
            last_refs[c][v] = blocks[2 * last + 1]


def gradients(n_seq, n_vocab, stats, logits, head):
    rows = logits.shape[0]
    n_chip = n_seq // 2
    block = (n_vocab, ACT_DEV, head.shape[0] // (n_vocab * PARTS))
    outs = [jax.ShapeDtypeStruct((n_chip,) + block, BF16)] * PARTS
    outs += [jax.ShapeDtypeStruct((n_chip - 1,) + block, BF16)] * PARTS
    outs += [jax.ShapeDtypeStruct(block, BF16)] * PARTS
    outs = pl.pallas_call(
        functools.partial(gradient_kernel, n_seq, n_vocab),
        in_specs=[pl.BlockSpec(memory_space=pltpu.VMEM)] * 3,
        out_shape=outs,
        scratch_shapes=[
            pltpu.VMEM((stats.shape[2], LANES), F32),
            pltpu.VMEM((rows, LANES), F32),
        ],
        compiler_params=params(),
        name="gradients",
    )(stats, logits, head)
    return [outs[k * PARTS : (k + 1) * PARTS] for k in range(3)]


def body(n_seq, n_vocab, hidden, head, mask):
    n_chip = n_seq // 2
    last = n_chip - 1
    bits = n_chip.bit_length() - 1

    def swap_core(value):
        return lax.ppermute(value, "seq", [(i, i ^ 1) for i in range(n_seq)])

    def swap_chip(value, step):
        flips = (2 << step, 2 << (bits - 1 - step))
        return lax.ppermute(value, "seq", [(i, i ^ flips[i & 1]) for i in range(n_seq)])

    def send_vocab(value, k):
        return lax.ppermute(value, "vocab", [(i, i ^ k) for i in range(n_vocab)])

    own, picker = select(mask, hidden)

    near = [own]
    mine = own_logits(own, head)
    for a in range(1, n_chip):
        step = a.bit_length() - 1
        source = near[a ^ (1 << step)]
        if a > 1 and a == 1 << step:
            source, mine = lax.optimization_barrier((jnp.concatenate(source, axis=1), mine))
            moved = swap_chip(source, step)
            near.append(jnp.split(moved, PARTS, axis=1))
        else:
            near.append([swap_chip(part, step) for part in source])
    early = jnp.concatenate([near[a][c] for c in range(PARTS) for a in range(last)], axis=0)
    early, near[last][0] = lax.optimization_barrier((early, near[last][0]))
    late = jnp.concatenate(near[last], axis=0)
    blocks = [early, swap_core(early), late, swap_core(late)]

    logits, stats = local_logits(n_seq, n_vocab, mine, blocks, head, picker)
    stats = lax.all_to_all(stats, ("seq", "vocab"), 0, 0, tiled=True)
    near, far, far_last = gradients(n_seq, n_vocab, stats, logits, head)
    moved = [swap_core(part) for part in far_last]
    far, _ = lax.optimization_barrier((far, moved))
    far = [swap_core(part) for part in far]
    sums = [[near[c][a].astype(F32) + far[c][a].astype(F32) for c in range(PARTS)] for a in range(last)]
    sums.append([near[c][last].astype(F32) + moved[c].astype(F32) for c in range(PARTS)])
    direct = {
        a: jnp.concatenate([part.astype(BF16) for part in sums[a]], axis=2)
        for a in range(2, n_chip)
        if a & (a - 1) == 0 and a > n_chip // 4
    }
    for a in range(last, 0, -1):
        step = a.bit_length() - 1
        target = sums[a ^ (1 << step)]
        if a in direct:
            moved = jnp.split(swap_chip(direct[a], step), PARTS, axis=2)
        else:
            moved = [swap_chip(part.astype(BF16), step) for part in sums[a]]
        for c in range(PARTS):
            if a == last:
                moved[c], _ = lax.optimization_barrier((moved[c], direct))
            target[c] += moved[c].astype(F32)

    stats, _ = lax.optimization_barrier((stats, sums[0]))
    each, average = entropies(n_vocab, stats, picker)
    column = lax.axis_index("vocab")

    def piece(k):
        parts = [lax.dynamic_index_in_dim(part, column ^ k, 0, keepdims=False) for part in sums[0]]
        return jnp.concatenate(parts, axis=1)

    result = piece(0)
    for k in range(n_vocab - 1, 0, -1):
        result = result + send_vocab(piece(k).astype(BF16), k).astype(F32)
    derivative = lax.dot_general(
        picker, result.astype(BF16), (((0,), (0,)), ((), ())), preferred_element_type=F32
    ).astype(BF16)
    return each.reshape(-1), average.reshape(()), derivative


def solution(mesh):
    n_seq, n_vocab = mesh.shape["seq"], mesh.shape["vocab"]

    def run(hidden, head, mask):
        return body(n_seq, n_vocab, hidden, head, mask)

    return jax.shard_map(
        run,
        mesh=mesh,
        in_specs=(P("seq", None), P(None, ("seq", "vocab")), P("seq")),
        out_specs=(P("seq"), P(), P("seq", "vocab")),
        check_vma=False,
    )
```

```python
import functools

import jax
import jax.numpy as jnp
from jax import lax
from jax.experimental import pallas as pl
from jax.experimental.pallas import tpu as pltpu
from jax.sharding import PartitionSpec as P

ACT_DEV = 16
PARTS = 2
LANES = 128
CHUNKS = 8
OWN_CHUNKS = 1
FLIGHT = 3
VMEM_BYTES = 24 * 2**20
F32, BF16 = jnp.float32, jnp.bfloat16


def params():
    return pltpu.CompilerParams(vmem_limit_bytes=VMEM_BYTES)


def in_hbm(value):
    return pltpu.with_memory_space_constraint(value, pltpu.HBM)


def iota(shape, axis):
    return lax.broadcasted_iota(jnp.int32, shape, axis)


def turn(bits, index):
    return sum(((index >> b) & 1) << (bits - 1 - b) for b in range(bits))


def row_order(n_seq):
    last = n_seq // 2 - 1
    early = [(core, chip) for core in (0, 1) for chip in range(last)]
    return early + [(0, last), (1, last)]


def owner_of(n_seq, core, chip):
    me = lax.axis_index("seq")
    bits = (n_seq // 2).bit_length() - 1
    odd = (me & 1) ^ core
    return me ^ (jnp.where(odd == 1, turn(bits, chip), chip) * 2 + core)


def lanes_of(n_seq):
    return -(-n_seq * ACT_DEV // LANES) * LANES


def arrive(copies, i):
    copies[i].wait()
    if i + FLIGHT < len(copies):
        copies[i + FLIGHT].start()


def select_kernel(mask_ref, hidden_ref, *refs):
    *own_refs, picker_ref, mask_here, hidden_here, mask_sem, sems = refs
    chunks, tokens, step = hidden_here.shape
    copies = [
        pltpu.make_async_copy(
            hidden_ref.at[:, pl.ds(i * step, step)], hidden_here.at[i], sems.at[i]
        )
        for i in range(chunks)
    ]
    mask_copy = pltpu.make_async_copy(mask_ref, mask_here, mask_sem)
    mask_copy.start()
    for copy in copies[:FLIGHT]:
        copy.start()
    mask_copy.wait()
    mask = mask_here[...]
    upper = (iota((tokens, tokens), 0) <= iota((tokens, tokens), 1)).astype(BF16)
    ones = jnp.broadcast_to(mask.astype(F32).astype(BF16), (ACT_DEV, tokens))
    slots = jnp.dot(ones, upper, preferred_element_type=F32).astype(jnp.int32) - 1
    picker = (slots == iota((ACT_DEV, tokens), 0)) & (mask == 1)
    picker = picker.astype(F32).astype(BF16)
    picker_ref[...] = picker
    each = chunks // len(own_refs)
    for i in range(chunks):
        arrive(copies, i)
        own = jnp.dot(picker, hidden_here[i], preferred_element_type=F32)
        at = (i % each) * step
        own_refs[i // each][:, at : at + step] = own.astype(BF16)


def select(mask, hidden):
    tokens, width = hidden.shape
    chunks = 4
    own = jax.ShapeDtypeStruct((ACT_DEV, width // PARTS), BF16)
    *own, picker = pl.pallas_call(
        select_kernel,
        in_specs=[pl.BlockSpec(memory_space=pltpu.HBM)] * 2,
        out_shape=[own] * PARTS + [jax.ShapeDtypeStruct((ACT_DEV, tokens), BF16)],
        scratch_shapes=[
            pltpu.VMEM((1, tokens), jnp.int32),
            pltpu.VMEM((chunks, tokens, width // chunks), BF16),
            pltpu.SemaphoreType.DMA,
            pltpu.SemaphoreType.DMA((chunks,)),
        ],
        compiler_params=params(),
        name="select_rows",
    )(in_hbm(mask.reshape(1, tokens)), in_hbm(hidden))
    return own, picker


def own_kernel(own_ref, head_ref, out_ref, head_here, sems):
    chunks, step, _ = head_here.shape
    copies = [
        pltpu.make_async_copy(head_ref.at[pl.ds(i * step, step), :], head_here.at[i], sems.at[i])
        for i in range(chunks)
    ]
    for copy in copies:
        copy.start()
    total = None
    for i in range(chunks):
        copies[i].wait()
        rows = own_ref[:, i * step : (i + 1) * step]
        part = jnp.dot(rows, head_here[i], preferred_element_type=F32)
        total = part if total is None else total + part
    out_ref[...] = total


def own_logits(own, head):
    width, shard = head.shape
    return pl.pallas_call(
        own_kernel,
        in_specs=[pl.BlockSpec(memory_space=pltpu.VMEM), pl.BlockSpec(memory_space=pltpu.HBM)],
        out_shape=jax.ShapeDtypeStruct((ACT_DEV, shard), F32),
        scratch_shapes=[
            pltpu.VMEM((OWN_CHUNKS, width // CHUNKS, shard), BF16),
            pltpu.SemaphoreType.DMA((OWN_CHUNKS,)),
        ],
        compiler_params=params(),
        name="own_logits",
    )(own[0], in_hbm(head))


def logits_kernel(n_seq, *refs):
    own_ref, *block_refs, head_ref, picker_ref, logits_ref, stats_ref, packed = refs
    step = head_ref.shape[0] // CHUNKS
    each = CHUNKS // PARTS
    logits = None
    for i in range(CHUNKS):
        at = (i % each) * step
        rows = []
        for k, ref in enumerate(block_refs):
            size = ref.shape[0] // PARTS
            start = (i // each) * size
            first = start + ACT_DEV if k == 0 and i < OWN_CHUNKS else start
            rows.append(ref[first : start + size, at : at + step])
        rows = jnp.concatenate(rows, axis=0)
        head = head_ref[i * step : (i + 1) * step, :]
        part = jnp.dot(rows, head, preferred_element_type=F32)
        if i < OWN_CHUNKS:
            mine = own_ref[...] if i == 0 else jnp.zeros(own_ref.shape, F32)
            part = jnp.concatenate([mine, part], axis=0)
        logits = part if logits is None else logits + part
    logits_ref[...] = logits
    top = jnp.max(logits, axis=1, keepdims=True)
    away = logits - top
    ex = jnp.exp(away)
    sums = jnp.sum(ex, axis=1, keepdims=True)
    weighted = jnp.sum(ex * away, axis=1, keepdims=True)
    lane = iota((logits.shape[0], LANES), 1)
    pack = jnp.where(lane == 0, top, jnp.where(lane == 1, sums, weighted))
    if packed.shape[0] > n_seq * ACT_DEV:
        packed[...] = jnp.ones(packed.shape, F32)
    for q, (core, chip) in enumerate(row_order(n_seq)):
        place = pl.multiple_of(owner_of(n_seq, core, chip) * ACT_DEV, ACT_DEV)
        packed[pl.ds(place, ACT_DEV), :] = pack[q * ACT_DEV : (q + 1) * ACT_DEV]
    lines = packed[...].T[:4]
    count = jnp.sum(picker_ref[...].astype(F32))
    mine = iota(lines.shape, 1) // ACT_DEV == lax.axis_index("seq")
    lines = jnp.where(iota(lines.shape, 0) == 3, jnp.where(mine, count, 0.0), lines)
    stats_ref[...] = jnp.broadcast_to(lines[None], stats_ref.shape)


def local_logits(n_seq, n_vocab, mine, blocks, head, picker):
    shard = head.shape[1]
    rows, lanes = n_seq * ACT_DEV, lanes_of(n_seq)
    return pl.pallas_call(
        functools.partial(logits_kernel, n_seq),
        in_specs=[pl.BlockSpec(memory_space=pltpu.VMEM)] * 7,
        out_shape=[
            jax.ShapeDtypeStruct((rows, shard), F32),
            jax.ShapeDtypeStruct((n_seq * n_vocab, 4, lanes), F32),
        ],
        scratch_shapes=[pltpu.VMEM((lanes, LANES), F32)],
        compiler_params=params(),
        name="local_logits",
    )(mine, *blocks, head, picker)


def merged(stats):
    tops, sums, weights = stats[:, 0], stats[:, 1], stats[:, 2]
    top = jnp.max(tops, axis=0, keepdims=True)
    offset = tops - top
    scale = jnp.exp(offset)
    total = jnp.sum(scale * sums, axis=0, keepdims=True)
    weighted = jnp.sum(scale * (weights + offset * sums), axis=0, keepdims=True)
    return top, total, weighted / total


def entropy_kernel(n_vocab, stats_ref, picker_ref, each_ref, average_ref, column):
    stats = stats_ref[...]
    _, total, centred = merged(stats)
    entropy = jnp.log(total) - centred
    counts = jnp.sum(stats[:, 3], axis=0, keepdims=True) / n_vocab
    valid = (iota(entropy.shape, 1) % ACT_DEV).astype(F32) + 0.5 < counts
    sums = jnp.sum(jnp.where(valid, entropy, 0.0), axis=1, keepdims=True)
    average_ref[...] = sums / jnp.sum(valid.astype(F32), axis=1, keepdims=True)
    column[...] = jnp.broadcast_to(entropy, (LANES, entropy.shape[1])).T
    place = pl.multiple_of(lax.axis_index("seq") * ACT_DEV, ACT_DEV)
    mine = column[pl.ds(place, ACT_DEV), :][:, :1]
    picked = picker_ref[...].astype(F32) > 0.5
    each_ref[...] = jnp.sum(jnp.where(picked, mine, 0.0), axis=0, keepdims=True)


def entropies(n_vocab, stats, picker):
    tokens = picker.shape[1]
    return pl.pallas_call(
        functools.partial(entropy_kernel, n_vocab),
        out_shape=[
            jax.ShapeDtypeStruct((1, tokens), F32),
            jax.ShapeDtypeStruct((1, 1), F32),
        ],
        scratch_shapes=[pltpu.VMEM((stats.shape[2], LANES), F32)],
        compiler_params=params(),
        name="entropies",
    )(stats, picker)


def gradient_kernel(n_seq, n_vocab, stats_ref, logits_ref, head_ref, *refs):
    *out_refs, columns, ordered = refs
    near_refs, far_refs, last_refs = (out_refs[k * PARTS : (k + 1) * PARTS] for k in range(3))
    top, total, centred = merged(stats_ref[...])
    row = iota((8, top.shape[1]), 0)
    lines = jnp.where(row == 0, top, jnp.where(row == 1, 1.0 / total, top + centred))
    columns[...] = jnp.concatenate([lines] * (LANES // 8), axis=0).T
    for q, (core, chip) in enumerate(row_order(n_seq)):
        place = pl.multiple_of(owner_of(n_seq, core, chip) * ACT_DEV, ACT_DEV)
        ordered[q * ACT_DEV : (q + 1) * ACT_DEV] = columns[pl.ds(place, ACT_DEV), :]
    logits = logits_ref[...]
    prob = jnp.exp(logits - ordered[:, 0:1]) * ordered[:, 1:2]
    score = (prob * (ordered[:, 2:3] - logits)).astype(BF16)
    n_chip = n_seq // 2
    last = n_chip - 1
    size = near_refs[0].shape[3]
    for v in range(n_vocab):
        for c in range(PARTS):
            start = (v * PARTS + c) * size
            part = lax.dot_general(
                score,
                head_ref[start : start + size, :],
                (((1,), (1,)), ((), ())),
                preferred_element_type=F32,
            ).astype(BF16)
            blocks = part.reshape(n_seq, ACT_DEV, size)
            near_refs[c][:last, v] = blocks[:last]
            far_refs[c][:, v] = blocks[last : 2 * last]
            near_refs[c][last, v] = blocks[2 * last]
            last_refs[c][v] = blocks[2 * last + 1]


def gradients(n_seq, n_vocab, stats, logits, head):
    rows = logits.shape[0]
    n_chip = n_seq // 2
    block = (n_vocab, ACT_DEV, head.shape[0] // (n_vocab * PARTS))
    outs = [jax.ShapeDtypeStruct((n_chip,) + block, BF16)] * PARTS
    outs += [jax.ShapeDtypeStruct((n_chip - 1,) + block, BF16)] * PARTS
    outs += [jax.ShapeDtypeStruct(block, BF16)] * PARTS
    outs = pl.pallas_call(
        functools.partial(gradient_kernel, n_seq, n_vocab),
        in_specs=[pl.BlockSpec(memory_space=pltpu.VMEM)] * 3,
        out_shape=outs,
        scratch_shapes=[
            pltpu.VMEM((stats.shape[2], LANES), F32),
            pltpu.VMEM((rows, LANES), F32),
        ],
        compiler_params=params(),
        name="gradients",
    )(stats, logits, head)
    return [outs[k * PARTS : (k + 1) * PARTS] for k in range(3)]


def body(n_seq, n_vocab, hidden, head, mask):
    n_chip = n_seq // 2
    last = n_chip - 1
    bits = n_chip.bit_length() - 1

    def swap_core(value):
        return lax.ppermute(value, "seq", [(i, i ^ 1) for i in range(n_seq)])

    def swap_chip(value, step):
        flips = (2 << step, 2 << (bits - 1 - step))
        return lax.ppermute(value, "seq", [(i, i ^ flips[i & 1]) for i in range(n_seq)])

    def send_vocab(value, k):
        return lax.ppermute(value, "vocab", [(i, i ^ k) for i in range(n_vocab)])

    own, picker = select(mask, hidden)

    near = [own]
    mine = own_logits(own, head)
    for a in range(1, n_chip):
        step = a.bit_length() - 1
        source = near[a ^ (1 << step)]
        if a > 1 and a == 1 << step:
            source, mine = lax.optimization_barrier((jnp.concatenate(source, axis=1), mine))
            moved = swap_chip(source, step)
            near.append(jnp.split(moved, PARTS, axis=1))
        else:
            near.append([swap_chip(part, step) for part in source])
    early = jnp.concatenate([near[a][c] for c in range(PARTS) for a in range(last)], axis=0)
    early, near[last][0] = lax.optimization_barrier((early, near[last][0]))
    late = jnp.concatenate(near[last], axis=0)
    blocks = [early, swap_core(early), late, swap_core(late)]

    logits, stats = local_logits(n_seq, n_vocab, mine, blocks, head, picker)
    stats = lax.all_to_all(stats, ("vocab", "seq"), 0, 0, tiled=True)
    near, far, far_last = gradients(n_seq, n_vocab, stats, logits, head)
    moved = [swap_core(part) for part in far_last]
    far, _ = lax.optimization_barrier((far, moved))
    far = [swap_core(part) for part in far]
    sums = [[near[c][a].astype(F32) + far[c][a].astype(F32) for c in range(PARTS)] for a in range(last)]
    sums.append([near[c][last].astype(F32) + moved[c].astype(F32) for c in range(PARTS)])
    direct = {
        a: jnp.concatenate([part.astype(BF16) for part in sums[a]], axis=2)
        for a in range(2, n_chip)
        if a & (a - 1) == 0 and a > n_chip // 4
    }
    for a in range(last, 0, -1):
        step = a.bit_length() - 1
        target = sums[a ^ (1 << step)]
        if a in direct:
            moved = jnp.split(swap_chip(direct[a], step), PARTS, axis=2)
        else:
            moved = [swap_chip(part.astype(BF16), step) for part in sums[a]]
        for c in range(PARTS):
            if a == last:
                moved[c], _ = lax.optimization_barrier((moved[c], direct))
            target[c] += moved[c].astype(F32)

    stats, _ = lax.optimization_barrier((stats, sums[0]))
    each, average = entropies(n_vocab, stats, picker)
    column = lax.axis_index("vocab")

    def piece(k):
        parts = [lax.dynamic_index_in_dim(part, column ^ k, 0, keepdims=False) for part in sums[0]]
        return jnp.concatenate(parts, axis=1)

    result = piece(0)
    for k in range(n_vocab - 1, 0, -1):
        result = result + send_vocab(piece(k).astype(BF16), k).astype(F32)
    derivative = lax.dot_general(
        picker, result.astype(BF16), (((0,), (0,)), ((), ())), preferred_element_type=F32
    ).astype(BF16)
    return each.reshape(-1), average.reshape(()), derivative


def solution(mesh):
    n_seq, n_vocab = mesh.shape["seq"], mesh.shape["vocab"]

    def run(hidden, head, mask):
        return body(n_seq, n_vocab, hidden, head, mask)

    return jax.shard_map(
        run,
        mesh=mesh,
        in_specs=(P("seq", None), P(None, ("seq", "vocab")), P("seq")),
        out_specs=(P("seq"), P(), P("seq", "vocab")),
        check_vma=False,
    )
```

```python
import functools

import jax
import jax.numpy as jnp
from jax import lax
from jax.experimental import pallas as pl
from jax.experimental.pallas import tpu as pltpu
from jax.sharding import PartitionSpec as P

ACT_DEV = 16
PARTS = 2
LANES = 128
CHUNKS = 8
OWN_CHUNKS = 1
FLIGHT = 3
VMEM_BYTES = 24 * 2**20
F32, BF16 = jnp.float32, jnp.bfloat16


def params():
    return pltpu.CompilerParams(vmem_limit_bytes=VMEM_BYTES)


def in_hbm(value):
    return pltpu.with_memory_space_constraint(value, pltpu.HBM)


def iota(shape, axis):
    return lax.broadcasted_iota(jnp.int32, shape, axis)


def turn(bits, index):
    return sum(((index >> b) & 1) << (bits - 1 - b) for b in range(bits))


def row_order(n_seq):
    last = n_seq // 2 - 1
    early = [(core, chip) for core in (0, 1) for chip in range(last)]
    return early + [(0, last), (1, last)]


def owner_of(n_seq, core, chip):
    me = lax.axis_index("seq")
    bits = (n_seq // 2).bit_length() - 1
    odd = (me & 1) ^ core
    return me ^ (jnp.where(odd == 1, turn(bits, chip), chip) * 2 + core)


def lanes_of(n_seq):
    return -(-n_seq * ACT_DEV // LANES) * LANES


def arrive(copies, i):
    copies[i].wait()
    if i + FLIGHT < len(copies):
        copies[i + FLIGHT].start()


def select_kernel(mask_ref, hidden_ref, *refs):
    *own_refs, picker_ref, mask_here, hidden_here, mask_sem, sems = refs
    chunks, tokens, step = hidden_here.shape
    copies = [
        pltpu.make_async_copy(
            hidden_ref.at[:, pl.ds(i * step, step)], hidden_here.at[i], sems.at[i]
        )
        for i in range(chunks)
    ]
    mask_copy = pltpu.make_async_copy(mask_ref, mask_here, mask_sem)
    mask_copy.start()
    for copy in copies[:FLIGHT]:
        copy.start()
    mask_copy.wait()
    mask = mask_here[...]
    upper = (iota((tokens, tokens), 0) <= iota((tokens, tokens), 1)).astype(BF16)
    ones = jnp.broadcast_to(mask.astype(F32).astype(BF16), (ACT_DEV, tokens))
    slots = jnp.dot(ones, upper, preferred_element_type=F32).astype(jnp.int32) - 1
    picker = (slots == iota((ACT_DEV, tokens), 0)) & (mask == 1)
    picker = picker.astype(F32).astype(BF16)
    picker_ref[...] = picker
    each = chunks // len(own_refs)
    for i in range(chunks):
        arrive(copies, i)
        own = jnp.dot(picker, hidden_here[i], preferred_element_type=F32)
        at = (i % each) * step
        own_refs[i // each][:, at : at + step] = own.astype(BF16)


def select(mask, hidden):
    tokens, width = hidden.shape
    chunks = 4
    own = jax.ShapeDtypeStruct((ACT_DEV, width // PARTS), BF16)
    *own, picker = pl.pallas_call(
        select_kernel,
        in_specs=[pl.BlockSpec(memory_space=pltpu.HBM)] * 2,
        out_shape=[own] * PARTS + [jax.ShapeDtypeStruct((ACT_DEV, tokens), BF16)],
        scratch_shapes=[
            pltpu.VMEM((1, tokens), jnp.int32),
            pltpu.VMEM((chunks, tokens, width // chunks), BF16),
            pltpu.SemaphoreType.DMA,
            pltpu.SemaphoreType.DMA((chunks,)),
        ],
        compiler_params=params(),
        name="select_rows",
    )(in_hbm(mask.reshape(1, tokens)), in_hbm(hidden))
    return own, picker


def own_kernel(own_ref, head_ref, out_ref, head_here, sems):
    chunks, step, _ = head_here.shape
    copies = [
        pltpu.make_async_copy(head_ref.at[pl.ds(i * step, step), :], head_here.at[i], sems.at[i])
        for i in range(chunks)
    ]
    for copy in copies:
        copy.start()
    total = None
    for i in range(chunks):
        copies[i].wait()
        rows = own_ref[:, i * step : (i + 1) * step]
        part = jnp.dot(rows, head_here[i], preferred_element_type=F32)
        total = part if total is None else total + part
    out_ref[...] = total


def own_logits(own, head):
    width, shard = head.shape
    return pl.pallas_call(
        own_kernel,
        in_specs=[pl.BlockSpec(memory_space=pltpu.VMEM), pl.BlockSpec(memory_space=pltpu.HBM)],
        out_shape=jax.ShapeDtypeStruct((ACT_DEV, shard), F32),
        scratch_shapes=[
            pltpu.VMEM((OWN_CHUNKS, width // CHUNKS, shard), BF16),
            pltpu.SemaphoreType.DMA((OWN_CHUNKS,)),
        ],
        compiler_params=params(),
        name="own_logits",
    )(own[0], in_hbm(head))


def logits_kernel(n_seq, *refs):
    own_ref, *block_refs, head_ref, picker_ref, logits_ref, stats_ref, packed = refs
    step = head_ref.shape[0] // CHUNKS
    each = CHUNKS // PARTS
    logits = None
    for i in range(CHUNKS):
        at = (i % each) * step
        rows = []
        for k, ref in enumerate(block_refs):
            size = ref.shape[0] // PARTS
            start = (i // each) * size
            first = start + ACT_DEV if k == 0 and i < OWN_CHUNKS else start
            rows.append(ref[first : start + size, at : at + step])
        rows = jnp.concatenate(rows, axis=0)
        head = head_ref[i * step : (i + 1) * step, :]
        part = jnp.dot(rows, head, preferred_element_type=F32)
        if i < OWN_CHUNKS:
            mine = own_ref[...] if i == 0 else jnp.zeros(own_ref.shape, F32)
            part = jnp.concatenate([mine, part], axis=0)
        logits = part if logits is None else logits + part
    logits_ref[...] = logits
    top = jnp.max(logits, axis=1, keepdims=True)
    away = logits - top
    ex = jnp.exp(away)
    sums = jnp.sum(ex, axis=1, keepdims=True)
    weighted = jnp.sum(ex * away, axis=1, keepdims=True)
    lane = iota((logits.shape[0], LANES), 1)
    pack = jnp.where(lane == 0, top, jnp.where(lane == 1, sums, weighted))
    if packed.shape[0] > n_seq * ACT_DEV:
        packed[...] = jnp.ones(packed.shape, F32)
    for q, (core, chip) in enumerate(row_order(n_seq)):
        place = pl.multiple_of(owner_of(n_seq, core, chip) * ACT_DEV, ACT_DEV)
        packed[pl.ds(place, ACT_DEV), :] = pack[q * ACT_DEV : (q + 1) * ACT_DEV]
    lines = packed[...].T[:4]
    count = jnp.sum(picker_ref[...].astype(F32))
    mine = iota(lines.shape, 1) // ACT_DEV == lax.axis_index("seq")
    lines = jnp.where(iota(lines.shape, 0) == 3, jnp.where(mine, count, 0.0), lines)
    stats_ref[...] = jnp.broadcast_to(lines[None], stats_ref.shape)


def local_logits(n_seq, n_vocab, mine, blocks, head, picker):
    shard = head.shape[1]
    rows, lanes = n_seq * ACT_DEV, lanes_of(n_seq)
    return pl.pallas_call(
        functools.partial(logits_kernel, n_seq),
        in_specs=[pl.BlockSpec(memory_space=pltpu.VMEM)] * 7,
        out_shape=[
            jax.ShapeDtypeStruct((rows, shard), F32),
            jax.ShapeDtypeStruct((n_seq * n_vocab, 4, lanes), F32),
        ],
        scratch_shapes=[pltpu.VMEM((lanes, LANES), F32)],
        compiler_params=params(),
        name="local_logits",
    )(mine, *blocks, head, picker)


def merged(stats):
    tops, sums, weights = stats[:, 0], stats[:, 1], stats[:, 2]
    top = jnp.max(tops, axis=0, keepdims=True)
    offset = tops - top
    scale = jnp.exp(offset)
    total = jnp.sum(scale * sums, axis=0, keepdims=True)
    weighted = jnp.sum(scale * (weights + offset * sums), axis=0, keepdims=True)
    return top, total, weighted / total


def entropy_kernel(n_vocab, stats_ref, picker_ref, each_ref, average_ref, column):
    stats = stats_ref[...]
    _, total, centred = merged(stats)
    entropy = jnp.log(total) - centred
    counts = jnp.sum(stats[:, 3], axis=0, keepdims=True) / n_vocab
    valid = (iota(entropy.shape, 1) % ACT_DEV).astype(F32) + 0.5 < counts
    sums = jnp.sum(jnp.where(valid, entropy, 0.0), axis=1, keepdims=True)
    average_ref[...] = sums / jnp.sum(valid.astype(F32), axis=1, keepdims=True)
    column[...] = jnp.broadcast_to(entropy, (LANES, entropy.shape[1])).T
    place = pl.multiple_of(lax.axis_index("seq") * ACT_DEV, ACT_DEV)
    mine = column[pl.ds(place, ACT_DEV), :][:, :1]
    picked = picker_ref[...].astype(F32) > 0.5
    each_ref[...] = jnp.sum(jnp.where(picked, mine, 0.0), axis=0, keepdims=True)


def entropies(n_vocab, stats, picker):
    tokens = picker.shape[1]
    return pl.pallas_call(
        functools.partial(entropy_kernel, n_vocab),
        out_shape=[
            jax.ShapeDtypeStruct((1, tokens), F32),
            jax.ShapeDtypeStruct((1, 1), F32),
        ],
        scratch_shapes=[pltpu.VMEM((stats.shape[2], LANES), F32)],
        compiler_params=params(),
        name="entropies",
    )(stats, picker)


def gradient_kernel(n_seq, n_vocab, stats_ref, logits_ref, head_ref, *refs):
    *out_refs, columns, ordered = refs
    near_refs, far_refs, last_refs = (out_refs[k * PARTS : (k + 1) * PARTS] for k in range(3))
    top, total, centred = merged(stats_ref[...])
    row = iota((8, top.shape[1]), 0)
    lines = jnp.where(row == 0, top, jnp.where(row == 1, 1.0 / total, top + centred))
    columns[...] = jnp.concatenate([lines] * (LANES // 8), axis=0).T
    for q, (core, chip) in enumerate(row_order(n_seq)):
        place = pl.multiple_of(owner_of(n_seq, core, chip) * ACT_DEV, ACT_DEV)
        ordered[q * ACT_DEV : (q + 1) * ACT_DEV] = columns[pl.ds(place, ACT_DEV), :]
    logits = logits_ref[...]
    prob = jnp.exp(logits - ordered[:, 0:1]) * ordered[:, 1:2]
    score = (prob * (ordered[:, 2:3] - logits)).astype(BF16)
    n_chip = n_seq // 2
    last = n_chip - 1
    size = near_refs[0].shape[3]
    for v in range(n_vocab):
        for c in range(PARTS):
            start = (v * PARTS + c) * size
            part = lax.dot_general(
                score,
                head_ref[start : start + size, :],
                (((1,), (1,)), ((), ())),
                preferred_element_type=F32,
            ).astype(BF16)
            blocks = part.reshape(n_seq, ACT_DEV, size)
            near_refs[c][:last, v] = blocks[:last]
            far_refs[c][:, v] = blocks[last : 2 * last]
            near_refs[c][last, v] = blocks[2 * last]
            last_refs[c][v] = blocks[2 * last + 1]


def gradients(n_seq, n_vocab, stats, logits, head):
    rows = logits.shape[0]
    n_chip = n_seq // 2
    block = (n_vocab, ACT_DEV, head.shape[0] // (n_vocab * PARTS))
    outs = [jax.ShapeDtypeStruct((n_chip,) + block, BF16)] * PARTS
    outs += [jax.ShapeDtypeStruct((n_chip - 1,) + block, BF16)] * PARTS
    outs += [jax.ShapeDtypeStruct(block, BF16)] * PARTS
    outs = pl.pallas_call(
        functools.partial(gradient_kernel, n_seq, n_vocab),
        in_specs=[pl.BlockSpec(memory_space=pltpu.VMEM)] * 3,
        out_shape=outs,
        scratch_shapes=[
            pltpu.VMEM((stats.shape[2], LANES), F32),
            pltpu.VMEM((rows, LANES), F32),
        ],
        compiler_params=params(),
        name="gradients",
    )(stats, logits, head)
    return [outs[k * PARTS : (k + 1) * PARTS] for k in range(3)]


def body(n_seq, n_vocab, hidden, head, mask):
    n_chip = n_seq // 2
    last = n_chip - 1
    bits = n_chip.bit_length() - 1

    def swap_core(value):
        return lax.ppermute(value, "seq", [(i, i ^ 1) for i in range(n_seq)])

    def swap_chip(value, step):
        flips = (2 << step, 2 << (bits - 1 - step))
        return lax.ppermute(value, "seq", [(i, i ^ flips[i & 1]) for i in range(n_seq)])

    def send_vocab(value, k):
        return lax.ppermute(value, "vocab", [(i, i ^ k) for i in range(n_vocab)])

    own, picker = select(mask, hidden)

    near = [own]
    mine = own_logits(own, head)
    for a in range(1, n_chip):
        step = a.bit_length() - 1
        source = near[a ^ (1 << step)]
        if a == 1 << step:
            source = jnp.concatenate(source, axis=1)
            if a > 1:
                source, mine = lax.optimization_barrier((source, mine))
            moved = swap_chip(source, step)
            near.append(jnp.split(moved, PARTS, axis=1))
        else:
            near.append([swap_chip(part, step) for part in source])
    early = jnp.concatenate([near[a][c] for c in range(PARTS) for a in range(last)], axis=0)
    early, near[last][0] = lax.optimization_barrier((early, near[last][0]))
    late = jnp.concatenate(near[last], axis=0)
    blocks = [early, swap_core(early), late, swap_core(late)]

    logits, stats = local_logits(n_seq, n_vocab, mine, blocks, head, picker)
    stats = lax.all_to_all(stats, ("seq", "vocab"), 0, 0, tiled=True)
    near, far, far_last = gradients(n_seq, n_vocab, stats, logits, head)
    moved = [swap_core(part) for part in far_last]
    far, _ = lax.optimization_barrier((far, moved))
    far = [swap_core(part) for part in far]
    sums = [[near[c][a].astype(F32) + far[c][a].astype(F32) for c in range(PARTS)] for a in range(last)]
    sums.append([near[c][last].astype(F32) + moved[c].astype(F32) for c in range(PARTS)])
    direct = {
        a: jnp.concatenate([part.astype(BF16) for part in sums[a]], axis=2)
        for a in range(2, n_chip)
        if a & (a - 1) == 0 and a > n_chip // 4
    }
    for a in range(last, 0, -1):
        step = a.bit_length() - 1
        target = sums[a ^ (1 << step)]
        if a in direct:
            moved = jnp.split(swap_chip(direct[a], step), PARTS, axis=2)
        else:
            moved = [swap_chip(part.astype(BF16), step) for part in sums[a]]
        for c in range(PARTS):
            if a == last:
                moved[c], _ = lax.optimization_barrier((moved[c], direct))
            target[c] += moved[c].astype(F32)

    stats, _ = lax.optimization_barrier((stats, sums[0]))
    each, average = entropies(n_vocab, stats, picker)
    column = lax.axis_index("vocab")

    def piece(k):
        parts = [lax.dynamic_index_in_dim(part, column ^ k, 0, keepdims=False) for part in sums[0]]
        return jnp.concatenate(parts, axis=1)

    result = piece(0)
    for k in range(n_vocab - 1, 0, -1):
        result = result + send_vocab(piece(k).astype(BF16), k).astype(F32)
    derivative = lax.dot_general(
        picker, result.astype(BF16), (((0,), (0,)), ((), ())), preferred_element_type=F32
    ).astype(BF16)
    return each.reshape(-1), average.reshape(()), derivative


def solution(mesh):
    n_seq, n_vocab = mesh.shape["seq"], mesh.shape["vocab"]

    def run(hidden, head, mask):
        return body(n_seq, n_vocab, hidden, head, mask)

    return jax.shard_map(
        run,
        mesh=mesh,
        in_specs=(P("seq", None), P(None, ("seq", "vocab")), P("seq")),
        out_specs=(P("seq"), P(), P("seq", "vocab")),
        check_vma=False,
    )
```

```python
import functools

import jax
import jax.numpy as jnp
from jax import lax
from jax.experimental import pallas as pl
from jax.experimental.pallas import tpu as pltpu
from jax.sharding import PartitionSpec as P

ACT_DEV = 16
PARTS = 2
LANES = 128
CHUNKS = 8
OWN_CHUNKS = 1
FLIGHT = 4
VMEM_BYTES = 24 * 2**20
F32, BF16 = jnp.float32, jnp.bfloat16


def params():
    return pltpu.CompilerParams(vmem_limit_bytes=VMEM_BYTES)


def in_hbm(value):
    return pltpu.with_memory_space_constraint(value, pltpu.HBM)


def iota(shape, axis):
    return lax.broadcasted_iota(jnp.int32, shape, axis)


def turn(bits, index):
    return sum(((index >> b) & 1) << (bits - 1 - b) for b in range(bits))


def row_order(n_seq):
    last = n_seq // 2 - 1
    early = [(core, chip) for core in (0, 1) for chip in range(last)]
    return early + [(0, last), (1, last)]


def owner_of(n_seq, core, chip):
    me = lax.axis_index("seq")
    bits = (n_seq // 2).bit_length() - 1
    odd = (me & 1) ^ core
    return me ^ (jnp.where(odd == 1, turn(bits, chip), chip) * 2 + core)


def lanes_of(n_seq):
    return -(-n_seq * ACT_DEV // LANES) * LANES


def arrive(copies, i):
    copies[i].wait()
    if i + FLIGHT < len(copies):
        copies[i + FLIGHT].start()


def select_kernel(mask_ref, hidden_ref, *refs):
    *own_refs, picker_ref, mask_here, hidden_here, mask_sem, sems = refs
    chunks, tokens, step = hidden_here.shape
    copies = [
        pltpu.make_async_copy(
            hidden_ref.at[:, pl.ds(i * step, step)], hidden_here.at[i], sems.at[i]
        )
        for i in range(chunks)
    ]
    mask_copy = pltpu.make_async_copy(mask_ref, mask_here, mask_sem)
    mask_copy.start()
    for copy in copies[:FLIGHT]:
        copy.start()
    mask_copy.wait()
    mask = mask_here[...]
    upper = (iota((tokens, tokens), 0) <= iota((tokens, tokens), 1)).astype(BF16)
    ones = jnp.broadcast_to(mask.astype(F32).astype(BF16), (ACT_DEV, tokens))
    slots = jnp.dot(ones, upper, preferred_element_type=F32).astype(jnp.int32) - 1
    picker = (slots == iota((ACT_DEV, tokens), 0)) & (mask == 1)
    picker = picker.astype(F32).astype(BF16)
    picker_ref[...] = picker
    each = chunks // len(own_refs)
    for i in range(chunks):
        arrive(copies, i)
        own = jnp.dot(picker, hidden_here[i], preferred_element_type=F32)
        at = (i % each) * step
        own_refs[i // each][:, at : at + step] = own.astype(BF16)


def select(mask, hidden):
    tokens, width = hidden.shape
    chunks = 4
    own = jax.ShapeDtypeStruct((ACT_DEV, width // PARTS), BF16)
    *own, picker = pl.pallas_call(
        select_kernel,
        in_specs=[pl.BlockSpec(memory_space=pltpu.HBM)] * 2,
        out_shape=[own] * PARTS + [jax.ShapeDtypeStruct((ACT_DEV, tokens), BF16)],
        scratch_shapes=[
            pltpu.VMEM((1, tokens), jnp.int32),
            pltpu.VMEM((chunks, tokens, width // chunks), BF16),
            pltpu.SemaphoreType.DMA,
            pltpu.SemaphoreType.DMA((chunks,)),
        ],
        compiler_params=params(),
        name="select_rows",
    )(in_hbm(mask.reshape(1, tokens)), in_hbm(hidden))
    return own, picker


def own_kernel(own_ref, head_ref, out_ref, head_here, sems):
    chunks, step, _ = head_here.shape
    copies = [
        pltpu.make_async_copy(head_ref.at[pl.ds(i * step, step), :], head_here.at[i], sems.at[i])
        for i in range(chunks)
    ]
    for copy in copies:
        copy.start()
    total = None
    for i in range(chunks):
        copies[i].wait()
        rows = own_ref[:, i * step : (i + 1) * step]
        part = jnp.dot(rows, head_here[i], preferred_element_type=F32)
        total = part if total is None else total + part
    out_ref[...] = total


def own_logits(own, head):
    width, shard = head.shape
    return pl.pallas_call(
        own_kernel,
        in_specs=[pl.BlockSpec(memory_space=pltpu.VMEM), pl.BlockSpec(memory_space=pltpu.HBM)],
        out_shape=jax.ShapeDtypeStruct((ACT_DEV, shard), F32),
        scratch_shapes=[
            pltpu.VMEM((OWN_CHUNKS, width // CHUNKS, shard), BF16),
            pltpu.SemaphoreType.DMA((OWN_CHUNKS,)),
        ],
        compiler_params=params(),
        name="own_logits",
    )(own[0], in_hbm(head))


def logits_kernel(n_seq, *refs):
    own_ref, *block_refs, head_ref, picker_ref, logits_ref, stats_ref, packed = refs
    step = head_ref.shape[0] // CHUNKS
    each = CHUNKS // PARTS
    logits = None
    for i in range(CHUNKS):
        at = (i % each) * step
        rows = []
        for k, ref in enumerate(block_refs):
            size = ref.shape[0] // PARTS
            start = (i // each) * size
            first = start + ACT_DEV if k == 0 and i < OWN_CHUNKS else start
            rows.append(ref[first : start + size, at : at + step])
        rows = jnp.concatenate(rows, axis=0)
        head = head_ref[i * step : (i + 1) * step, :]
        part = jnp.dot(rows, head, preferred_element_type=F32)
        if i < OWN_CHUNKS:
            mine = own_ref[...] if i == 0 else jnp.zeros(own_ref.shape, F32)
            part = jnp.concatenate([mine, part], axis=0)
        logits = part if logits is None else logits + part
    logits_ref[...] = logits
    top = jnp.max(logits, axis=1, keepdims=True)
    away = logits - top
    ex = jnp.exp(away)
    sums = jnp.sum(ex, axis=1, keepdims=True)
    weighted = jnp.sum(ex * away, axis=1, keepdims=True)
    lane = iota((logits.shape[0], LANES), 1)
    pack = jnp.where(lane == 0, top, jnp.where(lane == 1, sums, weighted))
    if packed.shape[0] > n_seq * ACT_DEV:
        packed[...] = jnp.ones(packed.shape, F32)
    for q, (core, chip) in enumerate(row_order(n_seq)):
        place = pl.multiple_of(owner_of(n_seq, core, chip) * ACT_DEV, ACT_DEV)
        packed[pl.ds(place, ACT_DEV), :] = pack[q * ACT_DEV : (q + 1) * ACT_DEV]
    lines = packed[...].T[:4]
    count = jnp.sum(picker_ref[...].astype(F32))
    mine = iota(lines.shape, 1) // ACT_DEV == lax.axis_index("seq")
    lines = jnp.where(iota(lines.shape, 0) == 3, jnp.where(mine, count, 0.0), lines)
    stats_ref[...] = jnp.broadcast_to(lines[None], stats_ref.shape)


def local_logits(n_seq, n_vocab, mine, blocks, head, picker):
    shard = head.shape[1]
    rows, lanes = n_seq * ACT_DEV, lanes_of(n_seq)
    return pl.pallas_call(
        functools.partial(logits_kernel, n_seq),
        in_specs=[pl.BlockSpec(memory_space=pltpu.VMEM)] * 7,
        out_shape=[
            jax.ShapeDtypeStruct((rows, shard), F32),
            jax.ShapeDtypeStruct((n_seq * n_vocab, 4, lanes), F32),
        ],
        scratch_shapes=[pltpu.VMEM((lanes, LANES), F32)],
        compiler_params=params(),
        name="local_logits",
    )(mine, *blocks, head, picker)


def merged(stats):
    tops, sums, weights = stats[:, 0], stats[:, 1], stats[:, 2]
    top = jnp.max(tops, axis=0, keepdims=True)
    offset = tops - top
    scale = jnp.exp(offset)
    total = jnp.sum(scale * sums, axis=0, keepdims=True)
    weighted = jnp.sum(scale * (weights + offset * sums), axis=0, keepdims=True)
    return top, total, weighted / total


def entropy_kernel(n_vocab, stats_ref, picker_ref, each_ref, average_ref, column):
    stats = stats_ref[...]
    _, total, centred = merged(stats)
    entropy = jnp.log(total) - centred
    counts = jnp.sum(stats[:, 3], axis=0, keepdims=True) / n_vocab
    valid = (iota(entropy.shape, 1) % ACT_DEV).astype(F32) + 0.5 < counts
    sums = jnp.sum(jnp.where(valid, entropy, 0.0), axis=1, keepdims=True)
    average_ref[...] = sums / jnp.sum(valid.astype(F32), axis=1, keepdims=True)
    column[...] = jnp.broadcast_to(entropy, (LANES, entropy.shape[1])).T
    place = pl.multiple_of(lax.axis_index("seq") * ACT_DEV, ACT_DEV)
    mine = column[pl.ds(place, ACT_DEV), :][:, :1]
    picked = picker_ref[...].astype(F32) > 0.5
    each_ref[...] = jnp.sum(jnp.where(picked, mine, 0.0), axis=0, keepdims=True)


def entropies(n_vocab, stats, picker):
    tokens = picker.shape[1]
    return pl.pallas_call(
        functools.partial(entropy_kernel, n_vocab),
        out_shape=[
            jax.ShapeDtypeStruct((1, tokens), F32),
            jax.ShapeDtypeStruct((1, 1), F32),
        ],
        scratch_shapes=[pltpu.VMEM((stats.shape[2], LANES), F32)],
        compiler_params=params(),
        name="entropies",
    )(stats, picker)


def gradient_kernel(n_seq, n_vocab, stats_ref, logits_ref, head_ref, *refs):
    *out_refs, columns, ordered = refs
    near_refs, far_refs, last_refs = (out_refs[k * PARTS : (k + 1) * PARTS] for k in range(3))
    top, total, centred = merged(stats_ref[...])
    row = iota((8, top.shape[1]), 0)
    lines = jnp.where(row == 0, top, jnp.where(row == 1, 1.0 / total, top + centred))
    columns[...] = jnp.concatenate([lines] * (LANES // 8), axis=0).T
    for q, (core, chip) in enumerate(row_order(n_seq)):
        place = pl.multiple_of(owner_of(n_seq, core, chip) * ACT_DEV, ACT_DEV)
        ordered[q * ACT_DEV : (q + 1) * ACT_DEV] = columns[pl.ds(place, ACT_DEV), :]
    logits = logits_ref[...]
    prob = jnp.exp(logits - ordered[:, 0:1]) * ordered[:, 1:2]
    score = (prob * (ordered[:, 2:3] - logits)).astype(BF16)
    n_chip = n_seq // 2
    last = n_chip - 1
    size = near_refs[0].shape[3]
    for v in range(n_vocab):
        for c in range(PARTS):
            start = (v * PARTS + c) * size
            part = lax.dot_general(
                score,
                head_ref[start : start + size, :],
                (((1,), (1,)), ((), ())),
                preferred_element_type=F32,
            ).astype(BF16)
            blocks = part.reshape(n_seq, ACT_DEV, size)
            near_refs[c][:last, v] = blocks[:last]
            far_refs[c][:, v] = blocks[last : 2 * last]
            near_refs[c][last, v] = blocks[2 * last]
            last_refs[c][v] = blocks[2 * last + 1]


def gradients(n_seq, n_vocab, stats, logits, head):
    rows = logits.shape[0]
    n_chip = n_seq // 2
    block = (n_vocab, ACT_DEV, head.shape[0] // (n_vocab * PARTS))
    outs = [jax.ShapeDtypeStruct((n_chip,) + block, BF16)] * PARTS
    outs += [jax.ShapeDtypeStruct((n_chip - 1,) + block, BF16)] * PARTS
    outs += [jax.ShapeDtypeStruct(block, BF16)] * PARTS
    outs = pl.pallas_call(
        functools.partial(gradient_kernel, n_seq, n_vocab),
        in_specs=[pl.BlockSpec(memory_space=pltpu.VMEM)] * 3,
        out_shape=outs,
        scratch_shapes=[
            pltpu.VMEM((stats.shape[2], LANES), F32),
            pltpu.VMEM((rows, LANES), F32),
        ],
        compiler_params=params(),
        name="gradients",
    )(stats, logits, head)
    return [outs[k * PARTS : (k + 1) * PARTS] for k in range(3)]


def body(n_seq, n_vocab, hidden, head, mask):
    n_chip = n_seq // 2
    last = n_chip - 1
    bits = n_chip.bit_length() - 1

    def swap_core(value):
        return lax.ppermute(value, "seq", [(i, i ^ 1) for i in range(n_seq)])

    def swap_chip(value, step):
        flips = (2 << step, 2 << (bits - 1 - step))
        return lax.ppermute(value, "seq", [(i, i ^ flips[i & 1]) for i in range(n_seq)])

    def send_vocab(value, k):
        return lax.ppermute(value, "vocab", [(i, i ^ k) for i in range(n_vocab)])

    own, picker = select(mask, hidden)

    near = [own]
    mine = own_logits(own, head)
    for a in range(1, n_chip):
        step = a.bit_length() - 1
        source = near[a ^ (1 << step)]
        if a > 1 and a == 1 << step:
            source, mine = lax.optimization_barrier((jnp.concatenate(source, axis=1), mine))
            moved = swap_chip(source, step)
            near.append(jnp.split(moved, PARTS, axis=1))
        else:
            near.append([swap_chip(part, step) for part in source])
    early = jnp.concatenate([near[a][c] for c in range(PARTS) for a in range(last)], axis=0)
    early, near[last][0] = lax.optimization_barrier((early, near[last][0]))
    late = jnp.concatenate(near[last], axis=0)
    blocks = [early, swap_core(early), late, swap_core(late)]

    logits, stats = local_logits(n_seq, n_vocab, mine, blocks, head, picker)
    stats = lax.all_to_all(stats, ("seq", "vocab"), 0, 0, tiled=True)
    near, far, far_last = gradients(n_seq, n_vocab, stats, logits, head)
    moved = [swap_core(part) for part in far_last]
    far, _ = lax.optimization_barrier((far, moved))
    far = [swap_core(part) for part in far]
    sums = [[near[c][a].astype(F32) + far[c][a].astype(F32) for c in range(PARTS)] for a in range(last)]
    sums.append([near[c][last].astype(F32) + moved[c].astype(F32) for c in range(PARTS)])
    direct = {
        a: jnp.concatenate([part.astype(BF16) for part in sums[a]], axis=2)
        for a in range(2, n_chip)
        if a & (a - 1) == 0 and a > n_chip // 4
    }
    for a in range(last, 0, -1):
        step = a.bit_length() - 1
        target = sums[a ^ (1 << step)]
        if a in direct:
            moved = jnp.split(swap_chip(direct[a], step), PARTS, axis=2)
        else:
            moved = [swap_chip(part.astype(BF16), step) for part in sums[a]]
        for c in range(PARTS):
            if a == last:
                moved[c], _ = lax.optimization_barrier((moved[c], direct))
            target[c] += moved[c].astype(F32)

    stats, _ = lax.optimization_barrier((stats, sums[0]))
    each, average = entropies(n_vocab, stats, picker)
    column = lax.axis_index("vocab")

    def piece(k):
        parts = [lax.dynamic_index_in_dim(part, column ^ k, 0, keepdims=False) for part in sums[0]]
        return jnp.concatenate(parts, axis=1)

    result = piece(0)
    for k in range(n_vocab - 1, 0, -1):
        result = result + send_vocab(piece(k).astype(BF16), k).astype(F32)
    derivative = lax.dot_general(
        picker, result.astype(BF16), (((0,), (0,)), ((), ())), preferred_element_type=F32
    ).astype(BF16)
    return each.reshape(-1), average.reshape(()), derivative


def solution(mesh):
    n_seq, n_vocab = mesh.shape["seq"], mesh.shape["vocab"]

    def run(hidden, head, mask):
        return body(n_seq, n_vocab, hidden, head, mask)

    return jax.shard_map(
        run,
        mesh=mesh,
        in_specs=(P("seq", None), P(None, ("seq", "vocab")), P("seq")),
        out_specs=(P("seq"), P(), P("seq", "vocab")),
        check_vma=False,
    )
```
